32 devices in a mesh: dp: 8 (over z, x), mp: 4 (over y, core).
Axes of the slice: x: 2, y: 2, z: 4, core: 2. Of those that a mesh axis runs over, the one named last changes fastest.
Arguments:
- patches: bfloat16 [16, 20480], P(None, ('dp', 'mp')), may hold values from -6 to 6
- target: float32 [32, 20480], P(None, ('dp', 'mp')), may hold values from -6 to 6
- segments: int32 [20480], P('dp'), may hold values from 0 to 15, as said below
- positions: int32 [2, 20480], P(None, 'dp'), may hold values from 0 to 31, as said below
- classes: int32 [128], P('dp'), may hold values from 0 to 1000
- timesteps: int32 [128], P('dp'), may hold values from 0 to 999
- t_weight: float32 [128], P('dp'), may hold values from 0.3 to 3
- step_count: int32 [1], replicated, may hold values from 2 to 20
- qkv_w: float32 [3, 1152, 1152], P(None, 'dp', 'mp'), may hold values from -0.1875 to 0.1875
- qkv_m: float32 [3, 1152, 1152], P(None, 'dp', 'mp'), may hold values from -4.172325e-07 to 4.172325e-07
- qkv_v: float32 [3, 1152, 1152], P(None, 'dp', 'mp'), may hold values from 1.096693e-14 to 1.7447389e-13
- out_w: float32 [1152, 1152], P('mp', 'dp'), may hold values from -0.75 to 0.75
- out_m: float32 [1152, 1152], P('mp', 'dp'), may hold values from -4.172325e-07 to 4.172325e-07
- out_v: float32 [1152, 1152], P('mp', 'dp'), may hold values from 1.096693e-14 to 1.7447389e-13
- ffn_in_w: float32 [2, 1152, 3072], P(None, 'dp', 'mp'), may hold values from -0.1875 to 0.1875
- ffn_in_m: float32 [2, 1152, 3072], P(None, 'dp', 'mp'), may hold values from -4.172325e-07 to 4.172325e-07
- ffn_in_v: float32 [2, 1152, 3072], P(None, 'dp', 'mp'), may hold values from 1.096693e-14 to 1.7447389e-13
- ffn_out_w: float32 [3072, 1152], P('mp', 'dp'), may hold values from -0.109375 to 0.109375
- ffn_out_m: float32 [3072, 1152], P('mp', 'dp'), may hold values from -4.172325e-07 to 4.172325e-07
- ffn_out_v: float32 [3072, 1152], P('mp', 'dp'), may hold values from 1.096693e-14 to 1.7447389e-13
- mod_w: float32 [1152, 9216], P('dp'), may hold values from -0.1875 to 0.1875
- mod_m: float32 [1152, 9216], P('dp'), may hold values from -4.172325e-07 to 4.172325e-07
- mod_v: float32 [1152, 9216], P('dp'), may hold values from 1.096693e-14 to 1.7447389e-13
- table_w: float32 [2468, 1152], P('mp'), as said below
- table_m: float32 [2468, 1152], P('mp'), may hold values from -4.172325e-07 to 4.172325e-07
- table_v: float32 [2468, 1152], P('mp'), may hold values from 1.096693e-14 to 1.7447389e-13
Outputs:
- loss: float32 [1], replicated
- grad_norm: float32 [1], replicated
- qkv_w_new: float32 [3, 1152, 1152], P(None, 'dp', 'mp')
- qkv_m_new: float32 [3, 1152, 1152], P(None, 'dp', 'mp')
- qkv_v_new: float32 [3, 1152, 1152], P(None, 'dp', 'mp')
- out_w_new: float32 [1152, 1152], P('mp', 'dp')
- out_m_new: float32 [1152, 1152], P('mp', 'dp')
- out_v_new: float32 [1152, 1152], P('mp', 'dp')
- ffn_in_w_new: float32 [2, 1152, 3072], P(None, 'dp', 'mp')
- ffn_in_m_new: float32 [2, 1152, 3072], P(None, 'dp', 'mp')
- ffn_in_v_new: float32 [2, 1152, 3072], P(None, 'dp', 'mp')
- ffn_out_w_new: float32 [3072, 1152], P('mp', 'dp')
- ffn_out_m_new: float32 [3072, 1152], P('mp', 'dp')
- ffn_out_v_new: float32 [3072, 1152], P('mp', 'dp')
- mod_w_new: float32 [1152, 9216], P('dp')
- mod_m_new: float32 [1152, 9216], P('dp')
- mod_v_new: float32 [1152, 9216], P('dp')
- table_w_new: float32 [2468, 1152], P('mp')
- table_m_new: float32 [2468, 1152], P('mp')
- table_v_new: float32 [2468, 1152], P('mp')
The draws below stay inside these ranges and needn't reach their ends.
Inputs may be any that keep to these rules, and one draw needn't show every extreme that they name: `segments`: within each group of 2560 consecutive tokens the values number the group's 16 images in order as runs of 64 to 256 tokens; images 2j and 2j+1 of a group hold 320 tokens together; every group has an image of 256 tokens and one of 64. For the k-th token of an image, positions holds k // w and k % w, with a width w of 8 to 16 for that image. `table_w`: rows are drawn with the scale of their fan-in; bias rows of the timestep MLP and the patch embedding are of order one.
All inputs are finite; a program needn't handle non-finite values.
Results may differ from the reference program's by a relative error of at most 0.0012.
The reference program's roundings to bfloat16 on the way count: a program that leaves them out, or rounds other values in their place, can miss the bound.
Values may be sent and summed in bfloat16 or wider, within the bound.
A program may use at most 384 MiB of HBM per device.

```python
import math
import jax
import jax.numpy as jnp
from jax import lax

D = 1152
HEADS = 16
HD = 72
FF = 3072
PATCH_IN = 16
OUT = 32
FREQ = 256
NCLS = 1001
TOK_GRP = 2560
IMG_GRP = 16
TOKENS = 20480
IMAGES = 128
MOD = 9216
ROWS = 2468
NPARAM = 29385216


def image_layout(key):
    group_count = TOKENS // TOK_GRP
    pair_count = TOK_GRP // 320
    pair_index = jnp.arange(pair_count, dtype=jnp.int32)[None, :]
    lead_len = jax.random.randint(jax.random.fold_in(key, 101), (group_count, pair_count), 64, 257)
    lead_len = jnp.where(pair_index == 0, 256, lead_len)
    swapped = jax.random.randint(jax.random.fold_in(key, 102), (group_count, pair_count), 0, 2)
    lead_len = jnp.where(swapped == 1, 320 - lead_len, lead_len)
    lengths = jnp.stack([lead_len, 320 - lead_len], 2).reshape(group_count, IMG_GRP)
    widths = jax.random.randint(jax.random.fold_in(key, 103), (group_count, IMG_GRP), 8, 17)
    widths = jnp.where(lengths == 256, 8, widths)
    ends = jnp.cumsum(lengths, 1)
    starts = ends - lengths
    token_pos = jnp.arange(TOK_GRP, dtype=jnp.int32)
    inside = ((token_pos[None, :, None] >= starts[:, None, :]) & (token_pos[None, :, None] < ends[:, None, :])).astype(jnp.int32)
    image_ids = jnp.sum(inside * jnp.arange(IMG_GRP, dtype=jnp.int32)[None, None, :], 2)
    local_pos = token_pos[None, :] - jnp.sum(inside * starts[:, None, :], 2)
    width_tok = jnp.sum(inside * widths[:, None, :], 2)
    coords = jnp.stack([(local_pos // width_tok).reshape(TOKENS), (local_pos % width_tok).reshape(TOKENS)], 0)
    return (image_ids.reshape(TOKENS).astype(jnp.int32), coords.astype(jnp.int32))


def draw_segments(key, part):
    return image_layout(key)[0]


def draw_positions(key, part):
    return image_layout(key)[1]


def draw_table_w(key, part):
    base = jax.random.normal(key, (ROWS, D), jnp.float32)
    row_ids = jnp.arange(ROWS, dtype=jnp.int32)
    row_b1 = NCLS + FREQ
    row_b2 = row_b1 + 1 + D
    row_pb = row_b2 + 1 + PATCH_IN
    scale = jnp.where(row_ids < NCLS, 0.05, D ** (-0.5))
    scale = jnp.where((row_ids >= NCLS) & (row_ids < row_b1), FREQ ** (-0.5), scale)
    scale = jnp.where((row_ids > row_b2) & (row_ids < row_pb), PATCH_IN ** (-0.5), scale)
    scale = jnp.where((row_ids == row_b1) | (row_ids == row_b2) | (row_ids == row_pb), 0.5, scale)
    return base * scale[:, None]


def set_ends(entries, key, smallest, largest):
    dims = entries.shape
    place = [jax.random.randint(jax.random.fold_in(key, axis), (), 0, dims[axis]) for axis in range(len(dims))]
    entries = entries.at[tuple(place)].set(smallest)
    longest = dims.index(max(dims))
    place[longest] = (place[longest] + 1) % dims[longest]
    return entries.at[tuple(place)].set(largest)


def levels(rng, dims, shards, smallest, largest):
    loudness, own = 1.0, jax.random.fold_in(rng, 6)
    for position, blocks in shards:
        draws = jnp.exp(jax.random.uniform(jax.random.fold_in(own, position), (blocks,), jnp.float32, smallest / len(shards), largest / len(shards)))
        loudness = loudness * jnp.repeat(draws, dims[position] // blocks).reshape([-1 if axis == position else 1 for axis in range(len(dims))])
    return loudness


def scatter_about(key, dims, spread, most, cuts=(), kind=jnp.bfloat16):
    drawn = spread * jax.random.normal(key, dims, jnp.float32)
    if cuts:
        drawn = drawn * levels(key, dims, cuts, -0.22, 0.18)
    return jnp.clip(drawn, -most, most).astype(kind)


def setup_inputs(seed: int = 0) -> dict:
    seeds = jax.random.split(jax.random.key(seed), 27)
    patches = scatter_about(seeds[0], (PATCH_IN, TOKENS), 1.0, 6.0, ((1, 32),))
    target = scatter_about(seeds[1], (OUT, TOKENS), 1.0, 6.0, ((1, 32),), jnp.float32)
    segments = draw_segments(jax.random.fold_in(seeds[26], 71), 0)
    positions = draw_positions(jax.random.fold_in(seeds[26], 71), 0)
    classes = set_ends(jax.random.randint(seeds[4], (IMAGES,), 0, NCLS), jax.random.fold_in(seeds[4], 1), 0, NCLS - 1).astype(jnp.int32)
    timesteps = set_ends(jax.random.randint(seeds[5], (IMAGES,), 0, 1000), jax.random.fold_in(seeds[5], 1), 0, 999).astype(jnp.int32)
    t_weight = jnp.clip(jnp.exp(math.log(3.0) - 2.3025851 * jax.random.uniform(seeds[6], (IMAGES,), jnp.float32) ** levels(seeds[6], (IMAGES,), ((0, 8),), -0.2, 0.2)), 0.3, 3.0)
    step_count = jax.random.randint(seeds[7], (1,), 2, 21).astype(jnp.int32)
    qkv_w = scatter_about(seeds[8], (3, D, D), D ** -0.5, 0.1875, ((1, 8), (2, 4)), jnp.float32)
    qkv_m = scatter_about(seeds[9], (3, D, D), (0.0555 * (TOKENS * NPARAM) ** -0.5), 4.172325134277344e-07, ((1, 8), (2, 4)), jnp.float32)
    qkv_v = jnp.clip(jnp.exp(math.log(1.7447389290704135e-13) - 2.7668907 * jax.random.uniform(seeds[10], (3, D, D), jnp.float32) ** levels(seeds[10], (3, D, D), ((1, 8), (2, 4)), -0.2, 0.2)), 1.0966930285454847e-14, 1.7447389290704135e-13)
    out_w = scatter_about(seeds[11], (D, D), (D // 16) ** -0.5, 0.75, ((0, 4), (1, 8)), jnp.float32)
    out_m = scatter_about(seeds[12], (D, D), (0.0555 * (TOKENS * NPARAM) ** -0.5), 4.172325134277344e-07, ((0, 4), (1, 8)), jnp.float32)
    out_v = jnp.clip(jnp.exp(math.log(1.7447389290704135e-13) - 2.7668907 * jax.random.uniform(seeds[13], (D, D), jnp.float32) ** levels(seeds[13], (D, D), ((0, 4), (1, 8)), -0.2, 0.2)), 1.0966930285454847e-14, 1.7447389290704135e-13)
    ffn_in_w = scatter_about(seeds[14], (2, D, FF), D ** -0.5, 0.1875, ((1, 8), (2, 4)), jnp.float32)
    ffn_in_m = scatter_about(seeds[15], (2, D, FF), (0.0555 * (TOKENS * NPARAM) ** -0.5), 4.172325134277344e-07, ((1, 8), (2, 4)), jnp.float32)
    ffn_in_v = jnp.clip(jnp.exp(math.log(1.7447389290704135e-13) - 2.7668907 * jax.random.uniform(seeds[16], (2, D, FF), jnp.float32) ** levels(seeds[16], (2, D, FF), ((1, 8), (2, 4)), -0.2, 0.2)), 1.0966930285454847e-14, 1.7447389290704135e-13)
    ffn_out_w = scatter_about(seeds[17], (FF, D), FF ** -0.5, 0.109375, ((0, 4), (1, 8)), jnp.float32)
    ffn_out_m = scatter_about(seeds[18], (FF, D), (0.0555 * (TOKENS * NPARAM) ** -0.5), 4.172325134277344e-07, ((0, 4), (1, 8)), jnp.float32)
    ffn_out_v = jnp.clip(jnp.exp(math.log(1.7447389290704135e-13) - 2.7668907 * jax.random.uniform(seeds[19], (FF, D), jnp.float32) ** levels(seeds[19], (FF, D), ((0, 4), (1, 8)), -0.2, 0.2)), 1.0966930285454847e-14, 1.7447389290704135e-13)
    mod_w = scatter_about(seeds[20], (D, MOD), D ** -0.5, 0.1875, ((0, 8),), jnp.float32)
    mod_m = scatter_about(seeds[21], (D, MOD), (0.0555 * (TOKENS * NPARAM) ** -0.5), 4.172325134277344e-07, ((0, 8),), jnp.float32)
    mod_v = jnp.clip(jnp.exp(math.log(1.7447389290704135e-13) - 2.7668907 * jax.random.uniform(seeds[22], (D, MOD), jnp.float32) ** levels(seeds[22], (D, MOD), ((0, 8),), -0.2, 0.2)), 1.0966930285454847e-14, 1.7447389290704135e-13)
    table_w = draw_table_w(jax.random.fold_in(seeds[26], 71), 0)
    table_m = scatter_about(seeds[24], (ROWS, D), (0.0555 * (TOKENS * NPARAM) ** -0.5), 4.172325134277344e-07, ((0, 4),), jnp.float32)
    table_v = jnp.clip(jnp.exp(math.log(1.7447389290704135e-13) - 2.7668907 * jax.random.uniform(seeds[25], (ROWS, D), jnp.float32) ** levels(seeds[25], (ROWS, D), ((0, 4),), -0.2, 0.2)), 1.0966930285454847e-14, 1.7447389290704135e-13)
    return {"patches": patches, "target": target, "segments": segments, "positions": positions, "classes": classes, "timesteps": timesteps, "t_weight": t_weight, "step_count": step_count, "qkv_w": qkv_w, "qkv_m": qkv_m, "qkv_v": qkv_v, "out_w": out_w, "out_m": out_m, "out_v": out_v, "ffn_in_w": ffn_in_w, "ffn_in_m": ffn_in_m, "ffn_in_v": ffn_in_v, "ffn_out_w": ffn_out_w, "ffn_out_m": ffn_out_m, "ffn_out_v": ffn_out_v, "mod_w": mod_w, "mod_m": mod_m, "mod_v": mod_v, "table_w": table_w, "table_m": table_m, "table_v": table_v}


@jax.custom_vjp
def low(v):
    return lax.optimization_barrier(v.astype(jnp.bfloat16)).astype(jnp.float32)

@jax.custom_vjp
def low_back(v):
    return v

def low_keep(v):
    return (low(v), None)

def low_pass(kept, grad):
    return (grad,)

def back_keep(v):
    return (v, None)

def back_low(kept, grad):
    return (low(grad),)
low.defvjp(low_keep, low_pass)
low_back.defvjp(back_keep, back_low)
EPS_NORM = 1e-06
BETA_ONE = 0.9
BETA_TWO = 0.95
ADAM_EPS = 1e-08
LEARN_RATE = 0.03
WEIGHT_DECAY = 0.1
CLIP_SCALE = 0.5
HIGH = lax.Precision.HIGHEST

def matmul(left, right):
    return jnp.dot(left, right, precision=HIGH)

def layer_norm(values):
    centred = values - lax.optimization_barrier(jnp.mean(values, -1, keepdims=True))
    return centred * lax.rsqrt(lax.optimization_barrier(jnp.mean(centred * centred, -1, keepdims=True)) + EPS_NORM)

def modulate(values, scale_rows, shift_rows):
    return layer_norm(values) * (1.0 + scale_rows) + shift_rows

def rope_tables(positions, quarter):
    freqs = jnp.exp(-math.log(10000.0) * jnp.arange(quarter, dtype=jnp.float32) / quarter)
    tables = []
    for axis_pos in (positions[0], positions[1]):
        angle = axis_pos.astype(jnp.float32)[:, None] * freqs[None, :]
        tables.append((jnp.cos(angle)[:, None, :], jnp.sin(angle)[:, None, :]))
    return tables

def rotate(values, tables, direction):
    quarter = values.shape[-1] // 4
    pieces = []
    for part_index in range(2):
        cosine, sine = tables[part_index]
        first = values[..., 2 * part_index * quarter:(2 * part_index + 1) * quarter]
        second = values[..., (2 * part_index + 1) * quarter:(2 * part_index + 2) * quarter]
        pieces.append(first * cosine - direction * second * sine)
        pieces.append(direction * first * sine + second * cosine)
    return jnp.concatenate(pieces, -1)

def attention(queries, key_rows, value_rows, segment_ids):
    token_count = segment_ids.shape[0]
    block = 640 if token_count % 640 == 0 else token_count
    span = min(token_count, block + 512)
    scale = HD ** (-0.5)

    @jax.checkpoint
    def one_block(start):
        key_start = jnp.clip(start - 256, 0, token_count - span)
        query_blk = lax.dynamic_slice_in_dim(queries, start, block, 0)
        key_blk = lax.dynamic_slice_in_dim(key_rows, key_start, span, 0)
        value_blk = lax.dynamic_slice_in_dim(value_rows, key_start, span, 0)
        query_seg = lax.dynamic_slice_in_dim(segment_ids, start, block, 0)
        key_seg = lax.dynamic_slice_in_dim(segment_ids, key_start, span, 0)
        scores = low_back(jnp.einsum('qhd,khd->hqk', query_blk, key_blk, precision=HIGH) * scale)
        scores = jnp.where((query_seg[:, None] == key_seg[None, :])[None], scores, -1e+30)
        peak = lax.optimization_barrier(jnp.max(scores, -1, keepdims=True))
        expo = jnp.exp(scores - peak)
        probs = low(expo / lax.optimization_barrier(jnp.sum(expo, -1, keepdims=True)))
        return jnp.einsum('hqk,khd->qhd', probs, value_blk, precision=HIGH)
    starts = jnp.arange(token_count // block, dtype=jnp.int32) * block
    return lax.map(one_block, starts).reshape(token_count, HEADS, HD)

def conditioning(table, modw, classes, timesteps):
    row_t1 = NCLS
    row_b1 = row_t1 + FREQ
    row_t2 = row_b1 + 1
    row_b2 = row_t2 + D
    row_mbias = row_b2 + 1 + PATCH_IN + 1 + OUT
    class_rows = table[:NCLS][classes]
    half_freq = FREQ // 2
    freqs = jnp.exp(-math.log(10000.0) * jnp.arange(half_freq, dtype=jnp.float32) / half_freq)
    angles = timesteps.astype(jnp.float32)[:, None] * freqs[None, :]
    embed = low(jnp.concatenate([jnp.cos(angles), jnp.sin(angles)], 1))
    pre = low_back(matmul(embed, table[row_t1:row_b1]) + table[row_b1])
    hidden = low(jax.nn.silu(pre))
    cond_vec = low_back(matmul(hidden, table[row_t2:row_b2]) + table[row_b2] + class_rows)
    scaled = low(jax.nn.silu(cond_vec))
    mod_bias = table[row_mbias:row_mbias + 8].reshape(MOD)
    return low_back(matmul(scaled, modw) + mod_bias)

def group_loss(weights, batch):
    qkv, outw, ffn_in, ffn_out, modw, table = weights
    patches, target, seg, pos, classes, timesteps, tweight = batch
    token_count = seg.shape[0]
    image_count = classes.shape[0]
    modulation = conditioning(table, modw, classes, timesteps)[seg]
    stretches = [modulation[:, j * D:(j + 1) * D] for j in range(8)]
    row_patch = NCLS + FREQ + D + 2
    row_pbias = row_patch + PATCH_IN
    row_head = row_pbias + 1
    x_zero = low_back(matmul(patches.T, table[row_patch:row_pbias]) + table[row_pbias])
    a_in = low(modulate(x_zero, stretches[1], stretches[0]))
    tables = rope_tables(pos, HD // 4)
    queries = low_back(matmul(a_in, qkv[0])).reshape(token_count, HEADS, HD)
    key_rows = low_back(matmul(a_in, qkv[1])).reshape(token_count, HEADS, HD)
    value_rows = low(low_back(matmul(a_in, qkv[2]))).reshape(token_count, HEADS, HD)
    queries = low(rotate(queries, tables, 1.0))
    key_rows = low(rotate(key_rows, tables, 1.0))
    att = low(low_back(attention(queries, key_rows, value_rows, seg).reshape(token_count, D)))
    attn_proj = low_back(matmul(att, outw))
    x_one = x_zero + stretches[2] * attn_proj
    m_in = low(modulate(x_one, stretches[4], stretches[3]))
    gate = low_back(matmul(m_in, ffn_in[0]))
    up_val = low_back(matmul(m_in, ffn_in[1]))
    hidden_mlp = low(jax.nn.silu(gate) * up_val)
    mlp_out = low_back(matmul(hidden_mlp, ffn_out))
    x_two = x_one + stretches[5] * mlp_out
    f_in = low(modulate(x_two, stretches[7], stretches[6]))
    pred = low_back(matmul(f_in, table[row_head:row_head + OUT].T))
    diff = pred - target.T
    counts = lax.optimization_barrier(jnp.sum((seg[:, None] == jnp.arange(image_count, dtype=jnp.int32)[None, :]).astype(jnp.float32), 0))
    tok_weight = (tweight / counts)[seg]
    return jnp.sum(tok_weight * lax.optimization_barrier(jnp.mean(diff * diff, 1)))

def total_loss(weights, batches, weight_sum):
    lowered = [low(w) for w in weights]

    def one_group(carry, batch):
        return (carry + jax.checkpoint(group_loss)(lowered, batch), None)
    numer, unused = lax.scan(one_group, jnp.zeros((), jnp.float32), batches)
    return numer / weight_sum

def adam(weight, first, second, grad, count):
    first = BETA_ONE * first + (1.0 - BETA_ONE) * grad
    second = BETA_TWO * second + (1.0 - BETA_TWO) * grad * grad
    m_hat = first / (1.0 - BETA_ONE ** count)
    v_hat = second / (1.0 - BETA_TWO ** count)
    weight = weight - LEARN_RATE * (m_hat / (jnp.sqrt(v_hat) + ADAM_EPS) + WEIGHT_DECAY * weight)
    return (weight, first, second)

def reference(patches, target, segments, positions, classes, timesteps, t_weight, step_count, qkv_w, qkv_m, qkv_v, out_w, out_m, out_v, ffn_in_w, ffn_in_m, ffn_in_v, ffn_out_w, ffn_out_m, ffn_out_v, mod_w, mod_m, mod_v, table_w, table_m, table_v):
    groups = TOKENS // TOK_GRP
    batches = (patches.astype(jnp.float32).reshape(PATCH_IN, groups, TOK_GRP).transpose(1, 0, 2), target.reshape(OUT, groups, TOK_GRP).transpose(1, 0, 2), segments.reshape(groups, TOK_GRP), positions.reshape(2, groups, TOK_GRP).transpose(1, 0, 2), classes.reshape(groups, IMG_GRP), timesteps.reshape(groups, IMG_GRP), t_weight.reshape(groups, IMG_GRP))
    weights = [qkv_w, out_w, ffn_in_w, ffn_out_w, mod_w, table_w]
    firsts = [qkv_m, out_m, ffn_in_m, ffn_out_m, mod_m, table_m]
    seconds = [qkv_v, out_v, ffn_in_v, ffn_out_v, mod_v, table_v]
    weight_sum = jnp.sum(t_weight)
    loss, pullback = jax.vjp(lambda ws: total_loss(ws, batches, weight_sum), weights)
    grads = pullback(jnp.ones_like(loss))[0]
    norm = jnp.sqrt(sum((jnp.sum(g * g) for g in grads)))
    clip = jnp.minimum(1.0, CLIP_SCALE / math.sqrt(TOKENS) / (norm + 1e-06))
    count = step_count[0].astype(jnp.float32)
    results = [loss.reshape(1), norm.reshape(1)]
    for weight, first, second, grad in zip(weights, firsts, seconds, grads):
        results.extend(adam(weight, first, second, grad * clip, count))
    return tuple(results)
```

```python
import functools
import math

import jax
import jax.numpy as jnp
from jax import lax
from jax.experimental import pallas as pl
from jax.experimental.pallas import tpu as pltpu
from jax.sharding import PartitionSpec as P

D = 1152
HD = 72
PATCH_IN = 16
OUT = 32
FREQ = 256
NCLS = 1001
PAIR = 320

ROW_TIME_IN = NCLS
ROW_TIME_BIAS = ROW_TIME_IN + FREQ
ROW_TIME_OUT = ROW_TIME_BIAS + 1
ROW_OUT_BIAS = ROW_TIME_OUT + D
ROW_PATCH = ROW_OUT_BIAS + 1
ROW_PATCH_BIAS = ROW_PATCH + PATCH_IN
ROW_HEAD = ROW_PATCH_BIAS + 1
ROW_MOD_BIAS = ROW_HEAD + OUT
ROWS = ROW_MOD_BIAS + 8
TAIL = ROWS - ROW_PATCH

EPS_NORM = 1e-06
BETA_ONE = 0.9
BETA_TWO = 0.95
ADAM_EPS = 1e-08
LEARN_RATE = 0.03
WEIGHT_DECAY = 0.1
CLIP_SCALE = 0.5
LOW = jnp.bfloat16
F32 = jnp.float32
BOTH = ("dp", "mp")
MESH = pl.DeviceIdType.MESH
STEP = 1152
HOOKS = (0, 1, 2, 4)
LINE_FIRST = (True, True, False)
DEPTH = 4


def matmul(left, right):
    return jnp.dot(left, right, preferred_element_type=F32)


def matmul_tn(left, right):
    return lax.dot_general(left, right, (((0,), (0,)), ((), ())), preferred_element_type=F32)


def matmul_nt(left, right):
    return lax.dot_general(left, right, (((1,), (1,)), ((), ())), preferred_element_type=F32)


def layer_norm(values):
    centred = values - jnp.mean(values, -1, keepdims=True)
    inv_std = lax.rsqrt(jnp.mean(centred * centred, -1, keepdims=True) + EPS_NORM)
    return (centred * inv_std, inv_std)


def norm_back(grad, normed, inv_std, scale_rows):
    inner = grad * (1.0 + scale_rows)
    return inv_std * (
        inner
        - jnp.mean(inner, -1, keepdims=True)
        - normed * jnp.mean(inner * normed, -1, keepdims=True)
    )


def silu_slope(values):
    sigma = jax.nn.sigmoid(values)
    return sigma * (1.0 + values * (1.0 - sigma))


def adam(weight, first, second, grad, count):
    first = BETA_ONE * first + (1.0 - BETA_ONE) * grad
    second = BETA_TWO * second + (1.0 - BETA_TWO) * grad * grad
    m_hat = first / (1.0 - BETA_ONE**count)
    v_hat = second / (1.0 - BETA_TWO**count)
    weight = weight - LEARN_RATE * (m_hat / (jnp.sqrt(v_hat) + ADAM_EPS) + WEIGHT_DECAY * weight)
    return (weight, first, second)


def rotary_tables(positions):
    quarter = HD // 4
    freqs = jnp.exp(-math.log(10000.0) * jnp.arange(quarter, dtype=F32) / quarter)
    angle = positions.astype(F32)[:, :, None] * freqs[None, None, :]
    cosine, sine = jnp.cos(angle), jnp.sin(angle)
    cos_row = jnp.concatenate([cosine[0], cosine[0], cosine[1], cosine[1]], 1)
    sin_row = jnp.concatenate([-sine[0], sine[0], -sine[1], sine[1]], 1)
    return cos_row, sin_row


def coordinates():
    dp, mp = lax.axis_index("dp"), lax.axis_index("mp")
    z, x = dp // 2, dp % 2
    y, c = mp // 2, mp % 2
    first = (x + (1 - c) * (1 - 2 * x), y + c * (1 - 2 * y))
    second = (x + c * (1 - 2 * x), y + (1 - c) * (1 - 2 * y))
    return z, x, y, c, first, second


def greet(z, x, y, c, first, second, depth):
    barrier = pltpu.get_barrier_semaphore()

    def signal(dp, mp):
        pl.semaphore_signal(barrier, inc=1, device_id=(dp, mp), device_id_type=MESH)

    signal(z * 2 + first[0], first[1] * 2 + c)
    signal(z * 2 + second[0], second[1] * 2 + c)
    signal(z * 2 + x, y * 2 + 1 - c)
    pl.when(z > 0)(lambda: signal((z - 1) * 2 + x, y * 2 + c))
    pl.when(z < depth - 1)(lambda: signal((z + 1) * 2 + x, y * 2 + c))
    peers = 3 + jnp.minimum(z, 1) + jnp.minimum(depth - 1 - z, 1)
    pl.semaphore_wait(barrier, peers)


def peers_greet(dp_count, mp_count):
    dp, mp = lax.axis_index("dp"), lax.axis_index("mp")
    barrier = pltpu.get_barrier_semaphore()
    for hop in range(1, dp_count):
        pl.semaphore_signal(
            barrier, inc=1, device_id=(lax.rem(dp + hop, dp_count), mp), device_id_type=MESH
        )
    for hop in range(1, mp_count):
        pl.semaphore_signal(
            barrier, inc=1, device_id=(dp, lax.rem(mp + hop, mp_count)), device_id_type=MESH
        )
    pl.semaphore_wait(barrier, dp_count + mp_count - 2)


class Round:
    def __init__(self, axis, count, source, target, send, recv, base):
        self.me = lax.axis_index(axis)
        self.axis, self.count, self.source, self.target = axis, count, source, target
        self.send, self.recv, self.base = send, recv, base

    def moves(self):
        for hop in range(1, self.count):
            peer = lax.rem(self.me + hop, self.count)
            other = {"dp": (peer, lax.axis_index("mp")), "mp": (lax.axis_index("dp"), peer)}[self.axis]
            yield pltpu.make_async_remote_copy(
                src_ref=self.source(peer), dst_ref=self.target.at[self.me],
                send_sem=self.send.at[self.base + hop], recv_sem=self.recv.at[self.base + hop],
                device_id=other, device_id_type=MESH,
            )

    def push(self):
        for move in self.moves():
            move.start()

    def wait(self):
        for hop in range(1, self.count):
            slot = self.target.at[lax.rem(self.me + self.count - hop, self.count)]
            pltpu.make_async_copy(slot, slot, self.recv.at[self.base + hop]).wait()

    def finish(self):
        for move in self.moves():
            move.wait_send()


def gather_kernel(
    depth, mp_count, wa_ref, wf_ref, info_ref, emb_ref, t1_ref, b1_ref, t2_ref, part_ref, tail_ref, mcol_ref,
    wa_all, wf_all, mod_ref, tails_ref, pre_ref, cond_ref, scaled_ref, infos_ref, hid_ref,
    info_buf, pre_sum, cond_sum, tail_buf, scaled_buf, hid_buf, mod_part, mod_sum, mod_buf,
    recv, send, local, little_recv, little_send,
):
    dp_count = 2 * depth
    z, x, y, c, first, second = coordinates()
    dp, mp = lax.axis_index("dp"), lax.axis_index("mp")
    rows = wa_ref.shape[0]
    images = emb_ref.shape[0]
    peers_greet(dp_count, mp_count)

    bases = iter(range(0, 64 * dp_count, dp_count))
    little = lambda axis, count, source, target: Round(
        axis, count, source, target, little_send, little_recv, next(bases)
    )
    own = lambda buf, me: lambda peer: buf.at[me]
    info = little("dp", dp_count, own(info_buf, dp), info_buf)
    pre_r = little("mp", mp_count, own(pre_sum, mp), pre_sum)
    tail_r = little("mp", mp_count, own(tail_buf, mp), tail_buf)
    cond_r = little("mp", mp_count, own(cond_sum, mp), cond_sum)
    scaled_a = little("dp", dp_count, own(scaled_buf, dp), scaled_buf)
    hid_a = little("dp", dp_count, own(hid_buf, dp), hid_buf)
    mod_r = little("dp", dp_count, lambda peer: mod_part.at[peer], mod_sum)
    mod_a = little("mp", mp_count, own(mod_buf, mp), mod_buf)
    rounds = (info, pre_r, tail_r, cond_r, scaled_a, hid_a, mod_r, mod_a)
    total = lambda buf, count: functools.reduce(lambda a, b: a + b, [buf[i] for i in range(count)])

    def begin():
        info_buf[dp] = info_ref[...]
        info.push()
        pre_sum[mp] = dot(emb_ref[...], t1_ref[...]) + b1_ref[...]
        pre_r.push()
        tail_buf[mp] = tail_ref[...]
        tail_r.push()

    def hidden():
        pre_r.wait()
        pre = total(pre_sum, mp_count)
        pre_ref[...] = pre
        act = (pre * lax.logistic(pre)).astype(LOW)
        cond_sum[mp] = dot(act, t2_ref[...]) + part_ref[...]
        cond_r.push()
        hid_buf[dp] = act

    def condition():
        cond_r.wait()
        cond = total(cond_sum, mp_count)
        cond_ref[...] = cond
        scaled_buf[dp] = (cond * lax.logistic(cond)).astype(LOW)
        scaled_a.push()

    def modulate():
        scaled_a.wait()
        scaled = scaled_buf[...].reshape(dp_count * images, D)
        row = lax.broadcasted_iota(jnp.int32, (D, rows), 0)
        col = lax.broadcasted_iota(jnp.int32, (D, rows), 1)
        pick = (row == col + dp * rows).astype(F32).astype(LOW)
        mine = dot(scaled, pick).astype(LOW)
        mod_part[...] = dot(mine, mcol_ref[...]).reshape(mod_part.shape)
        mod_sum[dp] = mod_part[dp]
        mod_r.push()

    def collect():
        mod_r.wait()
        mod_buf[mp] = total(mod_sum, dp_count)
        mod_a.push()
        hid_a.push()

    hooks = (hidden, condition, modulate, collect)

    sent = []
    corner = (first[0] + second[0] - x, first[1] + second[1] - y)
    spots = {"here": (x, y), "first": first, "second": second, "corner": corner}
    ids = {"here": 0, "first": 1, "second": 2, "corner": 3}
    swapped = {"here": 0, "first": 2, "second": 1, "corner": 3}
    groups = [(wa_ref, wa_all, 0, LINE_FIRST[0])]
    groups += [(wf_ref, wf_all, i * STEP, LINE_FIRST[1 + i]) for i in range(wf_ref.shape[1] // STEP)]
    count = len(groups)

    def slot(g, zz, spot, core):
        _, ref, column, _ = groups[g]
        return ref.at[spot[1] * 2 + core, pl.ds((zz * 2 + spot[0]) * rows, rows), pl.ds(column, STEP)]

    def mine(g):
        return groups[g][0].at[:, pl.ds(groups[g][2], STEP)]

    def copy(g, zz, kind, route, cond=None, own=False):
        plane, sem_kind = 0, kind
        if route == "up":
            target = ((z + 1) * 2 + x, mp)
        elif route == "down":
            target = ((z - 1) * 2 + x, mp)
        elif route == "first":
            target, sem_kind = (z * 2 + first[0], first[1] * 2 + c), "first"
        elif route == "second":
            target = (z * 2 + second[0], second[1] * 2 + c)
            sem_kind = "second" if kind == "here" else "corner"
        else:
            target, plane = (dp, y * 2 + 1 - c), 1
        made = pltpu.make_async_remote_copy(
            src_ref=mine(g) if own else slot(g, zz, spots[kind], c), dst_ref=slot(g, zz, spots[kind], c),
            send_sem=send.at[len(sent)], recv_sem=recv.at[g, plane, ids[sem_kind], zz],
            device_id=target, device_id_type=MESH,
        )
        sent.append((made, cond))
        if cond is None:
            made.start()
        else:
            pl.when(cond)(made.start)

    def arrive(g, zz, kind, cond=None, plane=0):
        dst = slot(g, zz, spots[kind], c if plane == 0 else 1 - c)
        sem = recv.at[g, plane, ids[kind] if plane == 0 else swapped[kind], zz]
        wait = pltpu.make_async_copy(dst, dst, sem)
        if cond is None:
            wait.wait()
        else:
            pl.when(cond)(wait.wait)

    def sides(k):
        below, above = jnp.maximum(z - k, 0), jnp.minimum(z + k, depth - 1)
        return ((below, z >= k, "up", z < depth - 1), (above, z < depth - k, "down", z > 0))[: 1 if k == 0 else 2]

    def stage(g, k):
        line_first = groups[g][3]
        if k == 0:
            pltpu.make_async_copy(mine(g), slot(g, z, spots["here"], c), local.at[g]).start()
            copy(g, z, "here", "first", None, True)
            copy(g, z, "here", "up", z < depth - 1, True)
            copy(g, z, "here", "down", z > 0, True)
            copy(g, z, "here", "second", None, True)
            copy(g, z, "here", "core", None, True)
        if k == 1 and not line_first:
            arrive(g, z, "first")
            copy(g, z, "first", "up", z < depth - 1)
            copy(g, z, "first", "down", z > 0)
            copy(g, z, "first", "second")
            copy(g, z, "first", "core")
        if 0 < k < depth:
            for kind in ("here",):
                for zz, cond, route, more in sides(k):
                    arrive(g, zz, kind, cond)
                    copy(g, zz, kind, route, cond & more)
                    if line_first:
                        copy(g, zz, kind, "first", cond)
                    copy(g, zz, kind, "second", cond)
                    copy(g, zz, kind, "core", cond)
        if line_first and 0 <= k - 1 < depth:
            for zz, cond, _, _ in sides(k - 1):
                arrive(g, zz, "first", cond)
                copy(g, zz, "first", "second", cond)
                copy(g, zz, "first", "core", cond)
        if not line_first and 0 < k - 1 < depth:
            for zz, cond, route, more in sides(k - 1):
                arrive(g, zz, "first", cond)
                copy(g, zz, "first", route, cond & more)
                copy(g, zz, "first", "second", cond)
                copy(g, zz, "first", "core", cond)
        if 0 <= k - 2 < depth:
            for zz, cond, _, _ in sides(k - 2):
                for kind in ("second", "corner"):
                    arrive(g, zz, kind, cond)
                    copy(g, zz, kind, "core", cond)

    begin()
    for moment in range(depth + 2 + count - 1):
        for g in range(count):
            if 0 <= moment - g < depth + 2:
                stage(g, moment - g)
        for number, hook in enumerate(hooks):
            if HOOKS[number] == moment:
                hook()
    mod_a.wait()
    hid_a.wait()
    info.wait()
    tail_r.wait()
    mod_ref[...] = mod_buf[...]
    tails_ref[...] = tail_buf[...]
    scaled_ref[...] = scaled_buf[...]
    infos_ref[...] = info_buf[...]
    hid_ref[...] = hid_buf[...]
    for g in range(count):
        for zz in range(depth):
            for kind in ("here", "first", "second", "corner"):
                arrive(g, zz, kind, None, 1)
        pltpu.make_async_copy(mine(g), slot(g, z, spots["here"], c), local.at[g]).wait()
    for made, cond in sent:
        if cond is None:
            made.wait_send()
        else:
            pl.when(cond)(made.wait_send)
    for one in rounds:
        one.finish()


def gather_pallas(wa, wf, small, dp, mp, collective_id=0):
    depth = dp // 2
    groups = 1 + wf.shape[1] // STEP
    images, width = small[1].shape[0], small[7].shape[1]
    tail = small[6].shape[0]
    shapes = [
        ((mp, images, width), F32), ((mp, tail, D), LOW), ((images, D), F32), ((images, D), F32),
        ((dp, images, D), LOW), ((dp, 8, 128), F32), ((dp, images, D), LOW),
    ]
    return pl.pallas_call(
        functools.partial(gather_kernel, depth, mp),
        out_shape=[jax.ShapeDtypeStruct((mp, dp * s.shape[0], s.shape[1]), s.dtype) for s in (wa, wf)]
        + [jax.ShapeDtypeStruct(*s) for s in shapes],
        in_specs=[pl.BlockSpec(memory_space=pl.ANY)] * 2 + [pl.BlockSpec(memory_space=pltpu.VMEM)] * 8,
        out_specs=[pl.BlockSpec(memory_space=pl.ANY)] * 2 + [pl.BlockSpec(memory_space=pltpu.VMEM)] * 7,
        scratch_shapes=[
            pltpu.VMEM((dp, 8, 128), F32), pltpu.VMEM((mp, images, D), F32), pltpu.VMEM((mp, images, D), F32),
            pltpu.VMEM((mp, tail, D), LOW), pltpu.VMEM((dp, images, D), LOW), pltpu.VMEM((dp, images, D), LOW),
            pltpu.VMEM((dp, images, width), F32), pltpu.VMEM((dp, images, width), F32),
            pltpu.VMEM((mp, images, width), F32),
            pltpu.SemaphoreType.DMA((groups, 2, 4, depth)),
            pltpu.SemaphoreType.DMA((groups * 64,)),
            pltpu.SemaphoreType.DMA((groups,)),
            pltpu.SemaphoreType.DMA((8 * dp,)),
            pltpu.SemaphoreType.DMA((8 * dp,)),
        ],
        compiler_params=pltpu.CompilerParams(
            collective_id=collective_id, has_side_effects=True, vmem_limit_bytes=48 * 1024 * 1024
        ),
        name="gather_weights",
    )(wa, wf, *small)


TOP = 32766.0
RING = 14
ORDER = (
    (0, 0, 0), (0, 0, 2), (0, 0, 1), (0, 2, 0), (0, 0, 3), (1, 0, 0), (0, 2, 2), (2, 0, 3), (1, 0, 1), (0, 2, 1),
    (0, 1, 0), (1, 1, 0), (1, 1, 1), (1, 2, 0), (2, 0, 0), (1, 2, 1), (1, 0, 2), (0, 1, 2), (2, 1, 1), (0, 1, 1),
    (1, 0, 3), (1, 3, 1), (1, 2, 2), (2, 0, 1), (1, 1, 2), (0, 3, 0), (2, 1, 0), (2, 1, 3), (0, 1, 3), (2, 0, 2),
    (0, 3, 1), (0, 3, 2), (2, 2, 0), (1, 2, 3), (2, 2, 1), (1, 3, 0), (2, 1, 2), (2, 2, 2), (1, 3, 2), (0, 2, 3),
    (2, 2, 3), (2, 3, 0), (2, 3, 1), (1, 1, 3), (2, 3, 2), (0, 3, 3), (1, 3, 3), (2, 3, 3),
)


def lookup(values, base, t):
    digits = {4: 15, 64: 5}[base]
    words = [
        sum(v * base**i for i, v in enumerate(values[at : at + digits])) for at in range(0, len(values), digits)
    ]
    word = functools.reduce(lambda a, iw: jnp.where(t // digits == iw[0], iw[1], a), enumerate(words), 0)
    unit = functools.reduce(lambda a, i: jnp.where(t % digits == i, base**i, a), range(digits), 1)
    return word // unit % base


def encode(value):
    peak = jnp.maximum(jnp.max(jnp.abs(value), 0, keepdims=True), 1e-30)
    return jnp.round(value * (TOP / peak)).astype(jnp.int32).astype(jnp.int16), peak * (1.0 / TOP)


def decode(code, unit):
    return code.astype(jnp.int32).astype(F32) * unit


def weight_grad_kernel(
    depth, widths, mp_count, at_ref, pt_ref, mt_ref, ot_ref, ya_ref, yf_ref, gmod_ref, mod_ref, t2_ref, cond_ref, pre_ref,
    out_ref, vec_ref,
    x_all, ya_all, yf_all, work, q_send, u_send, q_recv, u_recv,
    gmod, panel, scaled_send, scaled_recv, joined, own_vec, hid_part, vec_buf,
    moves, swaps, landing, send, recv, panel_sem, little_send, little_recv,
):
    z, x, y, c, first, second = coordinates()
    dp_count = 2 * depth
    peers_greet(dp_count, mp_count)
    rows = out_ref.shape[1]
    x_refs = (at_ref, pt_ref, mt_ref, ot_ref)
    tokens = at_ref.shape[1]
    width_a, width_f = widths
    here = (x, y)
    corner = (first[0] + second[0] - x, first[1] + second[1] - y)
    mate = (z * 2 + x, y * 2 + 1 - c)
    total = len(ORDER)

    own, theirs = pl.ds(0, tokens), pl.ds(tokens, tokens)
    local, remote = [], []

    def trade(mine, give, to, land):
        n = len(local)
        remote.append(pltpu.make_async_remote_copy(
            src_ref=give, dst_ref=land, send_sem=swaps.at[n], recv_sem=landing.at[n],
            device_id=mate, device_id_type=MESH,
        ))
        local.append(pltpu.make_async_copy(mine, to, moves.at[n]))
        remote[-1].start()
        local[-1].start()

    def trade_x(i):
        trade(x_refs[i], x_refs[i], x_all.at[i, :, own], x_all.at[i, :, theirs])

    def trade_y(ref, full, j):
        trade(ref.at[2 * j + c], ref.at[2 * j + 1 - c], full.at[j, own, :], full.at[j, theirs, :])

    trade_x(2)
    trade_y(yf_ref, yf_all, 1 - y)
    trade_x(3)
    trade_x(0)
    trade_x(1)
    trade_y(ya_ref, ya_all, 1 - y)
    trade_y(yf_ref, yf_all, y)
    trade_y(ya_ref, ya_all, y)
    waits, known = [], set()
    for t, (g, kind, _) in enumerate(ORDER):
        need = [{0, 1}, {0, 1, 2}, {3, 4, 5}][g] | (set() if kind == 0 else {7} if g == 2 else {6})
        if need - known:
            waits.append((t, sorted(need - known)))
            known |= need

    def ready(numbers):
        for n in numbers:
            local[n].wait()
            remote[n].wait_recv()

    codes = tuple(16 * g + 4 * kind + j for g, kind, j in ORDER)

    def plan(t):
        code = lookup(codes, 64, t)
        g, kind, j = code // 16, code // 4 % 4, code % 4
        falling = jnp.where(depth - 1 - j <= z, depth - 2 - j, depth - 1 - j)
        rising = jnp.where(j >= z, j + 1, j)
        zz = jnp.where(z * 2 < depth, falling, rising)
        zz = jnp.where(j == depth - 1, z, zz)
        pick = lambda i: jnp.where(
            kind == 0, corner[i], jnp.where(kind == 1, second[i], jnp.where(kind == 2, first[i], here[i]))
        )
        return g, kind, zz, pick(0), pick(1)

    def product(g, zz, xx, yy):
        cut = pl.ds((zz * 2 + xx) * rows, rows)

        @pl.when(g == 0)
        def _():
            work[...] = dot(x_all[2, cut, :], yf_all[yy, :, :STEP])

        @pl.when(g == 1)
        def _():
            middle = 2 * width_f - STEP
            work[:, :middle] = dot(x_all[2, cut, :], yf_all[yy, :, STEP : 2 * width_f])
            work[:, middle:] = dot(x_all[3, cut, :], yf_all[yy, :, 2 * width_f :])

        @pl.when(g == 2)
        def _():
            edge = 3 * width_a
            low, high = edge // 128 * 128, -(-edge // 128) * 128
            left = dot(x_all[0, cut, :], ya_all[yy, :, :high])
            right = dot(x_all[1, cut, :], ya_all[yy, :, low:])
            lane = lax.broadcasted_iota(jnp.int32, (rows, high - low), 1)
            work[:, :low] = left[:, :low]
            work[:, low:high] = jnp.where(lane < edge - low, left[:, low:], right[:, : high - low])
            work[:, high:] = right[:, high - low :]

    def sent(slot):
        return (
            pltpu.make_async_copy(q_send.at[slot], q_send.at[slot], send.at[0, slot]),
            pltpu.make_async_copy(u_send.at[slot], u_send.at[slot], send.at[1, slot]),
        )

    def ship(t, g, dst_slot, target):
        slot = t % RING

        @pl.when(t >= RING)
        def _():
            for move in sent(slot):
                move.wait()

        code, unit = encode(work[...])
        q_send[slot] = code
        u_send[slot] = unit
        for i, (a, b) in enumerate(((q_send, q_recv), (u_send, u_recv))):
            pltpu.make_async_remote_copy(
                src_ref=a.at[slot], dst_ref=b.at[g, dst_slot],
                send_sem=send.at[i, slot], recv_sem=recv.at[i, g, dst_slot],
                device_id=target, device_id_type=MESH,
            ).start()

    def landed(g, slot):
        pltpu.make_async_copy(q_recv.at[g, slot], q_recv.at[g, slot], recv.at[0, g, slot]).wait()
        pltpu.make_async_copy(u_recv.at[g, slot], u_recv.at[g, slot], recv.at[1, g, slot]).wait()
        work[...] += decode(q_recv[g, slot], u_recv[g, slot])

    dp, mp = lax.axis_index("dp"), lax.axis_index("mp")
    bases = iter(range(0, 64 * dp_count, dp_count))
    little = lambda axis, count, source, target: Round(
        axis, count, source, target, little_send, little_recv, next(bases)
    )
    own_slot = lambda buf, me: lambda peer: buf.at[me]
    gmod_a = little("dp", dp_count, own_slot(gmod, dp), gmod)
    scaled_r = little("dp", dp_count, lambda peer: scaled_send.at[peer], scaled_recv)
    vec_m = little("mp", mp_count, own_slot(own_vec, mp), own_vec)
    hid_r = little("mp", mp_count, own_slot(hid_part, mp), hid_part)
    vec_a = little("dp", dp_count, own_slot(vec_buf, dp), vec_buf)
    lines = gmod_ref.shape[0]
    images = lines // 8

    def panels(count, source, use):
        fetch = lambda i: pltpu.make_async_copy(source(i), panel.at[i % 2], panel_sem.at[i % 2])
        fetch(0).start()
        for i in range(count):
            if i + 1 < count:
                fetch(i + 1).start()
            fetch(i).wait()
            use(i, panel.at[i % 2])

    def one_hot(shape, hit):
        row, col = (lax.broadcasted_iota(jnp.int32, shape, i) for i in range(2))
        return hit(row, col).astype(F32).astype(LOW)

    def begin():
        gmod[dp] = gmod_ref[...]
        gmod_a.push()

    def scaled_grad():
        gmod_a.wait()
        every = gmod[...].reshape(dp_count * lines, D)
        scaled_send[...] = jnp.zeros(scaled_send.shape, F32)

        def use(j, piece):
            hit = lambda r, q: (r // 8 == q // lines) & (q % lines == j * images + r % 8) & (r % 8 < images)
            part = dot(one_hot((8 * dp_count, dp_count * lines), hit), every).astype(LOW)
            scaled_send[...] += dot_nt(part, piece[...]).reshape(scaled_send.shape)

        panels(8, lambda j: mod_ref.at[:, pl.ds(j * D, D)], use)
        scaled_recv[dp] = scaled_send[dp]
        scaled_r.push()

    def vector_grad():
        scaled_r.wait()
        for d in range(dp_count):
            joined[:, d * rows : (d + 1) * rows] = scaled_recv[d]
        own_vec[mp] = (joined[...] * silu_slope(cond_ref[mp])).astype(LOW).astype(F32)
        vec_m.push()

    def hidden_grad():
        vec_m.wait()
        vectors = own_vec[...].reshape(8 * mp_count, D).astype(LOW)
        def use(i, piece):
            hid_part[mp, :, i * rows : (i + 1) * rows] = dot_nt(vectors, piece[...])

        panels(D // rows, lambda i: t2_ref.at[pl.ds(i * rows, rows), :], use)
        hid_r.push()

    def first_grad():
        hid_r.wait()
        grad = functools.reduce(lambda a, b: a + b, [hid_part[i] for i in range(mp_count)])
        grad_pre = (grad * silu_slope(pre_ref[...])).astype(LOW)
        vectors = own_vec[...].reshape(8 * mp_count, D).astype(LOW)
        hit = lambda r, q: (r // images == q // 8) & (r % images == q % 8)
        pick = one_hot((images * mp_count, 8 * mp_count), hit)
        count = images * mp_count
        vec_buf[dp, :count, :] = dot(pick, vectors).astype(LOW)
        vec_buf[dp, count:, :] = dot(pick, grad_pre).astype(LOW)
        vec_a.push()

    hooks = ((0, begin), (8, scaled_grad), (15, vector_grad), (20, hidden_grad), (27, first_grad))

    to_second = (z * 2 + second[0], second[1] * 2 + c)
    to_first = (z * 2 + first[0], first[1] * 2 + c)
    to_up = ((z + 1) * 2 + x, y * 2 + c)
    to_down = ((z - 1) * 2 + x, y * 2 + c)
    kept, passed = 2 * depth, 3 * depth + 1
    after_line = passed + depth + 1

    def step(t, _):
        g, kind, zz, xx, yy = plan(t)
        for at, numbers in waits:
            pl.when(t == at)(functools.partial(ready, numbers))
        for at, hook in hooks:
            pl.when(t == at)(hook)
        product(g, zz, xx, yy)
        line_first = g < 2
        late, mine = kind >= 2, zz == z
        along = late & ((kind == 3) | line_first)
        line = jnp.where(kind == 3, kept, passed)

        @pl.when(kind < 2)
        def _():
            ship(t, g, kind * depth + zz, to_second)

        @pl.when(late)
        def _():
            landed(g, (kind - 2) * depth + zz)

        @pl.when((kind == 3) & (jnp.logical_not(line_first) | mine))
        def _():
            landed(g, jnp.where(line_first, after_line, passed + zz))

        @pl.when(along & (zz >= z) & (z > 0))
        def _():
            landed(g, line + zz)

        @pl.when(along & (zz <= z) & (z < depth - 1))
        def _():
            landed(g, line + jnp.where(mine, depth, zz))

        @pl.when(along & (zz > z))
        def _():
            ship(t, g, line + zz, to_up)

        @pl.when(along & (zz < z))
        def _():
            ship(t, g, line + jnp.where(zz == z - 1, depth, zz), to_down)

        @pl.when((kind == 2) & (jnp.logical_not(line_first) | mine))
        def _():
            ship(t, g, jnp.where(line_first, after_line, passed + zz), to_first)

        @pl.when((kind == 3) & mine)
        def _():
            out_ref[g] = work[...]

        return 0

    lax.fori_loop(0, total, step, 0)

    def drain(slot, _):
        for move in sent(slot):
            move.wait()
        return 0

    lax.fori_loop(0, RING, drain, 0)
    for move in remote:
        move.wait_send()
    vec_a.wait()
    vec_ref[...] = vec_buf[...]
    for one in (gmod_a, scaled_r, vec_m, hid_r, vec_a):
        one.finish()


def weight_grads(turned, ya, yf, grad_mod, mod_rows, second, cond, pre, dp, collective_id=1):
    depth, mp = dp // 2, ya.shape[0]
    tokens = turned[0].shape[1]
    rows = D // dp
    slots = 4 * depth + 3
    images = grad_mod.shape[0] // 8
    hbm, vmem = pl.BlockSpec(memory_space=pl.ANY), pl.BlockSpec(memory_space=pltpu.VMEM)
    vectors = (dp, 2 * images * mp, D)
    return pl.pallas_call(
        functools.partial(weight_grad_kernel, depth, (ya.shape[2] // 4, yf.shape[2] // 3), mp),
        out_shape=[jax.ShapeDtypeStruct((3, rows, STEP), F32), jax.ShapeDtypeStruct(vectors, LOW)],
        in_specs=[hbm] * 6 + [vmem, hbm, hbm, vmem, vmem],
        out_specs=[vmem, vmem],
        scratch_shapes=[
            pltpu.VMEM((4, D, 2 * tokens), LOW),
            pltpu.VMEM((2, 2 * tokens, ya.shape[2]), LOW),
            pltpu.VMEM((2, 2 * tokens, yf.shape[2]), LOW),
            pltpu.VMEM((rows, STEP), F32),
            pltpu.VMEM((RING, rows, STEP), jnp.int16),
            pltpu.VMEM((RING, 1, STEP), F32),
            pltpu.VMEM((3, slots, rows, STEP), jnp.int16),
            pltpu.VMEM((3, slots, 1, STEP), F32),
            pltpu.VMEM((dp, *grad_mod.shape), LOW),
            pltpu.VMEM((2, rows, D), LOW),
            pltpu.VMEM((dp, 8, rows), F32),
            pltpu.VMEM((dp, 8, rows), F32),
            pltpu.VMEM((8, D), F32),
            pltpu.VMEM((mp, 8, D), F32),
            pltpu.VMEM((mp, 8 * mp, D), F32),
            pltpu.VMEM(vectors, LOW),
            pltpu.SemaphoreType.DMA((8,)),
            pltpu.SemaphoreType.DMA((8,)),
            pltpu.SemaphoreType.DMA((8,)),
            pltpu.SemaphoreType.DMA((2, RING)),
            pltpu.SemaphoreType.DMA((2, 3, slots)),
            pltpu.SemaphoreType.DMA((2,)),
            pltpu.SemaphoreType.DMA((5 * dp,)),
            pltpu.SemaphoreType.DMA((5 * dp,)),
        ],
        compiler_params=pltpu.CompilerParams(
            collective_id=collective_id, has_side_effects=True, vmem_limit_bytes=62 * 1024 * 1024
        ),
        name="weight_grads",
    )(*turned, ya, yf, grad_mod, mod_rows, second, cond, pre)


def sum_kernel(mp_count, dp_count, in_ref, out_ref, over_dp, over_mp, send, recv):
    dp, mp = lax.axis_index("dp"), lax.axis_index("mp")
    peers_greet(dp_count, mp_count)
    first = Round("dp", dp_count, lambda peer: over_dp.at[dp], over_dp, send, recv, 0)
    second = Round("mp", mp_count, lambda peer: over_mp.at[mp], over_mp, send, recv, dp_count)
    over_dp[dp] = in_ref[...]
    first.push()
    first.wait()
    over_mp[mp] = functools.reduce(lambda a, b: a + b, [over_dp[i] for i in range(dp_count)])
    second.push()
    second.wait()
    out_ref[...] = functools.reduce(lambda a, b: a + b, [over_mp[i] for i in range(mp_count)])
    first.finish()
    second.finish()


def sum_pallas(values, dp, mp, collective_id=2):
    return pl.pallas_call(
        functools.partial(sum_kernel, mp, dp),
        out_shape=jax.ShapeDtypeStruct(values.shape, F32),
        in_specs=[pl.BlockSpec(memory_space=pltpu.VMEM)],
        out_specs=pl.BlockSpec(memory_space=pltpu.VMEM),
        scratch_shapes=[
            pltpu.VMEM((dp, *values.shape), F32), pltpu.VMEM((mp, *values.shape), F32),
            pltpu.SemaphoreType.DMA((dp + mp,)), pltpu.SemaphoreType.DMA((dp + mp,)),
        ],
        compiler_params=pltpu.CompilerParams(collective_id=collective_id, has_side_effects=True),
        name="sum_scalars",
    )(values)


SLAB = 64
VMEM_LIMIT = 60 * 1024 * 1024


def whole(shape):
    return pl.BlockSpec(shape, lambda m: (0,) * len(shape), pipeline_mode=pl.Buffered(1))


def by_block(*shape):
    return pl.BlockSpec((1, *shape), lambda m: (m, 0, 0))


def dot(left, right):
    return lax.dot_general(left, right, (((1,), (0,)), ((), ())), preferred_element_type=F32)


def dot_nt(left, right):
    return lax.dot_general(left, right, (((1,), (1,)), ((), ())), preferred_element_type=F32)


def dot_tn(left, right):
    return lax.dot_general(left, right, (((0,), (0,)), ((), ())), preferred_element_type=F32)


def slabs(tokens, body, sums=0):
    totals = []
    for block in range(tokens // PAIR):

        def step(i, carry, block=block):
            rows = pl.ds(pl.multiple_of(block * PAIR + i * SLAB, SLAB), SLAB)
            lead, values = body(block, rows)
            head, rest = carry
            head = tuple(h + jnp.sum(jnp.where(lead, v, 0.0), 0, keepdims=True) for h, v in zip(head, values))
            rest = tuple(r + jnp.sum(jnp.where(lead, 0.0, v), 0, keepdims=True) for r, v in zip(rest, values))
            return head, rest

        zero = tuple(jnp.zeros((1, D), F32) for _ in range(sums))
        totals.extend(lax.fori_loop(0, PAIR // SLAB, step, (zero, zero)))
    return totals


def spread(mod_ref, j, block, lead):
    row = lambda i: mod_ref[2 * block + i : 2 * block + i + 1, j * D : (j + 1) * D]
    return jnp.where(lead, row(0), row(1))


def turn(values, cos_row, sin_row, direction):
    quarter = HD // 4
    width = values.shape[1]
    lane = lax.broadcasted_iota(jnp.int32, values.shape, 1)
    ahead = pltpu.roll(values, width - quarter, 1)
    behind = pltpu.roll(values, quarter, 1)
    partner = jnp.where(lane % (2 * quarter) < quarter, ahead, behind)
    return values * cos_row + partner * (sin_row * direction)


def same_image(even_col, even_row, block):
    rows = slice(block * PAIR, (block + 1) * PAIR)
    return even_col[rows, :1] == even_row[block, :1, :]


def softmax(query, key, same):
    scores = jnp.where(same, dot_nt(query, key) * HD ** (-0.5), -1e30)
    expo = jnp.exp(scores - jnp.max(scores, -1, keepdims=True))
    return expo * (1.0 / jnp.sum(expo, -1, keepdims=True))


def attn_forward_kernel(
    patch_ref, prow_ref, pbias_ref, mod_ref, w_ref, cos_ref, sin_ref, col_ref, row_ref,
    x0_ref, x1_ref, proj_ref, m_ref, at_ref, mt_ref, qkv_ref, att_ref, a_ref,
):
    width = att_ref.shape[2]
    tokens = a_ref.shape[0]
    step, last = pl.program_id(0), pl.num_programs(0) - 1

    @pl.when(step == 0)
    def _():
        x0_ref[...] = dot_tn(patch_ref[...], prow_ref[...]) + pbias_ref[...]

        def body(block, rows):
            lead = col_ref[rows, :1] != 0
            normed, _ = layer_norm(x0_ref[rows, :])
            shift, scale = spread(mod_ref, 0, block, lead), spread(mod_ref, 1, block, lead)
            a_ref[rows, :] = (normed * (1.0 + scale) + shift).astype(LOW)
            return lead, ()

        slabs(tokens, body)
        at_ref[...] = a_ref[...].T

    made = dot(a_ref[...], w_ref[0, :, : 3 * width])
    qkv_ref[0, :, : 2 * width] = turn(made[:, : 2 * width], cos_ref[...], sin_ref[...], 1.0).astype(LOW)
    qkv_ref[0, :, 2 * width :] = made[:, 2 * width :].astype(LOW)
    for block in range(tokens // PAIR):
        same = same_image(col_ref, row_ref, block)
        rows = slice(block * PAIR, (block + 1) * PAIR)
        for head in range(width // HD):
            take = lambda i: qkv_ref[0, rows, i * width + head * HD : i * width + (head + 1) * HD]
            probs = softmax(take(0), take(1), same).astype(LOW)
            att_ref[0, rows, head * HD : (head + 1) * HD] = dot(probs, take(2)).astype(LOW)
    part = dot_nt(att_ref[0], w_ref[0, :, 3 * width :])

    @pl.when(step == 0)
    def _():
        proj_ref[...] = part

    @pl.when(step > 0)
    def _():
        proj_ref[...] += part

    @pl.when(step == last)
    def _():
        def body(block, rows):
            lead = col_ref[rows, :1] != 0
            x_one = x0_ref[rows, :] + spread(mod_ref, 2, block, lead) * proj_ref[rows, :]
            x1_ref[rows, :] = x_one
            normed, _ = layer_norm(x_one)
            shift, scale = spread(mod_ref, 3, block, lead), spread(mod_ref, 4, block, lead)
            m_ref[rows, :] = (normed * (1.0 + scale) + shift).astype(LOW)
            return lead, ()

        slabs(tokens, body)
        mt_ref[...] = m_ref[...].T


def attn_forward(patches, patch_rows, patch_bias, modulation, wa_all, tables):
    blocks, _, width = wa_all.shape
    width //= 4
    tokens = patches.shape[1]
    full, turned = (tokens, D), (D, tokens)
    ins = (patches, patch_rows, patch_bias, modulation)
    return pl.pallas_call(
        attn_forward_kernel,
        grid=(blocks,),
        out_shape=[jax.ShapeDtypeStruct(full, F32)] * 3
        + [jax.ShapeDtypeStruct(full, LOW)]
        + [jax.ShapeDtypeStruct(turned, LOW)] * 2
        + [
            jax.ShapeDtypeStruct((blocks, tokens, 3 * width), LOW),
            jax.ShapeDtypeStruct((blocks, tokens, width), LOW),
        ],
        in_specs=[whole(a.shape) for a in ins] + [by_block(D, 4 * width)] + [whole(a.shape) for a in tables],
        out_specs=[whole(full)] * 4
        + [whole(turned)] * 2
        + [by_block(tokens, 3 * width), by_block(tokens, width)],
        scratch_shapes=[pltpu.VMEM(full, LOW)],
        compiler_params=pltpu.CompilerParams(vmem_limit_bytes=VMEM_LIMIT),
        name="attn_forward",
    )(*ins, wa_all, *tables)


def ffn_kernel(
    m_ref, x1_ref, proj_ref, mod_ref, head_ref, target_ref, weight_ref, col_ref, w_ref,
    yf_ref, gx1_ref, gp_ref, gpt_ref, gmot_ref, ghead_ref, loss_ref, sums_ref,
    gu_ref, out_ref, back_ref, low_ref,
):
    width = gu_ref.shape[2] // 2
    tokens = m_ref.shape[0]
    step, count = pl.program_id(0), pl.num_programs(0) // 2

    @pl.when(step < count)
    def _():
        for block in range(tokens // PAIR):
            rows = slice(block * PAIR, (block + 1) * PAIR)
            made = dot(m_ref[rows, :], w_ref[0, :, : 2 * width])
            gu_ref[step, rows, :] = made
            gate, up_val = made[:, :width], made[:, width:]
            hidden = (gate * lax.logistic(gate) * up_val).astype(LOW)
            part = dot_nt(hidden, w_ref[0, :, 2 * width :])

            @pl.when(step == 0)
            def _(part=part, rows=rows):
                out_ref[rows, :] = part

            @pl.when(step > 0)
            def _(part=part, rows=rows):
                out_ref[rows, :] += part

    @pl.when(step == count - 1)
    def _():
        def final_norm(block, rows):
            lead = col_ref[rows, :1] != 0
            x_two = x1_ref[rows, :] + spread(mod_ref, 5, block, lead) * out_ref[rows, :]
            return lead, spread(mod_ref, 7, block, lead), *layer_norm(x_two)

        def before(block, rows):
            lead, scale, normed, _ = final_norm(block, rows)
            low_ref[rows, :] = (normed * (1.0 + scale) + spread(mod_ref, 6, block, lead)).astype(LOW)
            return lead, ()

        slabs(tokens, before)
        diff = dot_nt(head_ref[...], low_ref[...]) - target_ref[...]
        loss = jnp.sum(weight_ref[:1, :] * jnp.mean(diff * diff, 0, keepdims=True), 1, keepdims=True)
        loss_ref[...] = jnp.broadcast_to(loss, loss_ref.shape)
        grad_pred = (2.0 / OUT * diff * weight_ref[1:2, :]).astype(LOW)
        ghead_ref[...] = dot(grad_pred, low_ref[...])
        back_ref[...] = dot_tn(grad_pred, head_ref[...])

        def after(block, rows):
            lead, scale, normed, inv_std = final_norm(block, rows)
            grad_f = back_ref[rows, :]
            grad_x2 = norm_back(grad_f, normed, inv_std, scale)
            gx1_ref[rows, :] = grad_x2
            low_ref[rows, :] = (spread(mod_ref, 5, block, lead) * grad_x2).astype(LOW)
            return lead, (grad_f, grad_f * normed, grad_x2 * out_ref[rows, :])

        for image, rows in enumerate(slabs(tokens, after, 3)):
            for k in range(3):
                sums_ref[k, image : image + 1, :] = rows[k]
        gmot_ref[...] = low_ref[...].T

    @pl.when(step >= count)
    def _():
        for block in range(tokens // PAIR):
            rows = slice(block * PAIR, (block + 1) * PAIR)
            grad_hid = dot(low_ref[rows, :], w_ref[0, :, 2 * width :])
            made = gu_ref[2 * count - 1 - step, rows, :]
            gate, up_val = made[:, :width], made[:, width:]
            sigma = lax.logistic(gate)
            act = gate * sigma
            slope = sigma * (1.0 + gate * (1.0 - sigma))
            yf_ref[0, rows, :width] = (grad_hid * up_val * slope).astype(LOW)
            yf_ref[0, rows, width : 2 * width] = (grad_hid * act).astype(LOW)
            yf_ref[0, rows, 2 * width :] = (act * up_val).astype(LOW)
            part = dot_nt(yf_ref[0, rows, : 2 * width], w_ref[0, :, : 2 * width])

            @pl.when(step == count)
            def _(part=part, rows=rows):
                back_ref[rows, :] = part

            @pl.when(step > count)
            def _(part=part, rows=rows):
                back_ref[rows, :] += part

    @pl.when(step == 2 * count - 1)
    def _():
        def body(block, rows):
            lead = col_ref[rows, :1] != 0
            grad_m = back_ref[rows, :]
            normed, inv_std = layer_norm(x1_ref[rows, :])
            grad_x1 = gx1_ref[rows, :] + norm_back(grad_m, normed, inv_std, spread(mod_ref, 4, block, lead))
            gx1_ref[rows, :] = grad_x1
            gp_ref[rows, :] = (spread(mod_ref, 2, block, lead) * grad_x1).astype(LOW)
            return lead, (grad_m, grad_m * normed, grad_x1 * proj_ref[rows, :])

        for image, rows in enumerate(slabs(tokens, body, 3)):
            for k in range(3):
                sums_ref[3 + k, image : image + 1, :] = rows[k]
        gpt_ref[...] = gp_ref[...].T


def ffn(m_in, x_one, proj, modulation, head_rows, target, weights, even_col, wf_all):
    blocks, _, width = wf_all.shape
    width //= 3
    tokens = m_in.shape[0]
    full, turned = (tokens, D), (D, tokens)
    ins = (m_in, x_one, proj, modulation, head_rows, target, weights, even_col)
    there_and_back = lambda i: (jnp.where(i < blocks, i, 2 * blocks - 1 - i), 0, 0)
    back = lambda i: (jnp.where(i < blocks, blocks - 1, 2 * blocks - 1 - i), 0, 0)
    outs = [
        (full, F32), (full, LOW), (turned, LOW), (turned, LOW),
        ((OUT, D), F32), ((8, 128), F32), ((6, modulation.shape[0], D), F32),
    ]
    return pl.pallas_call(
        ffn_kernel,
        grid=(2 * blocks,),
        out_shape=[jax.ShapeDtypeStruct((blocks, tokens, 3 * width), LOW)]
        + [jax.ShapeDtypeStruct(*o) for o in outs],
        in_specs=[whole(a.shape) for a in ins] + [pl.BlockSpec((1, D, 3 * width), there_and_back)],
        out_specs=[pl.BlockSpec((1, tokens, 3 * width), back)] + [whole(o[0]) for o in outs],
        scratch_shapes=[
            pltpu.VMEM((blocks, tokens, 2 * width), F32),
            pltpu.VMEM(full, F32), pltpu.VMEM(full, F32), pltpu.VMEM(full, LOW),
        ],
        compiler_params=pltpu.CompilerParams(vmem_limit_bytes=VMEM_LIMIT),
        name="feed_forward",
    )(*ins, wf_all)


def attn_backward_kernel(
    grad_ref, gx1_ref, x0_ref, patch_ref, mod_ref, w_ref, qkv_ref, att_ref, cos_ref, sin_ref, col_ref, row_ref,
    out_ref, rows_ref, sums_ref, tmp_ref, back_att, back_ref, low_ref,
):
    width = att_ref.shape[2]
    tokens = grad_ref.shape[0]
    scale = HD ** (-0.5)
    step, last = pl.program_id(0), pl.num_programs(0) - 1
    back_att[...] = dot(grad_ref[...], w_ref[0, :, 3 * width :]).astype(LOW)
    for block in range(tokens // PAIR):
        same = same_image(col_ref, row_ref, block)
        rows = slice(block * PAIR, (block + 1) * PAIR)
        for head in range(width // HD):
            lanes = lambda i: slice(i * width + head * HD, i * width + (head + 1) * HD)
            query, key, value = (qkv_ref[0, rows, lanes(i)] for i in range(3))
            grad = back_att[rows, lanes(0)]
            probs = softmax(query, key, same)
            grad_p = dot_nt(grad, value)
            centre = jnp.sum(probs * grad_p, -1, keepdims=True)
            grad_s = (probs * (grad_p - centre)).astype(LOW)
            tmp_ref[rows, lanes(0)] = dot(grad_s, key) * scale
            tmp_ref[rows, lanes(1)] = dot_tn(grad_s, query) * scale
            tmp_ref[rows, lanes(2)] = dot_tn(probs.astype(LOW), grad)
    out_ref[0, :, : 2 * width] = turn(tmp_ref[:, : 2 * width], cos_ref[...], sin_ref[...], -1.0).astype(LOW)
    out_ref[0, :, 2 * width : 3 * width] = tmp_ref[:, 2 * width :].astype(LOW)
    out_ref[0, :, 3 * width :] = att_ref[0]
    part = dot_nt(out_ref[0, :, : 3 * width], w_ref[0, :, : 3 * width])

    @pl.when(step == 0)
    def _():
        back_ref[...] = part

    @pl.when(step > 0)
    def _():
        back_ref[...] += part

    @pl.when(step == last)
    def _():
        def body(block, rows):
            lead = col_ref[rows, :1] != 0
            grad_a = back_ref[rows, :]
            normed, inv_std = layer_norm(x0_ref[rows, :])
            back = norm_back(grad_a, normed, inv_std, spread(mod_ref, 1, block, lead))
            grad_x0 = (gx1_ref[rows, :] + back).astype(LOW)
            low_ref[rows, :] = grad_x0
            return lead, (grad_a, grad_a * normed, grad_x0.astype(F32))

        bias = jnp.zeros((1, D), F32)
        for image, rows in enumerate(slabs(tokens, body, 3)):
            for k in range(2):
                sums_ref[k, image : image + 1, :] = rows[k]
            bias = bias + rows[2]
        rows_ref[:PATCH_IN, :] = dot(patch_ref[...], low_ref[...])
        rows_ref[PATCH_IN : PATCH_IN + 1, :] = bias
        rows_ref[PATCH_IN + 1 :, :] = jnp.zeros((7, D), F32)


def attn_backward(grad_proj, gx1, x_zero, patches, modulation, wa_all, qkv, att, tables):
    blocks, tokens, width = att.shape
    full = (tokens, D)
    ins = (grad_proj, gx1, x_zero, patches, modulation)
    outs = [((PATCH_IN + 8, D), F32), ((2, modulation.shape[0], D), F32)]
    return pl.pallas_call(
        attn_backward_kernel,
        grid=(blocks,),
        out_shape=[jax.ShapeDtypeStruct((blocks, tokens, 4 * width), LOW)]
        + [jax.ShapeDtypeStruct(*o) for o in outs],
        in_specs=[whole(a.shape) for a in ins]
        + [by_block(D, 4 * width), by_block(tokens, 3 * width), by_block(tokens, width)]
        + [whole(a.shape) for a in tables],
        out_specs=[by_block(tokens, 4 * width)] + [whole(o[0]) for o in outs],
        scratch_shapes=[
            pltpu.VMEM((tokens, 3 * width), F32), pltpu.VMEM((tokens, width), LOW),
            pltpu.VMEM(full, F32), pltpu.VMEM(full, LOW),
        ],
        compiler_params=pltpu.CompilerParams(vmem_limit_bytes=VMEM_LIMIT),
        name="attn_backward",
    )(*ins, wa_all, qkv, att, *tables)


def gather_library(wa, wf, small):
    dp, mp = lax.axis_size("dp"), lax.axis_size("mp")
    info, embed, first, first_bias, second, part, tail, columns = small
    depth = wa.shape[0]

    def one(w):
        full = lax.all_gather(w, BOTH, axis=0)
        full = full.reshape(dp, mp, *w.shape).transpose(1, 0, 2, 3)
        return full.reshape(mp, dp * w.shape[0], w.shape[1])

    over_dp = lambda v: lax.all_gather(v, "dp", axis=0)
    pre = lax.psum(dot(embed, first) + first_bias, "mp")
    cond = lax.psum(dot(jax.nn.silu(pre).astype(LOW), second) + part, "mp")
    scaled_all = over_dp(jax.nn.silu(cond).astype(LOW))
    scaled = scaled_all.reshape(-1, D)
    mine = lax.dynamic_slice_in_dim(scaled, lax.axis_index("dp") * depth, depth, 1)
    mod = lax.psum_scatter(dot(mine, columns), "dp", scatter_dimension=0, tiled=True)
    over_mp = lambda v: lax.all_gather(v, "mp", axis=0)
    return one(wa), one(wf), over_mp(mod), over_mp(tail), pre, cond, scaled_all, over_dp(info), over_dp(jax.nn.silu(pre).astype(LOW))


def sibling(value):
    mp = lax.axis_size("mp")
    return lax.ppermute(value, "mp", [(i, i + 1 - 2 * (i % 2)) for i in range(mp)])


def vector_grads(grad_mod, mod_rows, second, cond, pre):
    images = grad_mod.shape[0] // 8
    group = lax.all_gather(grad_mod.reshape(8, images, D), "mp", axis=1, tiled=True)
    group = group.transpose(1, 0, 2).reshape(cond.shape[0], 8 * D)
    every = lax.all_gather(group, "dp", axis=0, tiled=True)
    scaled = lax.all_gather(dot_nt(every, mod_rows), "dp", axis=1, tiled=True)
    scaled = lax.dynamic_slice_in_dim(scaled, lax.axis_index("dp") * cond.shape[0], cond.shape[0], 0)
    grad_cond = (scaled * silu_slope(cond)).astype(LOW)
    hidden = lax.psum(dot_nt(grad_cond, second), "mp")
    grad_pre = (hidden * silu_slope(pre)).astype(LOW)
    return lax.all_gather(jnp.concatenate([grad_cond, grad_pre], 0), "dp", axis=0)


def plane_grads(turned, ya, yf):
    dp, mp = lax.axis_size("dp"), lax.axis_size("mp")
    core, place = lax.axis_index("mp") % 2, lax.axis_index("mp") // 2
    x_all = jnp.stack(turned)
    x_two = jnp.concatenate([x_all, sibling(x_all)], 2)
    width_a, width_f = ya.shape[2] // 4, yf.shape[2] // 3

    def halves(values):
        split = values.reshape(mp // 2, 2, *values.shape[1:])
        mine = lax.dynamic_index_in_dim(split, core, 1, False)
        theirs = lax.dynamic_index_in_dim(split, 1 - core, 1, False)
        return jnp.concatenate([mine, sibling(theirs)], 1)

    def product(x, values):
        return jnp.einsum("dt,btn->bdn", x, values, preferred_element_type=F32)

    ya_two, yf_two = halves(ya), halves(yf)
    grad_a = jnp.concatenate(
        [product(x_two[0], ya_two[..., : 3 * width_a]), product(x_two[1], ya_two[..., 3 * width_a :])], 2
    )
    grad_f = jnp.concatenate(
        [product(x_two[2], yf_two[..., : 2 * width_f]), product(x_two[3], yf_two[..., 2 * width_f :])], 2
    )
    grad = jnp.stack([grad_f[..., :STEP], grad_f[..., STEP:], grad_a])
    part = lax.psum_scatter(grad, "dp", scatter_dimension=2, tiled=True)
    total = lax.dynamic_index_in_dim(part, place, 1, False)
    for hop in range(1, mp // 2):
        perm = [(i, (i + 2 * hop) % mp) for i in range(mp)]
        out = lax.dynamic_index_in_dim(part, (place + hop) % (mp // 2), 1, False)
        total = total + lax.ppermute(out, "mp", perm)
    return total


def per_device(
    patches, target, segments, positions, classes, timesteps, t_weight, step_count,
    qkv_w, qkv_m, qkv_v, out_w, out_m, out_v, ffn_in_w, ffn_in_m, ffn_in_v,
    ffn_out_w, ffn_out_m, ffn_out_v, mod_w, mod_m, mod_v, table_w, table_m, table_v,
):
    mp_count, dp_count = lax.axis_size("mp"), lax.axis_size("dp")
    mp_index, dp_index = lax.axis_index("mp"), lax.axis_index("dp")
    tokens = patches.shape[1]
    pairs = tokens // PAIR
    images = 2 * pairs
    own_rows = table_w.shape[0]
    depth = mod_w.shape[0]
    width_a, width_f = qkv_w.shape[2], ffn_in_w.shape[2]

    regular = dp_count == 2 * DEPTH and mp_count == 4
    group_images = classes.shape[0]
    wa = jnp.concatenate([qkv_w[0], qkv_w[1], qkv_w[2], out_w.T], 1).astype(LOW)
    wf = jnp.concatenate([ffn_in_w[0], ffn_in_w[1], ffn_out_w.T], 1).astype(LOW)

    table_b = table_w.astype(LOW)
    mod_b = mod_w.astype(LOW)
    gap = D + 16
    padded = lax.dynamic_update_slice(jnp.zeros((2 * gap + own_rows, D), LOW), table_b, (gap, 0))

    def placed(row, count):
        return lax.dynamic_slice_in_dim(padded, row - mp_index * own_rows + gap, count, 0)

    half = FREQ // 2
    freqs = jnp.exp(-math.log(10000.0) * jnp.arange(half, dtype=F32) / half)

    def embedding(times):
        angles = times[:, None] * freqs[None, :]
        return jnp.concatenate([jnp.cos(angles), jnp.sin(angles)], 1).astype(LOW)

    row_ids = mp_index * own_rows + jnp.arange(own_rows, dtype=jnp.int32)
    own_hot = (classes[:, None] == row_ids[None, :]).astype(LOW)
    part = matmul(own_hot, table_b) + placed(ROW_OUT_BIAS, 1).astype(F32)
    info = jnp.zeros((8, 128), F32)
    for i, values in enumerate((classes, timesteps, t_weight)):
        info = info.at[i, :group_images].set(values.astype(F32))
    mod_cols = mod_w.shape[1] // mp_count
    small = (
        info, embedding(timesteps.astype(F32)), placed(ROW_TIME_IN, FREQ),
        placed(ROW_TIME_BIAS, 1).astype(F32), placed(ROW_TIME_OUT, D), part,
        jnp.pad(placed(ROW_PATCH, TAIL), ((0, 64 - TAIL), (0, 0))),
        lax.dynamic_slice_in_dim(mod_b, mp_index * mod_cols, mod_cols, 1),
    )
    if regular:
        gathered = gather_pallas(wa, wf, small, dp_count, mp_count)
    else:
        gathered = gather_library(wa, wf, small)
    wa_all, wf_all, mod_all, tails, pre, cond, scaled, infos, hidden = gathered
    count_all = dp_count * group_images
    scaled = scaled.reshape(count_all, D)
    classes_all, times_all, weights_all = (infos[:, i, :group_images].reshape(-1) for i in range(3))
    tail = jnp.sum(tails.astype(F32), 0)
    mod_own = lax.dynamic_slice_in_dim(mod_all, mp_index * images, images, 1)
    mod_bias = tail[ROW_MOD_BIAS - ROW_PATCH : TAIL].reshape(-1)
    modulation = mod_own.transpose(1, 0, 2).reshape(images, -1) + mod_bias
    patch_rows = tail[:PATCH_IN].astype(LOW)
    patch_bias = tail[PATCH_IN]
    head_rows = tail[PATCH_IN + 1 : PATCH_IN + 1 + OUT].astype(LOW)
    weight_sum = jnp.sum(weights_all)

    ones = jnp.ones((count_all, 1), LOW)
    zeros = lambda n: jnp.zeros((count_all, n), LOW)
    own_cols = lambda a: lax.dynamic_slice_in_dim(a, mp_index * own_rows, own_rows, 1)
    left_pre = own_cols(
        jnp.concatenate([zeros(NCLS), embedding(times_all), ones, zeros(ROWS - ROW_TIME_OUT)], 1)
    )
    class_hot = (classes_all[:, None] == jnp.arange(NCLS, dtype=F32)[None, :]).astype(LOW)
    hidden = hidden.reshape(count_all, D)
    left_cond = own_cols(
        jnp.concatenate(
            [class_hot, zeros(ROW_TIME_OUT - NCLS), hidden, ones, zeros(ROWS - ROW_PATCH)], 1
        )
    )
    own_scaled = lax.dynamic_slice_in_dim(scaled, dp_index * depth, depth, 1)

    own_seg = lax.dynamic_slice_in_dim(segments, mp_index * tokens, tokens)
    own_pos = lax.dynamic_slice_in_dim(positions, mp_index * tokens, tokens, 1)
    even = (own_seg % 2 == 0).reshape(pairs, PAIR)
    heads = 2 * width_a // HD
    cos_row, sin_row = (jnp.tile(t, (1, heads)) for t in rotary_tables(own_pos))
    even_col = even.astype(jnp.int32).reshape(tokens, 1)
    even_row = jnp.broadcast_to(even.astype(jnp.int32)[:, None], (pairs, 8, PAIR))
    tables = (cos_row, sin_row, even_col, even_row)
    x_zero, x_one, proj, m_in, a_turned, m_turned, qkv, att = attn_forward(
        patches, patch_rows, patch_bias[None, :], modulation, wa_all, tables
    )
    first_len = jnp.sum(even.astype(F32), 1)
    own_tw = lax.dynamic_slice_in_dim(t_weight, mp_index * images, images).reshape(pairs, 2)
    per_tok = own_tw / jnp.stack([first_len, PAIR - first_len], 1)
    tok_weight = jnp.where(even, per_tok[:, :1], per_tok[:, 1:]).reshape(1, tokens)
    weights = jnp.concatenate([tok_weight, tok_weight / weight_sum], 0)
    yf, grad_x1, grad_proj, proj_turned, mo_turned, grad_head, loss, sums_f = ffn(
        m_in, x_one, proj, modulation, head_rows, target, weights, even_col, wf_all
    )
    ya, grad_patch, sums_a = attn_backward(
        grad_proj, grad_x1, x_zero, patches, modulation, wa_all, qkv, att, tables
    )
    loss_part = loss[0, 0]
    x_turned = (a_turned, proj_turned, m_turned, mo_turned)
    grad_mod = jnp.concatenate(
        [sums_a[0], sums_a[1], sums_f[5], sums_f[3], sums_f[4], sums_f[2], sums_f[0], sums_f[1]], 0
    ).astype(LOW)
    cond_own = jnp.pad(cond.reshape(mp_count, images, D), ((0, 0), (0, 8 - images), (0, 0)))
    pre_own = jnp.pad(pre.reshape(mp_count, images, D), ((0, 0), (0, 8 - images), (0, 0)))
    if regular:
        summed, vectors = weight_grads(
            x_turned, ya, yf, grad_mod, mod_b, small[4], cond_own, pre_own.reshape(-1, D), dp_count
        )
    else:
        summed = plane_grads(x_turned, ya, yf)
        vectors = vector_grads(grad_mod, mod_b, small[4], cond, pre)
    own_wf, own_wa = jnp.concatenate([summed[0], summed[1]], 1), summed[2]

    grad_mod_all = lax.all_gather(grad_mod, BOTH, axis=0).reshape(-1, 8, images, D)
    grad_mod_all = grad_mod_all.transpose(0, 2, 1, 3).reshape(count_all, 8 * D)
    grad_mod_w = matmul_tn(own_scaled, grad_mod_all)
    grad_mod_bias = jnp.sum(grad_mod_all.astype(F32), 0).reshape(8, D)
    grad_cvec = vectors[:, :group_images].reshape(count_all, D)
    grad_pre = vectors[:, group_images:].reshape(count_all, D)
    token_rows = jnp.concatenate([grad_patch[: PATCH_IN + 1], grad_head], 0)
    token_rows = jnp.concatenate([lax.psum(token_rows, BOTH), grad_mod_bias], 0)
    blank = -(-own_rows // 8) * 8
    start = jnp.clip(mp_index * own_rows - ROW_PATCH + blank, 0, blank + 64)
    spaced = lax.dynamic_update_slice(jnp.zeros((2 * blank + 64, D), F32), token_rows, (blank, 0))
    tail_own = lax.dynamic_slice_in_dim(spaced, start, own_rows, 0)
    grad_table = matmul_tn(left_cond, grad_cvec) + matmul_tn(left_pre, grad_pre) + tail_own

    grad_qkv = jnp.stack([own_wa[:, j * width_a : (j + 1) * width_a] for j in range(3)])
    grad_out_w = own_wa[:, 3 * width_a :].T
    grad_ffn_in = jnp.stack([own_wf[:, j * width_f : (j + 1) * width_f] for j in range(2)])
    grad_ffn_out = own_wf[:, 2 * width_f :].T
    sharded_sq = jnp.sum(own_wa * own_wa) + jnp.sum(own_wf * own_wf)
    copied_sq = (
        jnp.sum(grad_mod_w * grad_mod_w) / mp_count + jnp.sum(grad_table * grad_table) / dp_count
    )
    scalars = jnp.concatenate(
        [jnp.full((1, 128), sharded_sq + copied_sq), jnp.full((1, 128), loss_part), jnp.zeros((6, 128), F32)], 0
    )
    scalars = sum_pallas(scalars, dp_count, mp_count) if regular else lax.psum(scalars, BOTH)
    square_sum, loss_sum = scalars[0, 0], scalars[1, 0]
    norm = jnp.sqrt(square_sum)
    total_tokens = tokens * mp_count * dp_count
    clip = jnp.minimum(1.0, CLIP_SCALE / math.sqrt(total_tokens) / (norm + 1e-06))
    count = step_count[0].astype(F32)
    results = [(loss_sum / weight_sum).reshape(1), norm.reshape(1)]
    for weight, first, second, grad in (
        (qkv_w, qkv_m, qkv_v, grad_qkv),
        (out_w, out_m, out_v, grad_out_w),
        (ffn_in_w, ffn_in_m, ffn_in_v, grad_ffn_in),
        (ffn_out_w, ffn_out_m, ffn_out_v, grad_ffn_out),
        (mod_w, mod_m, mod_v, grad_mod_w),
        (table_w, table_m, table_v, grad_table),
    ):
        results.extend(adam(weight, first, second, grad * clip, count))
    return tuple(results)


def solution(mesh):
    tok, grp = P(None, BOTH), P("dp")
    cols, rows = P(None, "dp", "mp"), P("mp", "dp")
    weights = (cols,) * 3 + (rows,) * 3 + (cols,) * 3 + (rows,) * 3
    weights += (P("dp", None),) * 3 + (P("mp", None),) * 3
    in_specs = (tok, tok, grp, P(None, "dp"), grp, grp, grp, P()) + weights
    return jax.shard_map(
        per_device, mesh=mesh, in_specs=in_specs, out_specs=(P(), P()) + weights, check_vma=False
    )
```

```python
import functools
import math

import jax
import jax.numpy as jnp
from jax import lax
from jax.experimental import pallas as pl
from jax.experimental.pallas import tpu as pltpu
from jax.sharding import PartitionSpec as P

D = 1152
HD = 72
PATCH_IN = 16
OUT = 32
FREQ = 256
NCLS = 1001
PAIR = 320

ROW_TIME_IN = NCLS
ROW_TIME_BIAS = ROW_TIME_IN + FREQ
ROW_TIME_OUT = ROW_TIME_BIAS + 1
ROW_OUT_BIAS = ROW_TIME_OUT + D
ROW_PATCH = ROW_OUT_BIAS + 1
ROW_PATCH_BIAS = ROW_PATCH + PATCH_IN
ROW_HEAD = ROW_PATCH_BIAS + 1
ROW_MOD_BIAS = ROW_HEAD + OUT
ROWS = ROW_MOD_BIAS + 8
TAIL = ROWS - ROW_PATCH

EPS_NORM = 1e-06
BETA_ONE = 0.9
BETA_TWO = 0.95
ADAM_EPS = 1e-08
LEARN_RATE = 0.03
WEIGHT_DECAY = 0.1
CLIP_SCALE = 0.5
LOW = jnp.bfloat16
F32 = jnp.float32
BOTH = ("dp", "mp")
MESH = pl.DeviceIdType.MESH
STEP = 1152
HOOKS = (0, 1, 2, 3)
LINE_FIRST = (True, True, False)
BEHIND = (0, 4, 5)
SENDS = 20
DEPTH = 4


def matmul(left, right):
    return jnp.dot(left, right, preferred_element_type=F32)


def matmul_tn(left, right):
    return lax.dot_general(left, right, (((0,), (0,)), ((), ())), preferred_element_type=F32)


def matmul_nt(left, right):
    return lax.dot_general(left, right, (((1,), (1,)), ((), ())), preferred_element_type=F32)


def layer_norm(values):
    centred = values - jnp.mean(values, -1, keepdims=True)
    inv_std = lax.rsqrt(jnp.mean(centred * centred, -1, keepdims=True) + EPS_NORM)
    return (centred * inv_std, inv_std)


def norm_back(grad, normed, inv_std, scale_rows):
    inner = grad * (1.0 + scale_rows)
    return inv_std * (
        inner
        - jnp.mean(inner, -1, keepdims=True)
        - normed * jnp.mean(inner * normed, -1, keepdims=True)
    )


def silu_slope(values):
    sigma = jax.nn.sigmoid(values)
    return sigma * (1.0 + values * (1.0 - sigma))


def adam(weight, first, second, grad, count):
    first = BETA_ONE * first + (1.0 - BETA_ONE) * grad
    second = BETA_TWO * second + (1.0 - BETA_TWO) * grad * grad
    m_hat = first / (1.0 - BETA_ONE**count)
    v_hat = second / (1.0 - BETA_TWO**count)
    weight = weight - LEARN_RATE * (m_hat / (jnp.sqrt(v_hat) + ADAM_EPS) + WEIGHT_DECAY * weight)
    return (weight, first, second)


def rotary_tables(positions):
    quarter = HD // 4
    freqs = jnp.exp(-math.log(10000.0) * jnp.arange(quarter, dtype=F32) / quarter)
    angle = positions.astype(F32)[:, :, None] * freqs[None, None, :]
    cosine, sine = jnp.cos(angle), jnp.sin(angle)
    cos_row = jnp.concatenate([cosine[0], cosine[0], cosine[1], cosine[1]], 1)
    sin_row = jnp.concatenate([-sine[0], sine[0], -sine[1], sine[1]], 1)
    return cos_row, sin_row


def coordinates():
    dp, mp = lax.axis_index("dp"), lax.axis_index("mp")
    z, x = dp // 2, dp % 2
    y, c = mp // 2, mp % 2
    first = (x + (1 - c) * (1 - 2 * x), y + c * (1 - 2 * y))
    second = (x + c * (1 - 2 * x), y + (1 - c) * (1 - 2 * y))
    return z, x, y, c, first, second


def greet(z, x, y, c, first, second, depth):
    barrier = pltpu.get_barrier_semaphore()

    def signal(dp, mp):
        pl.semaphore_signal(barrier, inc=1, device_id=(dp, mp), device_id_type=MESH)

    signal(z * 2 + first[0], first[1] * 2 + c)
    signal(z * 2 + second[0], second[1] * 2 + c)
    signal(z * 2 + x, y * 2 + 1 - c)
    pl.when(z > 0)(lambda: signal((z - 1) * 2 + x, y * 2 + c))
    pl.when(z < depth - 1)(lambda: signal((z + 1) * 2 + x, y * 2 + c))
    peers = 3 + jnp.minimum(z, 1) + jnp.minimum(depth - 1 - z, 1)
    pl.semaphore_wait(barrier, peers)


def peers_greet(dp_count, mp_count):
    dp, mp = lax.axis_index("dp"), lax.axis_index("mp")
    barrier = pltpu.get_barrier_semaphore()
    for hop in range(1, dp_count):
        pl.semaphore_signal(
            barrier, inc=1, device_id=(lax.rem(dp + hop, dp_count), mp), device_id_type=MESH
        )
    for hop in range(1, mp_count):
        pl.semaphore_signal(
            barrier, inc=1, device_id=(dp, lax.rem(mp + hop, mp_count)), device_id_type=MESH
        )
    pl.semaphore_wait(barrier, dp_count + mp_count - 2)


class Round:
    def __init__(self, axis, count, source, target, send, recv, base):
        self.me = lax.axis_index(axis)
        self.axis, self.count, self.source, self.target = axis, count, source, target
        self.send, self.recv, self.base = send, recv, base

    def moves(self):
        for hop in range(1, self.count):
            peer = lax.rem(self.me + hop, self.count)
            other = {"dp": (peer, lax.axis_index("mp")), "mp": (lax.axis_index("dp"), peer)}[self.axis]
            yield pltpu.make_async_remote_copy(
                src_ref=self.source(peer), dst_ref=self.target.at[self.me],
                send_sem=self.send.at[self.base + hop], recv_sem=self.recv.at[self.base + hop],
                device_id=other, device_id_type=MESH,
            )

    def push(self):
        for move in self.moves():
            move.start()

    def wait(self):
        for hop in range(1, self.count):
            slot = self.target.at[lax.rem(self.me + self.count - hop, self.count)]
            pltpu.make_async_copy(slot, slot, self.recv.at[self.base + hop]).wait()

    def finish(self):
        for move in self.moves():
            move.wait_send()


def gather_kernel(
    depth, mp_count, wa_ref, wf_ref, info_ref, emb_ref, t1_ref, b1_ref, t2_ref, part_ref, tail_ref, mcol_ref,
    patch_ref, cos_ref, sin_ref, col_ref, row_ref,
    wa_all, wf_all, mod_ref, tails_ref, pre_ref, cond_ref, scaled_ref, infos_ref, hid_ref,
    x0_ref, x1_ref, proj_ref, m_ref, at_ref, mt_ref, qkv_ref, att_ref,
    info_buf, pre_sum, cond_sum, tail_buf, scaled_buf, hid_buf, mod_part, mod_sum, mod_buf, a_ref, wa_buf,
    recv, send, local, little_recv, little_send, wa_sem,
):
    dp_count = 2 * depth
    z, x, y, c, first, second = coordinates()
    dp, mp = lax.axis_index("dp"), lax.axis_index("mp")
    rows = wa_ref.shape[0]
    images = emb_ref.shape[0]
    peers_greet(dp_count, mp_count)

    bases = iter(range(0, 64 * dp_count, dp_count))
    little = lambda axis, count, source, target: Round(
        axis, count, source, target, little_send, little_recv, next(bases)
    )
    own = lambda buf, me: lambda peer: buf.at[me]
    info = little("dp", dp_count, own(info_buf, dp), info_buf)
    pre_r = little("mp", mp_count, own(pre_sum, mp), pre_sum)
    tail_r = little("mp", mp_count, own(tail_buf, mp), tail_buf)
    cond_r = little("mp", mp_count, own(cond_sum, mp), cond_sum)
    scaled_a = little("dp", dp_count, own(scaled_buf, dp), scaled_buf)
    hid_a = little("dp", dp_count, own(hid_buf, dp), hid_buf)
    mod_r = little("dp", dp_count, lambda peer: mod_part.at[peer], mod_sum)
    mod_a = little("mp", mp_count, own(mod_buf, mp), mod_buf)
    rounds = (info, pre_r, tail_r, cond_r, scaled_a, hid_a, mod_r, mod_a)
    total = lambda buf, count: functools.reduce(lambda a, b: a + b, [buf[i] for i in range(count)])

    def begin():
        info_buf[dp] = info_ref[...]
        info.push()
        pre_sum[mp] = dot(emb_ref[...], t1_ref[...]) + b1_ref[...]
        pre_r.push()
        tail_buf[mp] = tail_ref[...]
        tail_r.push()

    def hidden():
        pre_r.wait()
        pre = total(pre_sum, mp_count)
        pre_ref[...] = pre
        act = (pre * lax.logistic(pre)).astype(LOW)
        cond_sum[mp] = dot(act, t2_ref[...]) + part_ref[...]
        cond_r.push()
        hid_buf[dp] = act

    def condition():
        cond_r.wait()
        cond = total(cond_sum, mp_count)
        cond_ref[...] = cond
        scaled_buf[dp] = (cond * lax.logistic(cond)).astype(LOW)
        scaled_a.push()

    def modulate():
        scaled_a.wait()
        scaled = scaled_buf[...].reshape(dp_count * images, D)
        row = lax.broadcasted_iota(jnp.int32, (D, rows), 0)
        col = lax.broadcasted_iota(jnp.int32, (D, rows), 1)
        pick = (row == col + dp * rows).astype(F32).astype(LOW)
        mine = dot(scaled, pick).astype(LOW)
        mod_part[...] = dot(mine, mcol_ref[...]).reshape(mod_part.shape)
        mod_sum[dp] = mod_part[dp]
        mod_r.push()

    def collect():
        mod_r.wait()
        mod_buf[mp] = total(mod_sum, dp_count)
        mod_a.push()
        hid_a.push()

    hooks = (hidden, condition, modulate, collect)

    corner = (first[0] + second[0] - x, first[1] + second[1] - y)
    spots = {"here": (x, y), "first": first, "second": second, "corner": corner}
    ids = {"here": 0, "first": 1, "second": 2, "corner": 3}
    swapped = {"here": 0, "first": 2, "second": 1, "corner": 3}
    groups = [(wa_ref, wa_all, 0, LINE_FIRST[0])]
    groups += [(wf_ref, wf_all, i * STEP, LINE_FIRST[1 + i]) for i in range(wf_ref.shape[1] // STEP)]
    count = len(groups)

    def slot(g, zz, spot, core):
        _, ref, column, _ = groups[g]
        return ref.at[spot[1] * 2 + core, pl.ds((zz * 2 + spot[0]) * rows, rows), pl.ds(column, STEP)]

    def mine(g):
        return groups[g][0].at[:, pl.ds(groups[g][2], STEP)]

    def arrive(g, zz, kind, cond=None, plane=0):
        dst = slot(g, zz, spots[kind], c if plane == 0 else 1 - c)
        sem = recv.at[g, plane, ids[kind] if plane == 0 else swapped[kind], zz]
        wait = pltpu.make_async_copy(dst, dst, sem)
        if cond is None:
            wait.wait()
        else:
            pl.when(cond)(wait.wait)

    def sides(k):
        below, above = jnp.maximum(z - k, 0), jnp.minimum(z + k, depth - 1)
        return ((below, z >= k, "up", z < depth - 1), (above, z < depth - k, "down", z > 0))[: 1 if k == 0 else 2]

    def stage(g, k, live=True):
        line_first = groups[g][3]
        numbers = iter(range((g * (depth + 2) + k) * SENDS, (g * (depth + 2) + k + 1) * SENDS))

        def copy(zz, kind, route, cond=None, own=False):
            plane, sem_kind = 0, kind
            if route == "up":
                target = ((z + 1) * 2 + x, mp)
            elif route == "down":
                target = ((z - 1) * 2 + x, mp)
            elif route == "first":
                target, sem_kind = (z * 2 + first[0], first[1] * 2 + c), "first"
            elif route == "second":
                target = (z * 2 + second[0], second[1] * 2 + c)
                sem_kind = "second" if kind == "here" else "corner"
            else:
                target, plane = (dp, y * 2 + 1 - c), 1
            made = pltpu.make_async_remote_copy(
                src_ref=mine(g) if own else slot(g, zz, spots[kind], c), dst_ref=slot(g, zz, spots[kind], c),
                send_sem=send.at[next(numbers)], recv_sem=recv.at[g, plane, ids[sem_kind], zz],
                device_id=target, device_id_type=MESH,
            )
            act = made.start if live else made.wait_send
            if cond is None:
                act()
            else:
                pl.when(cond)(act)

        def take(zz, kind, cond=None):
            if live:
                arrive(g, zz, kind, cond)

        if k == 0:
            if live:
                pltpu.make_async_copy(mine(g), slot(g, z, spots["here"], c), local.at[g]).start()
            copy(z, "here", "first", None, True)
            copy(z, "here", "up", z < depth - 1, True)
            copy(z, "here", "down", z > 0, True)
            copy(z, "here", "second", None, True)
            copy(z, "here", "core", None, True)
        if k == 1 and not line_first:
            take(z, "first")
            copy(z, "first", "up", z < depth - 1)
            copy(z, "first", "down", z > 0)
            copy(z, "first", "second")
            copy(z, "first", "core")
        if 0 < k < depth:
            for zz, cond, route, more in sides(k):
                take(zz, "here", cond)
                copy(zz, "here", route, cond & more)
                if line_first:
                    copy(zz, "here", "first", cond)
                copy(zz, "here", "second", cond)
                copy(zz, "here", "core", cond)
        if 0 <= k - 1 < depth and (line_first or k > 1):
            for zz, cond, route, more in sides(k - 1):
                take(zz, "first", cond)
                if not line_first:
                    copy(zz, "first", route, cond & more)
                copy(zz, "first", "second", cond)
                copy(zz, "first", "core", cond)
        if 0 <= k - 2 < depth:
            for zz, cond, _, _ in sides(k - 2):
                for kind in ("second", "corner"):
                    take(zz, kind, cond)
                    copy(zz, kind, "core", cond)

    def settle(g):
        for zz in range(depth):
            for kind in ("here", "first", "second", "corner"):
                arrive(g, zz, kind, None, 1)
        pltpu.make_async_copy(mine(g), slot(g, z, spots["here"], c), local.at[g]).wait()

    begin()
    steps = [
        [(g, moment - BEHIND[g]) for g in range(count) if 0 <= moment - BEHIND[g] < depth + 2]
        for moment in range(depth + 2 + max(BEHIND))
    ]
    for moment in range(depth + 2):
        for g, k in steps[moment]:
            stage(g, k)
        for number, hook in enumerate(hooks):
            if HOOKS[number] == moment:
                hook()
    settle(0)
    load = lambda m: pltpu.make_async_copy(wa_all.at[m], wa_buf.at[m % 2], wa_sem.at[m % 2])
    load(0).start()
    mod_a.wait()
    tail_r.wait()
    tails_ref[...] = functools.reduce(lambda a, b: a + b, [tail_buf[i].astype(F32) for i in range(mp_count)])
    own_images = images // mp_count
    width = mcol_ref.shape[1]
    for i in range(mp_count):
        rows_of = lambda m: mod_buf[i, m * own_images : (m + 1) * own_images, :]
        picked = functools.reduce(lambda a, m: jnp.where(mp == m, rows_of(m), a), range(1, mp_count), rows_of(0))
        mod_ref[:, i * width : (i + 1) * width] = picked
    for j in range(8):
        bias = tails_ref[ROW_MOD_BIAS - ROW_PATCH + j : ROW_MOD_BIAS - ROW_PATCH + j + 1, :]
        mod_ref[:, j * D : (j + 1) * D] += bias
    attn_begin(
        patch_ref, tails_ref[:PATCH_IN, :].astype(LOW), tails_ref[PATCH_IN : PATCH_IN + 1, :],
        mod_ref, col_ref, x0_ref, a_ref, at_ref,
    )
    proj_ref[...] = jnp.zeros(proj_ref.shape, F32)

    later = [pair for moment in steps[depth + 2 :] for pair in moment]

    def heads(m, _):
        pl.when(m + 1 < mp_count)(lambda: load(m + 1).start())
        load(m).wait()
        proj_ref[...] += attn_block(
            wa_buf.at[m % 2], cos_ref, sin_ref, col_ref, row_ref, a_ref, qkv_ref.at[m], att_ref.at[m]
        )
        for i in range(mp_count):
            part = later[i * len(later) // mp_count : (i + 1) * len(later) // mp_count]

            @pl.when(m == i)
            def _(part=part):
                for g, k in part:
                    stage(g, k)

        return 0

    lax.fori_loop(0, mp_count, heads, 0)
    hid_a.wait()
    info.wait()
    scaled_ref[...] = scaled_buf[...]
    infos_ref[...] = info_buf[...]
    hid_ref[...] = hid_buf[...]
    attn_end(mod_ref, col_ref, x0_ref, proj_ref, x1_ref, m_ref, mt_ref)
    for g in range(1, count):
        settle(g)
    for g in range(count):
        for k in range(depth + 2):
            stage(g, k, False)
    for one in rounds:
        one.finish()


def gather_pallas(wa, wf, small, patches, tables, dp, mp, collective_id=0):
    depth = dp // 2
    groups = 1 + wf.shape[1] // STEP
    images, width = small[1].shape[0], small[7].shape[1]
    tail = small[6].shape[0]
    tokens, heads = patches.shape[1], wa.shape[1] // 4
    full, turned = (tokens, D), (D, tokens)
    shapes = [
        ((images // mp, mp * width), F32), ((tail, D), F32), ((images, D), F32), ((images, D), F32),
        ((dp, images, D), LOW), ((dp, 8, 128), F32), ((dp, images, D), LOW),
        (full, F32), (full, F32), (full, F32), (full, LOW), (turned, LOW), (turned, LOW),
        ((mp, tokens, 3 * heads), LOW), ((mp, tokens, heads), LOW),
    ]
    hbm, vmem = pl.BlockSpec(memory_space=pl.ANY), pl.BlockSpec(memory_space=pltpu.VMEM)
    return pl.pallas_call(
        functools.partial(gather_kernel, depth, mp),
        out_shape=[jax.ShapeDtypeStruct((mp, dp * s.shape[0], s.shape[1]), s.dtype) for s in (wa, wf)]
        + [jax.ShapeDtypeStruct(*s) for s in shapes],
        in_specs=[hbm] * 2 + [vmem] * 13,
        out_specs=[hbm] * 2 + [vmem] * len(shapes),
        scratch_shapes=[
            pltpu.VMEM((dp, 8, 128), F32), pltpu.VMEM((mp, images, D), F32), pltpu.VMEM((mp, images, D), F32),
            pltpu.VMEM((mp, tail, D), LOW), pltpu.VMEM((dp, images, D), LOW), pltpu.VMEM((dp, images, D), LOW),
            pltpu.VMEM((dp, images, width), F32), pltpu.VMEM((dp, images, width), F32),
            pltpu.VMEM((mp, images, width), F32),
            pltpu.VMEM(full, LOW), pltpu.VMEM((2, D, wa.shape[1]), LOW),
            pltpu.SemaphoreType.DMA((groups, 2, 4, depth)),
            pltpu.SemaphoreType.DMA((groups * (depth + 2) * SENDS,)),
            pltpu.SemaphoreType.DMA((groups,)),
            pltpu.SemaphoreType.DMA((8 * dp,)),
            pltpu.SemaphoreType.DMA((8 * dp,)),
            pltpu.SemaphoreType.DMA((2,)),
        ],
        compiler_params=pltpu.CompilerParams(
            collective_id=collective_id, has_side_effects=True, vmem_limit_bytes=60 * 1024 * 1024
        ),
        name="gather_weights",
    )(wa, wf, *small, patches, *tables)


TOP = 32766.0
RING = 14
BETWEEN = (0, 12, 20, 28, 36)
ORDER = (
    (0, 0, 0), (0, 0, 2), (0, 0, 1), (0, 2, 0), (0, 0, 3), (1, 0, 0), (0, 2, 2), (2, 0, 3), (1, 0, 1), (0, 2, 1),
    (0, 1, 0), (1, 1, 0), (1, 1, 1), (1, 2, 0), (2, 0, 0), (1, 2, 1), (1, 0, 2), (0, 1, 2), (2, 1, 1), (0, 1, 1),
    (1, 0, 3), (1, 3, 1), (1, 2, 2), (2, 0, 1), (1, 1, 2), (0, 3, 0), (2, 1, 0), (2, 1, 3), (0, 1, 3), (2, 0, 2),
    (0, 3, 1), (0, 3, 2), (2, 2, 0), (1, 2, 3), (2, 2, 1), (1, 3, 0), (2, 1, 2), (2, 2, 2), (1, 3, 2), (0, 2, 3),
    (2, 2, 3), (2, 3, 0), (2, 3, 1), (1, 1, 3), (2, 3, 2), (0, 3, 3), (1, 3, 3), (2, 3, 3),
)


def lookup(values, base, t):
    digits = {4: 15, 64: 5}[base]
    words = [
        sum(v * base**i for i, v in enumerate(values[at : at + digits])) for at in range(0, len(values), digits)
    ]
    word = functools.reduce(lambda a, iw: jnp.where(t // digits == iw[0], iw[1], a), enumerate(words), 0)
    unit = functools.reduce(lambda a, i: jnp.where(t % digits == i, base**i, a), range(digits), 1)
    return word // unit % base


def encode(value):
    peak = jnp.maximum(jnp.max(jnp.abs(value), 0, keepdims=True), 1e-30)
    return jnp.round(value * (TOP / peak)).astype(jnp.int32).astype(jnp.int16), peak * (1.0 / TOP)


def decode(code, unit):
    return code.astype(jnp.int32).astype(F32) * unit


def weight_grad_kernel(
    depth, widths, mp_count, at_ref, pt_ref, mt_ref, ot_ref, ya_ref, yf_ref, gmod_ref, mod_ref, t2_ref, cond_ref, pre_ref,
    out_ref, vec_ref,
    x_all, ya_all, yf_all, work, q_send, u_send, q_recv, u_recv,
    gmod, panel, scaled_send, scaled_recv, joined, own_vec, hid_part, vec_buf,
    moves, swaps, landing, send, recv, panel_sem, little_send, little_recv,
):
    z, x, y, c, first, second = coordinates()
    dp_count = 2 * depth
    peers_greet(dp_count, mp_count)
    rows = out_ref.shape[1]
    x_refs = (at_ref, pt_ref, mt_ref, ot_ref)
    tokens = at_ref.shape[1]
    width_a, width_f = widths
    here = (x, y)
    corner = (first[0] + second[0] - x, first[1] + second[1] - y)
    mate = (z * 2 + x, y * 2 + 1 - c)
    total = len(ORDER)

    own, theirs = pl.ds(0, tokens), pl.ds(tokens, tokens)
    local, remote = [], []

    def trade(mine, give, to, land):
        n = len(local)
        remote.append(pltpu.make_async_remote_copy(
            src_ref=give, dst_ref=land, send_sem=swaps.at[n], recv_sem=landing.at[n],
            device_id=mate, device_id_type=MESH,
        ))
        local.append(pltpu.make_async_copy(mine, to, moves.at[n]))
        remote[-1].start()
        local[-1].start()

    def trade_x(i):
        trade(x_refs[i], x_refs[i], x_all.at[i, :, own], x_all.at[i, :, theirs])

    def trade_y(ref, full, j):
        trade(ref.at[2 * j + c], ref.at[2 * j + 1 - c], full.at[j, own, :], full.at[j, theirs, :])

    trade_x(2)
    trade_y(yf_ref, yf_all, 1 - y)
    trade_x(3)
    trade_x(0)
    trade_x(1)
    trade_y(ya_ref, ya_all, 1 - y)
    trade_y(yf_ref, yf_all, y)
    trade_y(ya_ref, ya_all, y)
    waits, known = [], set()
    for t, (g, kind, _) in enumerate(ORDER):
        need = [{0, 1}, {0, 1, 2}, {3, 4, 5}][g] | (set() if kind == 0 else {7} if g == 2 else {6})
        if need - known:
            waits.append((t, sorted(need - known)))
            known |= need

    def ready(numbers):
        for n in numbers:
            local[n].wait()
            remote[n].wait_recv()

    codes = tuple(16 * g + 4 * kind + j for g, kind, j in ORDER)

    def plan(t):
        code = lookup(codes, 64, t)
        g, kind, j = code // 16, code // 4 % 4, code % 4
        falling = jnp.where(depth - 1 - j <= z, depth - 2 - j, depth - 1 - j)
        rising = jnp.where(j >= z, j + 1, j)
        zz = jnp.where(z * 2 < depth, falling, rising)
        zz = jnp.where(j == depth - 1, z, zz)
        pick = lambda i: jnp.where(
            kind == 0, corner[i], jnp.where(kind == 1, second[i], jnp.where(kind == 2, first[i], here[i]))
        )
        return g, kind, zz, pick(0), pick(1)

    def product(g, zz, xx, yy):
        cut = pl.ds((zz * 2 + xx) * rows, rows)

        @pl.when(g == 0)
        def _():
            work[...] = dot(x_all[2, cut, :], yf_all[yy, :, :STEP])

        @pl.when(g == 1)
        def _():
            middle = 2 * width_f - STEP
            work[:, :middle] = dot(x_all[2, cut, :], yf_all[yy, :, STEP : 2 * width_f])
            work[:, middle:] = dot(x_all[3, cut, :], yf_all[yy, :, 2 * width_f :])

        @pl.when(g == 2)
        def _():
            edge = 3 * width_a
            low, high = edge // 128 * 128, -(-edge // 128) * 128
            left = dot(x_all[0, cut, :], ya_all[yy, :, :high])
            right = dot(x_all[1, cut, :], ya_all[yy, :, low:])
            lane = lax.broadcasted_iota(jnp.int32, (rows, high - low), 1)
            work[:, :low] = left[:, :low]
            work[:, low:high] = jnp.where(lane < edge - low, left[:, low:], right[:, : high - low])
            work[:, high:] = right[:, high - low :]

    def sent(slot):
        return (
            pltpu.make_async_copy(q_send.at[slot], q_send.at[slot], send.at[0, slot]),
            pltpu.make_async_copy(u_send.at[slot], u_send.at[slot], send.at[1, slot]),
        )

    def ship(t, g, dst_slot, target):
        slot = t % RING

        @pl.when(t >= RING)
        def _():
            for move in sent(slot):
                move.wait()

        code, unit = encode(work[...])
        q_send[slot] = code
        u_send[slot] = unit
        for i, (a, b) in enumerate(((q_send, q_recv), (u_send, u_recv))):
            pltpu.make_async_remote_copy(
                src_ref=a.at[slot], dst_ref=b.at[g, dst_slot],
                send_sem=send.at[i, slot], recv_sem=recv.at[i, g, dst_slot],
                device_id=target, device_id_type=MESH,
            ).start()

    def landed(g, slot):
        pltpu.make_async_copy(q_recv.at[g, slot], q_recv.at[g, slot], recv.at[0, g, slot]).wait()
        pltpu.make_async_copy(u_recv.at[g, slot], u_recv.at[g, slot], recv.at[1, g, slot]).wait()
        work[...] += decode(q_recv[g, slot], u_recv[g, slot])

    dp, mp = lax.axis_index("dp"), lax.axis_index("mp")
    bases = iter(range(0, 64 * dp_count, dp_count))
    little = lambda axis, count, source, target: Round(
        axis, count, source, target, little_send, little_recv, next(bases)
    )
    own_slot = lambda buf, me: lambda peer: buf.at[me]
    gmod_a = little("dp", dp_count, own_slot(gmod, dp), gmod)
    scaled_r = little("dp", dp_count, lambda peer: scaled_send.at[peer], scaled_recv)
    vec_m = little("mp", mp_count, own_slot(own_vec, mp), own_vec)
    hid_r = little("mp", mp_count, own_slot(hid_part, mp), hid_part)
    vec_a = little("dp", dp_count, own_slot(vec_buf, dp), vec_buf)
    lines = gmod_ref.shape[0]
    images = lines // 8

    def panels(count, source, use):
        fetch = lambda i: pltpu.make_async_copy(source(i), panel.at[i % 2], panel_sem.at[i % 2])
        fetch(0).start()
        for i in range(count):
            if i + 1 < count:
                fetch(i + 1).start()
            fetch(i).wait()
            use(i, panel.at[i % 2])

    def one_hot(shape, hit):
        row, col = (lax.broadcasted_iota(jnp.int32, shape, i) for i in range(2))
        return hit(row, col).astype(F32).astype(LOW)

    def begin():
        gmod[dp] = gmod_ref[...]
        gmod_a.push()

    def scaled_grad():
        gmod_a.wait()
        every = gmod[...].reshape(dp_count * lines, D)
        scaled_send[...] = jnp.zeros(scaled_send.shape, F32)

        def use(j, piece):
            hit = lambda r, q: (r // 8 == q // lines) & (q % lines == j * images + r % 8) & (r % 8 < images)
            part = dot(one_hot((8 * dp_count, dp_count * lines), hit), every).astype(LOW)
            scaled_send[...] += dot_nt(part, piece[...]).reshape(scaled_send.shape)

        panels(8, lambda j: mod_ref.at[:, pl.ds(j * D, D)], use)
        scaled_recv[dp] = scaled_send[dp]
        scaled_r.push()

    def vector_grad():
        scaled_r.wait()
        for d in range(dp_count):
            joined[:, d * rows : (d + 1) * rows] = scaled_recv[d]
        own_vec[mp] = (joined[...] * silu_slope(cond_ref[mp])).astype(LOW).astype(F32)
        vec_m.push()

    def hidden_grad():
        vec_m.wait()
        vectors = own_vec[...].reshape(8 * mp_count, D).astype(LOW)
        def use(i, piece):
            hid_part[mp, :, i * rows : (i + 1) * rows] = dot_nt(vectors, piece[...])

        panels(D // rows, lambda i: t2_ref.at[pl.ds(i * rows, rows), :], use)
        hid_r.push()

    def first_grad():
        hid_r.wait()
        grad = functools.reduce(lambda a, b: a + b, [hid_part[i] for i in range(mp_count)])
        grad_pre = (grad * silu_slope(pre_ref[...])).astype(LOW)
        vectors = own_vec[...].reshape(8 * mp_count, D).astype(LOW)
        hit = lambda r, q: (r // images == q // 8) & (r % images == q % 8)
        pick = one_hot((images * mp_count, 8 * mp_count), hit)
        count = images * mp_count
        vec_buf[dp, :count, :] = dot(pick, vectors).astype(LOW)
        vec_buf[dp, count:, :] = dot(pick, grad_pre).astype(LOW)
        vec_a.push()

    hooks = tuple(zip(BETWEEN, (begin, scaled_grad, vector_grad, hidden_grad, first_grad), strict=True))

    to_second = (z * 2 + second[0], second[1] * 2 + c)
    to_first = (z * 2 + first[0], first[1] * 2 + c)
    to_up = ((z + 1) * 2 + x, y * 2 + c)
    to_down = ((z - 1) * 2 + x, y * 2 + c)
    kept, passed = 2 * depth, 3 * depth + 1
    after_line = passed + depth + 1

    def step(t, _):
        g, kind, zz, xx, yy = plan(t)
        for at, numbers in waits:
            pl.when(t == at)(functools.partial(ready, numbers))
        for at, hook in hooks:
            pl.when(t == at)(hook)
        product(g, zz, xx, yy)
        line_first = g < 2
        late, mine = kind >= 2, zz == z
        along = late & ((kind == 3) | line_first)
        line = jnp.where(kind == 3, kept, passed)

        @pl.when(kind < 2)
        def _():
            ship(t, g, kind * depth + zz, to_second)

        @pl.when(late)
        def _():
            landed(g, (kind - 2) * depth + zz)

        @pl.when((kind == 3) & (jnp.logical_not(line_first) | mine))
        def _():
            landed(g, jnp.where(line_first, after_line, passed + zz))

        @pl.when(along & (zz >= z) & (z > 0))
        def _():
            landed(g, line + zz)

        @pl.when(along & (zz <= z) & (z < depth - 1))
        def _():
            landed(g, line + jnp.where(mine, depth, zz))

        @pl.when(along & (zz > z))
        def _():
            ship(t, g, line + zz, to_up)

        @pl.when(along & (zz < z))
        def _():
            ship(t, g, line + jnp.where(zz == z - 1, depth, zz), to_down)

        @pl.when((kind == 2) & (jnp.logical_not(line_first) | mine))
        def _():
            ship(t, g, jnp.where(line_first, after_line, passed + zz), to_first)

        @pl.when((kind == 3) & mine)
        def _():
            out_ref[g] = work[...]

        return 0

    lax.fori_loop(0, total, step, 0)

    def drain(slot, _):
        for move in sent(slot):
            move.wait()
        return 0

    lax.fori_loop(0, RING, drain, 0)
    for move in remote:
        move.wait_send()
    vec_a.wait()
    vec_ref[...] = vec_buf[...]
    for one in (gmod_a, scaled_r, vec_m, hid_r, vec_a):
        one.finish()


def weight_grads(turned, ya, yf, grad_mod, mod_rows, second, cond, pre, dp, collective_id=1):
    depth, mp = dp // 2, ya.shape[0]
    tokens = turned[0].shape[1]
    rows = D // dp
    slots = 4 * depth + 3
    images = grad_mod.shape[0] // 8
    hbm, vmem = pl.BlockSpec(memory_space=pl.ANY), pl.BlockSpec(memory_space=pltpu.VMEM)
    vectors = (dp, 2 * images * mp, D)
    return pl.pallas_call(
        functools.partial(weight_grad_kernel, depth, (ya.shape[2] // 4, yf.shape[2] // 3), mp),
        out_shape=[jax.ShapeDtypeStruct((3, rows, STEP), F32), jax.ShapeDtypeStruct(vectors, LOW)],
        in_specs=[hbm] * 6 + [vmem, hbm, hbm, vmem, vmem],
        out_specs=[vmem, vmem],
        scratch_shapes=[
            pltpu.VMEM((4, D, 2 * tokens), LOW),
            pltpu.VMEM((2, 2 * tokens, ya.shape[2]), LOW),
            pltpu.VMEM((2, 2 * tokens, yf.shape[2]), LOW),
            pltpu.VMEM((rows, STEP), F32),
            pltpu.VMEM((RING, rows, STEP), jnp.int16),
            pltpu.VMEM((RING, 1, STEP), F32),
            pltpu.VMEM((3, slots, rows, STEP), jnp.int16),
            pltpu.VMEM((3, slots, 1, STEP), F32),
            pltpu.VMEM((dp, *grad_mod.shape), LOW),
            pltpu.VMEM((2, rows, D), LOW),
            pltpu.VMEM((dp, 8, rows), F32),
            pltpu.VMEM((dp, 8, rows), F32),
            pltpu.VMEM((8, D), F32),
            pltpu.VMEM((mp, 8, D), F32),
            pltpu.VMEM((mp, 8 * mp, D), F32),
            pltpu.VMEM(vectors, LOW),
            pltpu.SemaphoreType.DMA((8,)),
            pltpu.SemaphoreType.DMA((8,)),
            pltpu.SemaphoreType.DMA((8,)),
            pltpu.SemaphoreType.DMA((2, RING)),
            pltpu.SemaphoreType.DMA((2, 3, slots)),
            pltpu.SemaphoreType.DMA((2,)),
            pltpu.SemaphoreType.DMA((5 * dp,)),
            pltpu.SemaphoreType.DMA((5 * dp,)),
        ],
        compiler_params=pltpu.CompilerParams(
            collective_id=collective_id, has_side_effects=True, vmem_limit_bytes=62 * 1024 * 1024
        ),
        name="weight_grads",
    )(*turned, ya, yf, grad_mod, mod_rows, second, cond, pre)


def sum_kernel(mp_count, dp_count, in_ref, out_ref, over_dp, over_mp, send, recv):
    dp, mp = lax.axis_index("dp"), lax.axis_index("mp")
    peers_greet(dp_count, mp_count)
    first = Round("dp", dp_count, lambda peer: over_dp.at[dp], over_dp, send, recv, 0)
    second = Round("mp", mp_count, lambda peer: over_mp.at[mp], over_mp, send, recv, dp_count)
    over_dp[dp] = in_ref[...]
    first.push()
    first.wait()
    over_mp[mp] = functools.reduce(lambda a, b: a + b, [over_dp[i] for i in range(dp_count)])
    second.push()
    second.wait()
    out_ref[...] = functools.reduce(lambda a, b: a + b, [over_mp[i] for i in range(mp_count)])
    first.finish()
    second.finish()


def sum_pallas(values, dp, mp, collective_id=2):
    return pl.pallas_call(
        functools.partial(sum_kernel, mp, dp),
        out_shape=jax.ShapeDtypeStruct(values.shape, F32),
        in_specs=[pl.BlockSpec(memory_space=pltpu.VMEM)],
        out_specs=pl.BlockSpec(memory_space=pltpu.VMEM),
        scratch_shapes=[
            pltpu.VMEM((dp, *values.shape), F32), pltpu.VMEM((mp, *values.shape), F32),
            pltpu.SemaphoreType.DMA((dp + mp,)), pltpu.SemaphoreType.DMA((dp + mp,)),
        ],
        compiler_params=pltpu.CompilerParams(collective_id=collective_id, has_side_effects=True),
        name="sum_scalars",
    )(values)


SLAB = 64
VMEM_LIMIT = 60 * 1024 * 1024


def whole(shape):
    return pl.BlockSpec(shape, lambda m: (0,) * len(shape), pipeline_mode=pl.Buffered(1))


def by_block(*shape):
    return pl.BlockSpec((1, *shape), lambda m: (m, 0, 0))


def dot(left, right):
    return lax.dot_general(left, right, (((1,), (0,)), ((), ())), preferred_element_type=F32)


def dot_nt(left, right):
    return lax.dot_general(left, right, (((1,), (1,)), ((), ())), preferred_element_type=F32)


def dot_tn(left, right):
    return lax.dot_general(left, right, (((0,), (0,)), ((), ())), preferred_element_type=F32)


def slabs(tokens, body, sums=0):
    totals = []
    for block in range(tokens // PAIR):

        def step(i, carry, block=block):
            rows = pl.ds(pl.multiple_of(block * PAIR + i * SLAB, SLAB), SLAB)
            lead, values = body(block, rows)
            head, rest = carry
            head = tuple(h + jnp.sum(jnp.where(lead, v, 0.0), 0, keepdims=True) for h, v in zip(head, values))
            rest = tuple(r + jnp.sum(jnp.where(lead, 0.0, v), 0, keepdims=True) for r, v in zip(rest, values))
            return head, rest

        zero = tuple(jnp.zeros((1, D), F32) for _ in range(sums))
        totals.extend(lax.fori_loop(0, PAIR // SLAB, step, (zero, zero)))
    return totals


def spread(mod_ref, j, block, lead):
    row = lambda i: mod_ref[2 * block + i : 2 * block + i + 1, j * D : (j + 1) * D]
    return jnp.where(lead, row(0), row(1))


def turn(values, cos_row, sin_row, direction):
    quarter = HD // 4
    width = values.shape[1]
    lane = lax.broadcasted_iota(jnp.int32, values.shape, 1)
    ahead = pltpu.roll(values, width - quarter, 1)
    behind = pltpu.roll(values, quarter, 1)
    partner = jnp.where(lane % (2 * quarter) < quarter, ahead, behind)
    return values * cos_row + partner * (sin_row * direction)


def same_image(even_col, even_row, block):
    rows = slice(block * PAIR, (block + 1) * PAIR)
    return even_col[rows, :1] == even_row[block, :1, :]


def softmax(query, key, same):
    scores = jnp.where(same, dot_nt(query, key) * HD ** (-0.5), -1e30)
    expo = jnp.exp(scores - jnp.max(scores, -1, keepdims=True))
    return expo * (1.0 / jnp.sum(expo, -1, keepdims=True))


def attn_begin(patch_ref, patch_rows, patch_bias, mod_ref, col_ref, x0_ref, a_ref, at_ref):
    x0_ref[...] = dot_tn(patch_ref[...], patch_rows) + patch_bias

    def body(block, rows):
        lead = col_ref[rows, :1] != 0
        normed, _ = layer_norm(x0_ref[rows, :])
        shift, scale = spread(mod_ref, 0, block, lead), spread(mod_ref, 1, block, lead)
        a_ref[rows, :] = (normed * (1.0 + scale) + shift).astype(LOW)
        return lead, ()

    slabs(a_ref.shape[0], body)
    at_ref[...] = a_ref[...].T


def attn_block(w_ref, cos_ref, sin_ref, col_ref, row_ref, a_ref, qkv_ref, att_ref):
    tokens, width = att_ref.shape
    made = dot(a_ref[...], w_ref[:, : 3 * width])
    qkv_ref[:, : 2 * width] = turn(made[:, : 2 * width], cos_ref[...], sin_ref[...], 1.0).astype(LOW)
    qkv_ref[:, 2 * width :] = made[:, 2 * width :].astype(LOW)
    for block in range(tokens // PAIR):
        same = same_image(col_ref, row_ref, block)
        rows = slice(block * PAIR, (block + 1) * PAIR)
        for head in range(width // HD):
            take = lambda i: qkv_ref[rows, i * width + head * HD : i * width + (head + 1) * HD]
            probs = softmax(take(0), take(1), same).astype(LOW)
            att_ref[rows, head * HD : (head + 1) * HD] = dot(probs, take(2)).astype(LOW)
    return dot_nt(att_ref[...], w_ref[:, 3 * width :])


def attn_end(mod_ref, col_ref, x0_ref, proj_ref, x1_ref, m_ref, mt_ref):
    def body(block, rows):
        lead = col_ref[rows, :1] != 0
        x_one = x0_ref[rows, :] + spread(mod_ref, 2, block, lead) * proj_ref[rows, :]
        x1_ref[rows, :] = x_one
        normed, _ = layer_norm(x_one)
        shift, scale = spread(mod_ref, 3, block, lead), spread(mod_ref, 4, block, lead)
        m_ref[rows, :] = (normed * (1.0 + scale) + shift).astype(LOW)
        return lead, ()

    slabs(m_ref.shape[0], body)
    mt_ref[...] = m_ref[...].T


def attn_forward_kernel(
    patch_ref, prow_ref, pbias_ref, mod_ref, w_ref, cos_ref, sin_ref, col_ref, row_ref,
    x0_ref, x1_ref, proj_ref, m_ref, at_ref, mt_ref, qkv_ref, att_ref, a_ref,
):
    step, last = pl.program_id(0), pl.num_programs(0) - 1

    @pl.when(step == 0)
    def _():
        attn_begin(patch_ref, prow_ref[...], pbias_ref[...], mod_ref, col_ref, x0_ref, a_ref, at_ref)
        proj_ref[...] = jnp.zeros(proj_ref.shape, F32)

    proj_ref[...] += attn_block(
        w_ref.at[0], cos_ref, sin_ref, col_ref, row_ref, a_ref, qkv_ref.at[0], att_ref.at[0]
    )

    @pl.when(step == last)
    def _():
        attn_end(mod_ref, col_ref, x0_ref, proj_ref, x1_ref, m_ref, mt_ref)


def attn_forward(patches, patch_rows, patch_bias, modulation, wa_all, tables):
    blocks, _, width = wa_all.shape
    width //= 4
    tokens = patches.shape[1]
    full, turned = (tokens, D), (D, tokens)
    ins = (patches, patch_rows, patch_bias, modulation)
    return pl.pallas_call(
        attn_forward_kernel,
        grid=(blocks,),
        out_shape=[jax.ShapeDtypeStruct(full, F32)] * 3
        + [jax.ShapeDtypeStruct(full, LOW)]
        + [jax.ShapeDtypeStruct(turned, LOW)] * 2
        + [
            jax.ShapeDtypeStruct((blocks, tokens, 3 * width), LOW),
            jax.ShapeDtypeStruct((blocks, tokens, width), LOW),
        ],
        in_specs=[whole(a.shape) for a in ins] + [by_block(D, 4 * width)] + [whole(a.shape) for a in tables],
        out_specs=[whole(full)] * 4
        + [whole(turned)] * 2
        + [by_block(tokens, 3 * width), by_block(tokens, width)],
        scratch_shapes=[pltpu.VMEM(full, LOW)],
        compiler_params=pltpu.CompilerParams(vmem_limit_bytes=VMEM_LIMIT),
        name="attn_forward",
    )(*ins, wa_all, *tables)


PARTS = 1


def units(part, width):
    size = width // PARTS
    return slice(part * size, (part + 1) * size), slice(width + part * size, width + (part + 1) * size)


def ffn_kernel(
    m_ref, x1_ref, proj_ref, mod_ref, head_ref, target_ref, weight_ref, col_ref, w_ref,
    yf_ref, gx1_ref, gp_ref, gpt_ref, gmot_ref, ghead_ref, loss_ref, sums_ref,
    gu_ref, out_ref, back_ref, low_ref,
):
    width = gu_ref.shape[2] // 2
    tokens = m_ref.shape[0]
    step, count = pl.program_id(0), pl.num_programs(0) // 2

    @pl.when(step == 0)
    def _():
        out_ref[...] = jnp.zeros(out_ref.shape, F32)

    @pl.when(step == count)
    def _():
        back_ref[...] = jnp.zeros(back_ref.shape, F32)

    @pl.when(step < count)
    def _():
        for part in range(PARTS):
            own, other = units(part, width)
            gate, up_val = dot(m_ref[...], w_ref[0, :, own]), dot(m_ref[...], w_ref[0, :, other])
            gu_ref[step, :, own] = gate
            gu_ref[step, :, other] = up_val
            hidden = (gate * lax.logistic(gate) * up_val).astype(LOW)
            last = slice(other.start + width, other.stop + width)
            out_ref[...] += dot_nt(hidden, w_ref[0, :, last])

    @pl.when(step == count - 1)
    def _():
        def final_norm(block, rows):
            lead = col_ref[rows, :1] != 0
            x_two = x1_ref[rows, :] + spread(mod_ref, 5, block, lead) * out_ref[rows, :]
            return lead, spread(mod_ref, 7, block, lead), *layer_norm(x_two)

        def before(block, rows):
            lead, scale, normed, _ = final_norm(block, rows)
            low_ref[rows, :] = (normed * (1.0 + scale) + spread(mod_ref, 6, block, lead)).astype(LOW)
            return lead, ()

        slabs(tokens, before)
        diff = dot_nt(head_ref[...], low_ref[...]) - target_ref[...]
        loss = jnp.sum(weight_ref[:1, :] * jnp.mean(diff * diff, 0, keepdims=True), 1, keepdims=True)
        loss_ref[...] = jnp.broadcast_to(loss, loss_ref.shape)
        grad_pred = (2.0 / OUT * diff * weight_ref[1:2, :]).astype(LOW)
        ghead_ref[...] = dot(grad_pred, low_ref[...])
        back_ref[...] = dot_tn(grad_pred, head_ref[...])

        def after(block, rows):
            lead, scale, normed, inv_std = final_norm(block, rows)
            grad_f = back_ref[rows, :]
            grad_x2 = norm_back(grad_f, normed, inv_std, scale)
            gx1_ref[rows, :] = grad_x2
            low_ref[rows, :] = (spread(mod_ref, 5, block, lead) * grad_x2).astype(LOW)
            return lead, (grad_f, grad_f * normed, grad_x2 * out_ref[rows, :])

        for image, rows in enumerate(slabs(tokens, after, 3)):
            for k in range(3):
                sums_ref[k, image : image + 1, :] = rows[k]
        gmot_ref[...] = low_ref[...].T

    @pl.when(step >= count)
    def _():
        for part in range(PARTS):
            own, other = units(part, width)
            last = slice(other.start + width, other.stop + width)
            grad_hid = dot(low_ref[...], w_ref[0, :, last])
            back = 2 * count - 1 - step
            gate, up_val = gu_ref[back, :, own], gu_ref[back, :, other]
            sigma = lax.logistic(gate)
            act = gate * sigma
            slope = sigma * (1.0 + gate * (1.0 - sigma))
            yf_ref[0, :, own] = (grad_hid * up_val * slope).astype(LOW)
            yf_ref[0, :, other] = (grad_hid * act).astype(LOW)
            yf_ref[0, :, last] = (act * up_val).astype(LOW)
        back_ref[...] += dot_nt(yf_ref[0, :, : 2 * width], w_ref[0, :, : 2 * width])

    @pl.when(step == 2 * count - 1)
    def _():
        def body(block, rows):
            lead = col_ref[rows, :1] != 0
            grad_m = back_ref[rows, :]
            normed, inv_std = layer_norm(x1_ref[rows, :])
            grad_x1 = gx1_ref[rows, :] + norm_back(grad_m, normed, inv_std, spread(mod_ref, 4, block, lead))
            gx1_ref[rows, :] = grad_x1
            gp_ref[rows, :] = (spread(mod_ref, 2, block, lead) * grad_x1).astype(LOW)
            return lead, (grad_m, grad_m * normed, grad_x1 * proj_ref[rows, :])

        for image, rows in enumerate(slabs(tokens, body, 3)):
            for k in range(3):
                sums_ref[3 + k, image : image + 1, :] = rows[k]
        gpt_ref[...] = gp_ref[...].T


def ffn(m_in, x_one, proj, modulation, head_rows, target, weights, even_col, wf_all):
    blocks, _, width = wf_all.shape
    width //= 3
    tokens = m_in.shape[0]
    full, turned = (tokens, D), (D, tokens)
    ins = (m_in, x_one, proj, modulation, head_rows, target, weights, even_col)
    there_and_back = lambda i: (jnp.where(i < blocks, i, 2 * blocks - 1 - i), 0, 0)
    back = lambda i: (jnp.where(i < blocks, blocks - 1, 2 * blocks - 1 - i), 0, 0)
    outs = [
        (full, F32), (full, LOW), (turned, LOW), (turned, LOW),
        ((OUT, D), F32), ((8, 128), F32), ((6, modulation.shape[0], D), F32),
    ]
    return pl.pallas_call(
        ffn_kernel,
        grid=(2 * blocks,),
        out_shape=[jax.ShapeDtypeStruct((blocks, tokens, 3 * width), LOW)]
        + [jax.ShapeDtypeStruct(*o) for o in outs],
        in_specs=[whole(a.shape) for a in ins] + [pl.BlockSpec((1, D, 3 * width), there_and_back)],
        out_specs=[pl.BlockSpec((1, tokens, 3 * width), back)] + [whole(o[0]) for o in outs],
        scratch_shapes=[
            pltpu.VMEM((blocks, tokens, 2 * width), F32),
            pltpu.VMEM(full, F32), pltpu.VMEM(full, F32), pltpu.VMEM(full, LOW),
        ],
        compiler_params=pltpu.CompilerParams(vmem_limit_bytes=VMEM_LIMIT),
        name="feed_forward",
    )(*ins, wf_all)


def attn_backward_kernel(
    grad_ref, gx1_ref, x0_ref, patch_ref, mod_ref, w_ref, qkv_ref, att_ref, cos_ref, sin_ref, col_ref, row_ref,
    out_ref, rows_ref, sums_ref, tmp_ref, back_att, back_ref, low_ref,
):
    width = att_ref.shape[2]
    tokens = grad_ref.shape[0]
    scale = HD ** (-0.5)
    step, last = pl.program_id(0), pl.num_programs(0) - 1
    back_att[...] = dot(grad_ref[...], w_ref[0, :, 3 * width :]).astype(LOW)
    for block in range(tokens // PAIR):
        same = same_image(col_ref, row_ref, block)
        rows = slice(block * PAIR, (block + 1) * PAIR)
        for head in range(width // HD):
            lanes = lambda i: slice(i * width + head * HD, i * width + (head + 1) * HD)
            query, key, value = (qkv_ref[0, rows, lanes(i)] for i in range(3))
            grad = back_att[rows, lanes(0)]
            probs = softmax(query, key, same)
            grad_p = dot_nt(grad, value)
            centre = jnp.sum(probs * grad_p, -1, keepdims=True)
            grad_s = (probs * (grad_p - centre)).astype(LOW)
            tmp_ref[rows, lanes(0)] = dot(grad_s, key) * scale
            tmp_ref[rows, lanes(1)] = dot_tn(grad_s, query) * scale
            tmp_ref[rows, lanes(2)] = dot_tn(probs.astype(LOW), grad)
    out_ref[0, :, : 2 * width] = turn(tmp_ref[:, : 2 * width], cos_ref[...], sin_ref[...], -1.0).astype(LOW)
    out_ref[0, :, 2 * width : 3 * width] = tmp_ref[:, 2 * width :].astype(LOW)
    out_ref[0, :, 3 * width :] = att_ref[0]
    part = dot_nt(out_ref[0, :, : 3 * width], w_ref[0, :, : 3 * width])

    @pl.when(step == 0)
    def _():
        back_ref[...] = part

    @pl.when(step > 0)
    def _():
        back_ref[...] += part

    @pl.when(step == last)
    def _():
        def body(block, rows):
            lead = col_ref[rows, :1] != 0
            grad_a = back_ref[rows, :]
            normed, inv_std = layer_norm(x0_ref[rows, :])
            back = norm_back(grad_a, normed, inv_std, spread(mod_ref, 1, block, lead))
            grad_x0 = (gx1_ref[rows, :] + back).astype(LOW)
            low_ref[rows, :] = grad_x0
            return lead, (grad_a, grad_a * normed, grad_x0.astype(F32))

        bias = jnp.zeros((1, D), F32)
        for image, rows in enumerate(slabs(tokens, body, 3)):
            for k in range(2):
                sums_ref[k, image : image + 1, :] = rows[k]
            bias = bias + rows[2]
        rows_ref[:PATCH_IN, :] = dot(patch_ref[...], low_ref[...])
        rows_ref[PATCH_IN : PATCH_IN + 1, :] = bias
        rows_ref[PATCH_IN + 1 :, :] = jnp.zeros((7, D), F32)


def attn_backward(grad_proj, gx1, x_zero, patches, modulation, wa_all, qkv, att, tables):
    blocks, tokens, width = att.shape
    full = (tokens, D)
    ins = (grad_proj, gx1, x_zero, patches, modulation)
    outs = [((PATCH_IN + 8, D), F32), ((2, modulation.shape[0], D), F32)]
    return pl.pallas_call(
        attn_backward_kernel,
        grid=(blocks,),
        out_shape=[jax.ShapeDtypeStruct((blocks, tokens, 4 * width), LOW)]
        + [jax.ShapeDtypeStruct(*o) for o in outs],
        in_specs=[whole(a.shape) for a in ins]
        + [by_block(D, 4 * width), by_block(tokens, 3 * width), by_block(tokens, width)]
        + [whole(a.shape) for a in tables],
        out_specs=[by_block(tokens, 4 * width)] + [whole(o[0]) for o in outs],
        scratch_shapes=[
            pltpu.VMEM((tokens, 3 * width), F32), pltpu.VMEM((tokens, width), LOW),
            pltpu.VMEM(full, F32), pltpu.VMEM(full, LOW),
        ],
        compiler_params=pltpu.CompilerParams(vmem_limit_bytes=VMEM_LIMIT),
        name="attn_backward",
    )(*ins, wa_all, qkv, att, *tables)


def gather_library(wa, wf, small):
    dp, mp = lax.axis_size("dp"), lax.axis_size("mp")
    info, embed, first, first_bias, second, part, tail, columns = small
    depth = wa.shape[0]

    def one(w):
        full = lax.all_gather(w, BOTH, axis=0)
        full = full.reshape(dp, mp, *w.shape).transpose(1, 0, 2, 3)
        return full.reshape(mp, dp * w.shape[0], w.shape[1])

    over_dp = lambda v: lax.all_gather(v, "dp", axis=0)
    pre = lax.psum(dot(embed, first) + first_bias, "mp")
    cond = lax.psum(dot(jax.nn.silu(pre).astype(LOW), second) + part, "mp")
    scaled_all = over_dp(jax.nn.silu(cond).astype(LOW))
    scaled = scaled_all.reshape(-1, D)
    mine = lax.dynamic_slice_in_dim(scaled, lax.axis_index("dp") * depth, depth, 1)
    mod = lax.psum_scatter(dot(mine, columns), "dp", scatter_dimension=0, tiled=True)
    over_mp = lambda v: lax.all_gather(v, "mp", axis=0)
    return one(wa), one(wf), over_mp(mod), over_mp(tail), pre, cond, scaled_all, over_dp(info), over_dp(jax.nn.silu(pre).astype(LOW))


def sibling(value):
    mp = lax.axis_size("mp")
    return lax.ppermute(value, "mp", [(i, i + 1 - 2 * (i % 2)) for i in range(mp)])


def vector_grads(grad_mod, mod_rows, second, cond, pre):
    images = grad_mod.shape[0] // 8
    group = lax.all_gather(grad_mod.reshape(8, images, D), "mp", axis=1, tiled=True)
    group = group.transpose(1, 0, 2).reshape(cond.shape[0], 8 * D)
    every = lax.all_gather(group, "dp", axis=0, tiled=True)
    scaled = lax.all_gather(dot_nt(every, mod_rows), "dp", axis=1, tiled=True)
    scaled = lax.dynamic_slice_in_dim(scaled, lax.axis_index("dp") * cond.shape[0], cond.shape[0], 0)
    grad_cond = (scaled * silu_slope(cond)).astype(LOW)
    hidden = lax.psum(dot_nt(grad_cond, second), "mp")
    grad_pre = (hidden * silu_slope(pre)).astype(LOW)
    return lax.all_gather(jnp.concatenate([grad_cond, grad_pre], 0), "dp", axis=0)


def plane_grads(turned, ya, yf):
    dp, mp = lax.axis_size("dp"), lax.axis_size("mp")
    core, place = lax.axis_index("mp") % 2, lax.axis_index("mp") // 2
    x_all = jnp.stack(turned)
    x_two = jnp.concatenate([x_all, sibling(x_all)], 2)
    width_a, width_f = ya.shape[2] // 4, yf.shape[2] // 3

    def halves(values):
        split = values.reshape(mp // 2, 2, *values.shape[1:])
        mine = lax.dynamic_index_in_dim(split, core, 1, False)
        theirs = lax.dynamic_index_in_dim(split, 1 - core, 1, False)
        return jnp.concatenate([mine, sibling(theirs)], 1)

    def product(x, values):
        return jnp.einsum("dt,btn->bdn", x, values, preferred_element_type=F32)

    ya_two, yf_two = halves(ya), halves(yf)
    grad_a = jnp.concatenate(
        [product(x_two[0], ya_two[..., : 3 * width_a]), product(x_two[1], ya_two[..., 3 * width_a :])], 2
    )
    grad_f = jnp.concatenate(
        [product(x_two[2], yf_two[..., : 2 * width_f]), product(x_two[3], yf_two[..., 2 * width_f :])], 2
    )
    grad = jnp.stack([grad_f[..., :STEP], grad_f[..., STEP:], grad_a])
    part = lax.psum_scatter(grad, "dp", scatter_dimension=2, tiled=True)
    total = lax.dynamic_index_in_dim(part, place, 1, False)
    for hop in range(1, mp // 2):
        perm = [(i, (i + 2 * hop) % mp) for i in range(mp)]
        out = lax.dynamic_index_in_dim(part, (place + hop) % (mp // 2), 1, False)
        total = total + lax.ppermute(out, "mp", perm)
    return total


def per_device(
    patches, target, segments, positions, classes, timesteps, t_weight, step_count,
    qkv_w, qkv_m, qkv_v, out_w, out_m, out_v, ffn_in_w, ffn_in_m, ffn_in_v,
    ffn_out_w, ffn_out_m, ffn_out_v, mod_w, mod_m, mod_v, table_w, table_m, table_v,
):
    mp_count, dp_count = lax.axis_size("mp"), lax.axis_size("dp")
    mp_index, dp_index = lax.axis_index("mp"), lax.axis_index("dp")
    tokens = patches.shape[1]
    pairs = tokens // PAIR
    images = 2 * pairs
    own_rows = table_w.shape[0]
    depth = mod_w.shape[0]
    width_a, width_f = qkv_w.shape[2], ffn_in_w.shape[2]

    regular = dp_count == 2 * DEPTH and mp_count == 4
    group_images = classes.shape[0]
    wa = jnp.concatenate([qkv_w[0], qkv_w[1], qkv_w[2], out_w.T], 1).astype(LOW)
    wf = jnp.concatenate([ffn_in_w[0], ffn_in_w[1], ffn_out_w.T], 1).astype(LOW)

    table_b = table_w.astype(LOW)
    mod_b = mod_w.astype(LOW)
    gap = D + 16
    padded = lax.dynamic_update_slice(jnp.zeros((2 * gap + own_rows, D), LOW), table_b, (gap, 0))

    def placed(row, count):
        return lax.dynamic_slice_in_dim(padded, row - mp_index * own_rows + gap, count, 0)

    half = FREQ // 2
    freqs = jnp.exp(-math.log(10000.0) * jnp.arange(half, dtype=F32) / half)

    def embedding(times):
        angles = times[:, None] * freqs[None, :]
        return jnp.concatenate([jnp.cos(angles), jnp.sin(angles)], 1).astype(LOW)

    row_ids = mp_index * own_rows + jnp.arange(own_rows, dtype=jnp.int32)
    own_hot = (classes[:, None] == row_ids[None, :]).astype(LOW)
    part = matmul(own_hot, table_b) + placed(ROW_OUT_BIAS, 1).astype(F32)
    info = jnp.zeros((8, 128), F32)
    for i, values in enumerate((classes, timesteps, t_weight)):
        info = info.at[i, :group_images].set(values.astype(F32))
    mod_cols = mod_w.shape[1] // mp_count
    small = (
        info, embedding(timesteps.astype(F32)), placed(ROW_TIME_IN, FREQ),
        placed(ROW_TIME_BIAS, 1).astype(F32), placed(ROW_TIME_OUT, D), part,
        jnp.pad(placed(ROW_PATCH, TAIL), ((0, 64 - TAIL), (0, 0))),
        lax.dynamic_slice_in_dim(mod_w, mp_index * mod_cols, mod_cols, 1).astype(LOW),
    )
    own_seg = lax.dynamic_slice_in_dim(segments, mp_index * tokens, tokens)
    own_pos = lax.dynamic_slice_in_dim(positions, mp_index * tokens, tokens, 1)
    even = (own_seg % 2 == 0).reshape(pairs, PAIR)
    heads = 2 * width_a // HD
    cos_row, sin_row = (jnp.tile(t, (1, heads)) for t in rotary_tables(own_pos))
    even_col = even.astype(jnp.int32).reshape(tokens, 1)
    even_row = jnp.broadcast_to(even.astype(jnp.int32)[:, None], (pairs, 8, PAIR))
    tables = (cos_row, sin_row, even_col, even_row)

    if regular:
        gathered = gather_pallas(wa, wf, small, patches, tables, dp_count, mp_count)
        wa_all, wf_all, modulation, tail, pre, cond, scaled, infos, hidden = gathered[:9]
        x_zero, x_one, proj, m_in, a_turned, m_turned, qkv, att = gathered[9:]
    else:
        wa_all, wf_all, mod_all, tails, pre, cond, scaled, infos, hidden = gather_library(wa, wf, small)
        tail = jnp.sum(tails.astype(F32), 0)
        mod_own = lax.dynamic_slice_in_dim(mod_all, mp_index * images, images, 1)
        mod_bias = tail[ROW_MOD_BIAS - ROW_PATCH : TAIL].reshape(-1)
        modulation = mod_own.transpose(1, 0, 2).reshape(images, -1) + mod_bias
        x_zero, x_one, proj, m_in, a_turned, m_turned, qkv, att = attn_forward(
            patches, tail[:PATCH_IN].astype(LOW), tail[PATCH_IN][None, :], modulation, wa_all, tables
        )
    count_all = dp_count * group_images
    scaled = scaled.reshape(count_all, D)
    classes_all, times_all, weights_all = (infos[:, i, :group_images].reshape(-1) for i in range(3))
    head_rows = tail[PATCH_IN + 1 : PATCH_IN + 1 + OUT].astype(LOW)
    weight_sum = jnp.sum(weights_all)

    ones = jnp.ones((count_all, 1), LOW)
    zeros = lambda n: jnp.zeros((count_all, n), LOW)
    own_cols = lambda a: lax.dynamic_slice_in_dim(a, mp_index * own_rows, own_rows, 1)
    left_pre = own_cols(
        jnp.concatenate([zeros(NCLS), embedding(times_all), ones, zeros(ROWS - ROW_TIME_OUT)], 1)
    )
    class_hot = (classes_all[:, None] == jnp.arange(NCLS, dtype=F32)[None, :]).astype(LOW)
    hidden = hidden.reshape(count_all, D)
    left_cond = own_cols(
        jnp.concatenate(
            [class_hot, zeros(ROW_TIME_OUT - NCLS), hidden, ones, zeros(ROWS - ROW_PATCH)], 1
        )
    )
    own_scaled = lax.dynamic_slice_in_dim(scaled, dp_index * depth, depth, 1)

    first_len = jnp.sum(even.astype(F32), 1)
    own_tw = lax.dynamic_slice_in_dim(t_weight, mp_index * images, images).reshape(pairs, 2)
    per_tok = own_tw / jnp.stack([first_len, PAIR - first_len], 1)
    tok_weight = jnp.where(even, per_tok[:, :1], per_tok[:, 1:]).reshape(1, tokens)
    weights = jnp.concatenate([tok_weight, tok_weight / weight_sum], 0)
    yf, grad_x1, grad_proj, proj_turned, mo_turned, grad_head, loss, sums_f = ffn(
        m_in, x_one, proj, modulation, head_rows, target, weights, even_col, wf_all
    )
    ya, grad_patch, sums_a = attn_backward(
        grad_proj, grad_x1, x_zero, patches, modulation, wa_all, qkv, att, tables
    )
    loss_part = loss[0, 0]
    x_turned = (a_turned, proj_turned, m_turned, mo_turned)
    grad_mod = jnp.concatenate(
        [sums_a[0], sums_a[1], sums_f[5], sums_f[3], sums_f[4], sums_f[2], sums_f[0], sums_f[1]], 0
    ).astype(LOW)
    cond_own = jnp.pad(cond.reshape(mp_count, images, D), ((0, 0), (0, 8 - images), (0, 0)))
    pre_own = jnp.pad(pre.reshape(mp_count, images, D), ((0, 0), (0, 8 - images), (0, 0)))
    if regular:
        summed, vectors = weight_grads(
            x_turned, ya, yf, grad_mod, mod_b, small[4], cond_own, pre_own.reshape(-1, D), dp_count
        )
    else:
        summed = plane_grads(x_turned, ya, yf)
        vectors = vector_grads(grad_mod, mod_b, small[4], cond, pre)
    own_wf, own_wa = jnp.concatenate([summed[0], summed[1]], 1), summed[2]

    grad_mod_all = lax.all_gather(grad_mod, BOTH, axis=0).reshape(-1, 8, images, D)
    grad_mod_all = grad_mod_all.transpose(0, 2, 1, 3).reshape(count_all, 8 * D)
    grad_mod_w = matmul_tn(own_scaled, grad_mod_all)
    grad_mod_bias = jnp.sum(grad_mod_all.astype(F32), 0).reshape(8, D)
    grad_cvec = vectors[:, :group_images].reshape(count_all, D)
    grad_pre = vectors[:, group_images:].reshape(count_all, D)
    token_rows = jnp.concatenate([grad_patch[: PATCH_IN + 1], grad_head], 0)
    token_rows = jnp.concatenate([lax.psum(token_rows, BOTH), grad_mod_bias], 0)
    blank = -(-own_rows // 8) * 8
    start = jnp.clip(mp_index * own_rows - ROW_PATCH + blank, 0, blank + 64)
    spaced = lax.dynamic_update_slice(jnp.zeros((2 * blank + 64, D), F32), token_rows, (blank, 0))
    tail_own = lax.dynamic_slice_in_dim(spaced, start, own_rows, 0)
    grad_table = matmul_tn(left_cond, grad_cvec) + matmul_tn(left_pre, grad_pre) + tail_own

    grad_qkv = jnp.stack([own_wa[:, j * width_a : (j + 1) * width_a] for j in range(3)])
    grad_out_w = own_wa[:, 3 * width_a :].T
    grad_ffn_in = jnp.stack([own_wf[:, j * width_f : (j + 1) * width_f] for j in range(2)])
    grad_ffn_out = own_wf[:, 2 * width_f :].T
    sharded_sq = jnp.sum(own_wa * own_wa) + jnp.sum(own_wf * own_wf)
    copied_sq = (
        jnp.sum(grad_mod_w * grad_mod_w) / mp_count + jnp.sum(grad_table * grad_table) / dp_count
    )
    scalars = jnp.concatenate(
        [jnp.full((1, 128), sharded_sq + copied_sq), jnp.full((1, 128), loss_part), jnp.zeros((6, 128), F32)], 0
    )
    scalars = sum_pallas(scalars, dp_count, mp_count) if regular else lax.psum(scalars, BOTH)
    square_sum, loss_sum = scalars[0, 0], scalars[1, 0]
    norm = jnp.sqrt(square_sum)
    total_tokens = tokens * mp_count * dp_count
    clip = jnp.minimum(1.0, CLIP_SCALE / math.sqrt(total_tokens) / (norm + 1e-06))
    count = step_count[0].astype(F32)
    results = [(loss_sum / weight_sum).reshape(1), norm.reshape(1)]
    for weight, first, second, grad in (
        (qkv_w, qkv_m, qkv_v, grad_qkv),
        (out_w, out_m, out_v, grad_out_w),
        (ffn_in_w, ffn_in_m, ffn_in_v, grad_ffn_in),
        (ffn_out_w, ffn_out_m, ffn_out_v, grad_ffn_out),
        (mod_w, mod_m, mod_v, grad_mod_w),
        (table_w, table_m, table_v, grad_table),
    ):
        results.extend(adam(weight, first, second, grad * clip, count))
    return tuple(results)


def solution(mesh):
    tok, grp = P(None, BOTH), P("dp")
    cols, rows = P(None, "dp", "mp"), P("mp", "dp")
    weights = (cols,) * 3 + (rows,) * 3 + (cols,) * 3 + (rows,) * 3
    weights += (P("dp", None),) * 3 + (P("mp", None),) * 3
    in_specs = (tok, tok, grp, P(None, "dp"), grp, grp, grp, P()) + weights
    return jax.shard_map(
        per_device, mesh=mesh, in_specs=in_specs, out_specs=(P(), P()) + weights, check_vma=False
    )
```

```python
import functools
import math

import jax
import jax.numpy as jnp
from jax import lax
from jax.experimental import pallas as pl
from jax.experimental.pallas import tpu as pltpu
from jax.sharding import PartitionSpec as P

D = 1152
HD = 72
PATCH_IN = 16
OUT = 32
FREQ = 256
NCLS = 1001
PAIR = 320

ROW_TIME_IN = NCLS
ROW_TIME_BIAS = ROW_TIME_IN + FREQ
ROW_TIME_OUT = ROW_TIME_BIAS + 1
ROW_OUT_BIAS = ROW_TIME_OUT + D
ROW_PATCH = ROW_OUT_BIAS + 1
ROW_PATCH_BIAS = ROW_PATCH + PATCH_IN
ROW_HEAD = ROW_PATCH_BIAS + 1
ROW_MOD_BIAS = ROW_HEAD + OUT
ROWS = ROW_MOD_BIAS + 8
TAIL = ROWS - ROW_PATCH

EPS_NORM = 1e-06
BETA_ONE = 0.9
BETA_TWO = 0.95
ADAM_EPS = 1e-08
LEARN_RATE = 0.03
WEIGHT_DECAY = 0.1
CLIP_SCALE = 0.5
LOW = jnp.bfloat16
F32 = jnp.float32
BOTH = ("dp", "mp")
MESH = pl.DeviceIdType.MESH
STEP = 1152
HOOKS = (0, 1, 2, 3)
LINE_FIRST = (True, True, False)
BEHIND = (0, 4, 5)
SENDS = 20
DEPTH = 4


def matmul(left, right):
    return jnp.dot(left, right, preferred_element_type=F32)


def matmul_tn(left, right):
    return lax.dot_general(left, right, (((0,), (0,)), ((), ())), preferred_element_type=F32)


def matmul_nt(left, right):
    return lax.dot_general(left, right, (((1,), (1,)), ((), ())), preferred_element_type=F32)


def layer_norm(values):
    centred = values - jnp.mean(values, -1, keepdims=True)
    inv_std = lax.rsqrt(jnp.mean(centred * centred, -1, keepdims=True) + EPS_NORM)
    return (centred * inv_std, inv_std)


def norm_back(grad, normed, inv_std, scale_rows):
    inner = grad * (1.0 + scale_rows)
    return inv_std * (
        inner
        - jnp.mean(inner, -1, keepdims=True)
        - normed * jnp.mean(inner * normed, -1, keepdims=True)
    )


def silu_slope(values):
    sigma = jax.nn.sigmoid(values)
    return sigma * (1.0 + values * (1.0 - sigma))


def adam(weight, first, second, grad, count):
    first = BETA_ONE * first + (1.0 - BETA_ONE) * grad
    second = BETA_TWO * second + (1.0 - BETA_TWO) * grad * grad
    m_hat = first / (1.0 - BETA_ONE**count)
    v_hat = second / (1.0 - BETA_TWO**count)
    weight = weight - LEARN_RATE * (m_hat / (jnp.sqrt(v_hat) + ADAM_EPS) + WEIGHT_DECAY * weight)
    return (weight, first, second)


def rotary_tables(positions):
    quarter = HD // 4
    freqs = jnp.exp(-math.log(10000.0) * jnp.arange(quarter, dtype=F32) / quarter)
    angle = positions.astype(F32)[:, :, None] * freqs[None, None, :]
    cosine, sine = jnp.cos(angle), jnp.sin(angle)
    cos_row = jnp.concatenate([cosine[0], cosine[0], cosine[1], cosine[1]], 1)
    sin_row = jnp.concatenate([-sine[0], sine[0], -sine[1], sine[1]], 1)
    return cos_row, sin_row


def coordinates():
    dp, mp = lax.axis_index("dp"), lax.axis_index("mp")
    z, x = dp // 2, dp % 2
    y, c = mp // 2, mp % 2
    first = (x + (1 - c) * (1 - 2 * x), y + c * (1 - 2 * y))
    second = (x + c * (1 - 2 * x), y + (1 - c) * (1 - 2 * y))
    return z, x, y, c, first, second


def greet(z, x, y, c, first, second, depth):
    barrier = pltpu.get_barrier_semaphore()

    def signal(dp, mp):
        pl.semaphore_signal(barrier, inc=1, device_id=(dp, mp), device_id_type=MESH)

    signal(z * 2 + first[0], first[1] * 2 + c)
    signal(z * 2 + second[0], second[1] * 2 + c)
    signal(z * 2 + x, y * 2 + 1 - c)
    pl.when(z > 0)(lambda: signal((z - 1) * 2 + x, y * 2 + c))
    pl.when(z < depth - 1)(lambda: signal((z + 1) * 2 + x, y * 2 + c))
    peers = 3 + jnp.minimum(z, 1) + jnp.minimum(depth - 1 - z, 1)
    pl.semaphore_wait(barrier, peers)


def peers_greet(dp_count, mp_count):
    dp, mp = lax.axis_index("dp"), lax.axis_index("mp")
    barrier = pltpu.get_barrier_semaphore()
    for hop in range(1, dp_count):
        pl.semaphore_signal(
            barrier, inc=1, device_id=(lax.rem(dp + hop, dp_count), mp), device_id_type=MESH
        )
    for hop in range(1, mp_count):
        pl.semaphore_signal(
            barrier, inc=1, device_id=(dp, lax.rem(mp + hop, mp_count)), device_id_type=MESH
        )
    pl.semaphore_wait(barrier, dp_count + mp_count - 2)


class Round:
    def __init__(self, axis, count, source, target, send, recv, base):
        self.me = lax.axis_index(axis)
        self.axis, self.count, self.source, self.target = axis, count, source, target
        self.send, self.recv, self.base = send, recv, base

    def moves(self):
        for hop in range(1, self.count):
            peer = lax.rem(self.me + hop, self.count)
            other = {"dp": (peer, lax.axis_index("mp")), "mp": (lax.axis_index("dp"), peer)}[self.axis]
            yield pltpu.make_async_remote_copy(
                src_ref=self.source(peer), dst_ref=self.target.at[self.me],
                send_sem=self.send.at[self.base + hop], recv_sem=self.recv.at[self.base + hop],
                device_id=other, device_id_type=MESH,
            )

    def push(self):
        for move in self.moves():
            move.start()

    def wait(self):
        for hop in range(1, self.count):
            slot = self.target.at[lax.rem(self.me + self.count - hop, self.count)]
            pltpu.make_async_copy(slot, slot, self.recv.at[self.base + hop]).wait()

    def finish(self):
        for move in self.moves():
            move.wait_send()


def gather_kernel(
    depth, mp_count, wa_ref, wf_ref, info_ref, emb_ref, t1_ref, b1_ref, t2_ref, part_ref, tail_ref, mcol_ref,
    patch_ref, cos_ref, sin_ref, col_ref, row_ref,
    wa_all, wf_all, mod_ref, tails_ref, pre_ref, cond_ref, scaled_ref, infos_ref, hid_ref,
    x0_out, x1_out, proj_out, m_out, at_out, mt_out, qkv_out, att_out, probs_out,
    info_buf, pre_sum, cond_sum, tail_buf, scaled_buf, hid_buf, mod_part, mod_sum, mod_buf, a_ref, wa_buf,
    x0_ref, x1_ref, proj_ref, m_ref, at_ref, mt_ref, qkv_ref, att_ref, probs_buf,
    recv, send, local, little_recv, little_send, wa_sem, out_sem, probs_sem,
):
    dp_count = 2 * depth
    z, x, y, c, first, second = coordinates()
    dp, mp = lax.axis_index("dp"), lax.axis_index("mp")
    rows = wa_ref.shape[0]
    images = emb_ref.shape[0]
    peers_greet(dp_count, mp_count)

    bases = iter(range(0, 64 * dp_count, dp_count))
    little = lambda axis, count, source, target: Round(
        axis, count, source, target, little_send, little_recv, next(bases)
    )
    own = lambda buf, me: lambda peer: buf.at[me]
    info = little("dp", dp_count, own(info_buf, dp), info_buf)
    pre_r = little("mp", mp_count, own(pre_sum, mp), pre_sum)
    tail_r = little("mp", mp_count, own(tail_buf, mp), tail_buf)
    cond_r = little("mp", mp_count, own(cond_sum, mp), cond_sum)
    scaled_a = little("dp", dp_count, own(scaled_buf, dp), scaled_buf)
    hid_a = little("dp", dp_count, own(hid_buf, dp), hid_buf)
    mod_r = little("dp", dp_count, lambda peer: mod_part.at[peer], mod_sum)
    mod_a = little("mp", mp_count, own(mod_buf, mp), mod_buf)
    rounds = (info, pre_r, tail_r, cond_r, scaled_a, hid_a, mod_r, mod_a)
    total = lambda buf, count: functools.reduce(lambda a, b: a + b, [buf[i] for i in range(count)])

    def begin():
        info_buf[dp] = info_ref[...]
        info.push()
        pre_sum[mp] = dot(emb_ref[...], t1_ref[...]) + b1_ref[...]
        pre_r.push()
        tail_buf[mp] = tail_ref[...]
        tail_r.push()

    def hidden():
        pre_r.wait()
        pre = total(pre_sum, mp_count)
        pre_ref[...] = pre
        act = (pre * lax.logistic(pre)).astype(LOW)
        cond_sum[mp] = dot(act, t2_ref[...]) + part_ref[...]
        cond_r.push()
        hid_buf[dp] = act

    def condition():
        cond_r.wait()
        cond = total(cond_sum, mp_count)
        cond_ref[...] = cond
        scaled_buf[dp] = (cond * lax.logistic(cond)).astype(LOW)
        scaled_a.push()

    def modulate():
        scaled_a.wait()
        scaled = scaled_buf[...].reshape(dp_count * images, D)
        row = lax.broadcasted_iota(jnp.int32, (D, rows), 0)
        col = lax.broadcasted_iota(jnp.int32, (D, rows), 1)
        pick = (row == col + dp * rows).astype(F32).astype(LOW)
        mine = dot(scaled, pick).astype(LOW)
        mod_part[...] = dot(mine, mcol_ref[...]).reshape(mod_part.shape)
        mod_sum[dp] = mod_part[dp]
        mod_r.push()

    def collect():
        mod_r.wait()
        mod_buf[mp] = total(mod_sum, dp_count)
        mod_a.push()
        hid_a.push()

    hooks = (hidden, condition, modulate, collect)

    corner = (first[0] + second[0] - x, first[1] + second[1] - y)
    spots = {"here": (x, y), "first": first, "second": second, "corner": corner}
    ids = {"here": 0, "first": 1, "second": 2, "corner": 3}
    swapped = {"here": 0, "first": 2, "second": 1, "corner": 3}
    groups = [(wa_ref, wa_all, 0, LINE_FIRST[0])]
    groups += [(wf_ref, wf_all, i * STEP, LINE_FIRST[1 + i]) for i in range(wf_ref.shape[1] // STEP)]
    count = len(groups)

    def slot(g, zz, spot, core):
        _, ref, column, _ = groups[g]
        return ref.at[spot[1] * 2 + core, pl.ds((zz * 2 + spot[0]) * rows, rows), pl.ds(column, STEP)]

    def mine(g):
        return groups[g][0].at[:, pl.ds(groups[g][2], STEP)]

    def arrive(g, zz, kind, cond=None, plane=0):
        dst = slot(g, zz, spots[kind], c if plane == 0 else 1 - c)
        sem = recv.at[g, plane, ids[kind] if plane == 0 else swapped[kind], zz]
        wait = pltpu.make_async_copy(dst, dst, sem)
        if cond is None:
            wait.wait()
        else:
            pl.when(cond)(wait.wait)

    def sides(k):
        below, above = jnp.maximum(z - k, 0), jnp.minimum(z + k, depth - 1)
        return ((below, z >= k, "up", z < depth - 1), (above, z < depth - k, "down", z > 0))[: 1 if k == 0 else 2]

    def stage(g, k, live=True):
        line_first = groups[g][3]
        numbers = iter(range((g * (depth + 2) + k) * SENDS, (g * (depth + 2) + k + 1) * SENDS))

        def copy(zz, kind, route, cond=None, own=False):
            plane, sem_kind = 0, kind
            if route == "up":
                target = ((z + 1) * 2 + x, mp)
            elif route == "down":
                target = ((z - 1) * 2 + x, mp)
            elif route == "first":
                target, sem_kind = (z * 2 + first[0], first[1] * 2 + c), "first"
            elif route == "second":
                target = (z * 2 + second[0], second[1] * 2 + c)
                sem_kind = "second" if kind == "here" else "corner"
            else:
                target, plane = (dp, y * 2 + 1 - c), 1
            made = pltpu.make_async_remote_copy(
                src_ref=mine(g) if own else slot(g, zz, spots[kind], c), dst_ref=slot(g, zz, spots[kind], c),
                send_sem=send.at[next(numbers)], recv_sem=recv.at[g, plane, ids[sem_kind], zz],
                device_id=target, device_id_type=MESH,
            )
            act = made.start if live else made.wait_send
            if cond is None:
                act()
            else:
                pl.when(cond)(act)

        def take(zz, kind, cond=None):
            if live:
                arrive(g, zz, kind, cond)

        if k == 0:
            if live:
                pltpu.make_async_copy(mine(g), slot(g, z, spots["here"], c), local.at[g]).start()
            copy(z, "here", "first", None, True)
            copy(z, "here", "up", z < depth - 1, True)
            copy(z, "here", "down", z > 0, True)
            copy(z, "here", "second", None, True)
            copy(z, "here", "core", None, True)
        if k == 1 and not line_first:
            take(z, "first")
            copy(z, "first", "up", z < depth - 1)
            copy(z, "first", "down", z > 0)
            copy(z, "first", "second")
            copy(z, "first", "core")
        if 0 < k < depth:
            for zz, cond, route, more in sides(k):
                take(zz, "here", cond)
                copy(zz, "here", route, cond & more)
                if line_first:
                    copy(zz, "here", "first", cond)
                copy(zz, "here", "second", cond)
                copy(zz, "here", "core", cond)
        if 0 <= k - 1 < depth and (line_first or k > 1):
            for zz, cond, route, more in sides(k - 1):
                take(zz, "first", cond)
                if not line_first:
                    copy(zz, "first", route, cond & more)
                copy(zz, "first", "second", cond)
                copy(zz, "first", "core", cond)
        if 0 <= k - 2 < depth:
            for zz, cond, _, _ in sides(k - 2):
                for kind in ("second", "corner"):
                    take(zz, kind, cond)
                    copy(zz, kind, "core", cond)

    def settle(g):
        for zz in range(depth):
            for kind in ("here", "first", "second", "corner"):
                arrive(g, zz, kind, None, 1)
        pltpu.make_async_copy(mine(g), slot(g, z, spots["here"], c), local.at[g]).wait()

    begin()
    steps = [
        [(g, moment - BEHIND[g]) for g in range(count) if 0 <= moment - BEHIND[g] < depth + 2]
        for moment in range(depth + 2 + max(BEHIND))
    ]
    for moment in range(depth + 2):
        for g, k in steps[moment]:
            stage(g, k)
        for number, hook in enumerate(hooks):
            if HOOKS[number] == moment:
                hook()
    settle(0)
    load = lambda m: pltpu.make_async_copy(wa_all.at[m], wa_buf.at[m % 2], wa_sem.at[m % 2])
    load(0).start()
    mod_a.wait()
    tail_r.wait()
    tails_ref[...] = functools.reduce(lambda a, b: a + b, [tail_buf[i].astype(F32) for i in range(mp_count)])
    own_images = images // mp_count
    width = mcol_ref.shape[1]
    for i in range(mp_count):
        rows_of = lambda m: mod_buf[i, m * own_images : (m + 1) * own_images, :]
        picked = functools.reduce(lambda a, m: jnp.where(mp == m, rows_of(m), a), range(1, mp_count), rows_of(0))
        mod_ref[:, i * width : (i + 1) * width] = picked
    for j in range(8):
        bias = tails_ref[ROW_MOD_BIAS - ROW_PATCH + j : ROW_MOD_BIAS - ROW_PATCH + j + 1, :]
        mod_ref[:, j * D : (j + 1) * D] += bias
    attn_begin(
        patch_ref, tails_ref[:PATCH_IN, :].astype(LOW), tails_ref[PATCH_IN : PATCH_IN + 1, :],
        mod_ref, col_ref, x0_ref, a_ref, at_ref,
    )
    proj_ref[...] = jnp.zeros(proj_ref.shape, F32)

    later = [pair for moment in steps[depth + 2 :] for pair in moment]

    def stored(m, i):
        return pltpu.make_async_copy(probs_buf.at[i % 2], probs_out.at[m, i], probs_sem.at[i % 2])

    def heads(m, _):
        pl.when(m + 1 < mp_count)(lambda: load(m + 1).start())
        load(m).wait()

        def keep(i, probs):
            if i > 1:
                stored(m, i - 2).wait()
            else:
                pl.when(m > 0)(lambda: stored(m - 1, probs_out.shape[1] - 2 + i).wait())
            probs_buf[i % 2] = probs
            stored(m, i).start()

        proj_ref[...] += attn_block(
            wa_buf.at[m % 2], cos_ref, sin_ref, col_ref, row_ref, a_ref, qkv_ref.at[m], att_ref.at[m], keep
        )
        for i in range(mp_count):
            part = later[i * len(later) // mp_count : (i + 1) * len(later) // mp_count]

            @pl.when(m == i)
            def _(part=part):
                for g, k in part:
                    stage(g, k)

        return 0

    lax.fori_loop(0, mp_count, heads, 0)
    for i in range(2):
        stored(mp_count - 1, probs_out.shape[1] - 2 + i).wait()
    hid_a.wait()
    info.wait()
    scaled_ref[...] = scaled_buf[...]
    infos_ref[...] = info_buf[...]
    hid_ref[...] = hid_buf[...]
    attn_end(mod_ref, col_ref, x0_ref, proj_ref, x1_ref, m_ref, mt_ref)
    made = (
        (x0_ref, x0_out), (x1_ref, x1_out), (proj_ref, proj_out), (m_ref, m_out),
        (at_ref, at_out), (mt_ref, mt_out), (qkv_ref, qkv_out), (att_ref, att_out),
    )
    leaving = [pltpu.make_async_copy(a, b, out_sem.at[i]) for i, (a, b) in enumerate(made)]
    for move in leaving:
        move.start()
    for g in range(1, count):
        settle(g)
    for move in leaving:
        move.wait()
    for g in range(count):
        for k in range(depth + 2):
            stage(g, k, False)
    for one in rounds:
        one.finish()


def gather_pallas(wa, wf, small, patches, tables, dp, mp, collective_id=0):
    depth = dp // 2
    groups = 1 + wf.shape[1] // STEP
    images, width = small[1].shape[0], small[7].shape[1]
    tail = small[6].shape[0]
    tokens, heads = patches.shape[1], wa.shape[1] // 4
    full, turned = (tokens, D), (D, tokens)
    shapes = [
        ((images // mp, mp * width), F32), ((tail, D), F32), ((images, D), F32), ((images, D), F32),
        ((dp, images, D), LOW), ((dp, 8, 128), F32), ((dp, images, D), LOW),
    ]
    late = [
        (full, F32), (full, F32), (full, F32), (full, LOW), (turned, LOW), (turned, LOW),
        ((mp, tokens, 3 * heads), LOW), ((mp, tokens, heads), LOW),
    ]
    probs = ((mp, tokens // PAIR * (heads // HD), PAIR, PAIR), F32)
    hbm, vmem = pl.BlockSpec(memory_space=pl.ANY), pl.BlockSpec(memory_space=pltpu.VMEM)
    return pl.pallas_call(
        functools.partial(gather_kernel, depth, mp),
        out_shape=[jax.ShapeDtypeStruct((mp, dp * s.shape[0], s.shape[1]), s.dtype) for s in (wa, wf)]
        + [jax.ShapeDtypeStruct(*s) for s in shapes + late + [probs]],
        in_specs=[hbm] * 2 + [vmem] * 13,
        out_specs=[hbm] * 2 + [vmem] * len(shapes) + [hbm] * (len(late) + 1),
        scratch_shapes=[
            pltpu.VMEM((dp, 8, 128), F32), pltpu.VMEM((mp, images, D), F32), pltpu.VMEM((mp, images, D), F32),
            pltpu.VMEM((mp, tail, D), LOW), pltpu.VMEM((dp, images, D), LOW), pltpu.VMEM((dp, images, D), LOW),
            pltpu.VMEM((dp, images, width), F32), pltpu.VMEM((dp, images, width), F32),
            pltpu.VMEM((mp, images, width), F32),
            pltpu.VMEM(full, LOW), pltpu.VMEM((2, D, wa.shape[1]), LOW),
            *(pltpu.VMEM(*s) for s in late),
            pltpu.VMEM((2, PAIR, PAIR), F32),
            pltpu.SemaphoreType.DMA((groups, 2, 4, depth)),
            pltpu.SemaphoreType.DMA((groups * (depth + 2) * SENDS,)),
            pltpu.SemaphoreType.DMA((groups,)),
            pltpu.SemaphoreType.DMA((8 * dp,)),
            pltpu.SemaphoreType.DMA((8 * dp,)),
            pltpu.SemaphoreType.DMA((2,)),
            pltpu.SemaphoreType.DMA((len(late),)),
            pltpu.SemaphoreType.DMA((2,)),
        ],
        compiler_params=pltpu.CompilerParams(
            collective_id=collective_id, has_side_effects=True, vmem_limit_bytes=60 * 1024 * 1024
        ),
        name="gather_weights",
    )(wa, wf, *small, patches, *tables)


TOP = 32766.0
RING = 14
BETWEEN = (0, 12, 20, 28, 36)
ORDER = (
    (0, 0, 0), (0, 0, 2), (0, 0, 1), (0, 2, 0), (0, 0, 3), (1, 0, 0), (0, 2, 2), (2, 0, 3), (1, 0, 1), (0, 2, 1),
    (0, 1, 0), (1, 1, 0), (1, 1, 1), (1, 2, 0), (2, 0, 0), (1, 2, 1), (1, 0, 2), (0, 1, 2), (2, 1, 1), (0, 1, 1),
    (1, 0, 3), (1, 3, 1), (1, 2, 2), (2, 0, 1), (1, 1, 2), (0, 3, 0), (2, 1, 0), (2, 1, 3), (0, 1, 3), (2, 0, 2),
    (0, 3, 1), (0, 3, 2), (2, 2, 0), (1, 2, 3), (2, 2, 1), (1, 3, 0), (2, 1, 2), (2, 2, 2), (1, 3, 2), (0, 2, 3),
    (2, 2, 3), (2, 3, 0), (2, 3, 1), (1, 1, 3), (2, 3, 2), (0, 3, 3), (1, 3, 3), (2, 3, 3),
)


def lookup(values, base, t):
    digits = {4: 15, 64: 5}[base]
    words = [
        sum(v * base**i for i, v in enumerate(values[at : at + digits])) for at in range(0, len(values), digits)
    ]
    word = functools.reduce(lambda a, iw: jnp.where(t // digits == iw[0], iw[1], a), enumerate(words), 0)
    unit = functools.reduce(lambda a, i: jnp.where(t % digits == i, base**i, a), range(digits), 1)
    return word // unit % base


def encode(value):
    peak = jnp.maximum(jnp.max(jnp.abs(value), 0, keepdims=True), 1e-30)
    return jnp.round(value * (TOP / peak)).astype(jnp.int32).astype(jnp.int16), peak * (1.0 / TOP)


def decode(code, unit):
    return code.astype(jnp.int32).astype(F32) * unit


def weight_grad_kernel(
    depth, widths, mp_count, at_ref, pt_ref, mt_ref, ot_ref, ya_ref, yf_ref, gmod_ref, mod_ref, t2_ref, cond_ref, pre_ref,
    out_ref, vec_ref,
    x_all, ya_all, yf_all, work, q_send, u_send, q_recv, u_recv,
    gmod, panel, panel_f, scaled_send, scaled_recv, joined, own_vec, hid_part, vec_buf,
    moves, swaps, landing, send, recv, panel_sem, little_send, little_recv,
):
    z, x, y, c, first, second = coordinates()
    dp_count = 2 * depth
    peers_greet(dp_count, mp_count)
    rows = out_ref.shape[1]
    x_refs = (at_ref, pt_ref, mt_ref, ot_ref)
    tokens = at_ref.shape[1]
    width_a, width_f = widths
    here = (x, y)
    corner = (first[0] + second[0] - x, first[1] + second[1] - y)
    mate = (z * 2 + x, y * 2 + 1 - c)
    total = len(ORDER)

    own, theirs = pl.ds(0, tokens), pl.ds(tokens, tokens)
    local, remote = [], []

    def trade(mine, give, to, land):
        n = len(local)
        remote.append(pltpu.make_async_remote_copy(
            src_ref=give, dst_ref=land, send_sem=swaps.at[n], recv_sem=landing.at[n],
            device_id=mate, device_id_type=MESH,
        ))
        local.append(pltpu.make_async_copy(mine, to, moves.at[n]))
        remote[-1].start()
        local[-1].start()

    def trade_x(i):
        trade(x_refs[i], x_refs[i], x_all.at[i, :, own], x_all.at[i, :, theirs])

    def trade_y(ref, full, j):
        trade(ref.at[2 * j + c], ref.at[2 * j + 1 - c], full.at[j, own, :], full.at[j, theirs, :])

    trade_x(2)
    for columns in (pl.ds(0, STEP), pl.ds(STEP, STEP)):
        j = 1 - y
        trade(
            yf_ref.at[2 * j + c, :, columns], yf_ref.at[2 * j + 1 - c, :, columns],
            yf_all.at[j, own, columns], yf_all.at[j, theirs, columns],
        )
    trade_x(3)
    trade_x(0)
    trade_x(1)
    trade_y(ya_ref, ya_all, 1 - y)
    trade_y(yf_ref, yf_all, y)
    trade_y(ya_ref, ya_all, y)
    waits, known = [], set()
    for t, (g, kind, _) in enumerate(ORDER):
        need = [{0, 1}, {0, 2, 3}, {4, 5, 6}][g] | (set() if kind == 0 else {8} if g == 2 else {7})
        if need - known:
            waits.append((t, sorted(need - known)))
            known |= need

    def ready(numbers):
        for n in numbers:
            local[n].wait()
            remote[n].wait_recv()

    codes = tuple(16 * g + 4 * kind + j for g, kind, j in ORDER)

    def plan(t):
        code = lookup(codes, 64, t)
        g, kind, j = code // 16, code // 4 % 4, code % 4
        falling = jnp.where(depth - 1 - j <= z, depth - 2 - j, depth - 1 - j)
        rising = jnp.where(j >= z, j + 1, j)
        zz = jnp.where(z * 2 < depth, falling, rising)
        zz = jnp.where(j == depth - 1, z, zz)
        pick = lambda i: jnp.where(
            kind == 0, corner[i], jnp.where(kind == 1, second[i], jnp.where(kind == 2, first[i], here[i]))
        )
        return g, kind, zz, pick(0), pick(1)

    def product(g, zz, xx, yy):
        cut = pl.ds((zz * 2 + xx) * rows, rows)

        @pl.when(g == 0)
        def _():
            work[...] = dot(x_all[2, cut, :], yf_all[yy, :, :STEP])

        @pl.when(g == 1)
        def _():
            middle = 2 * width_f - STEP
            work[:, :middle] = dot(x_all[2, cut, :], yf_all[yy, :, STEP : 2 * width_f])
            work[:, middle:] = dot(x_all[3, cut, :], yf_all[yy, :, 2 * width_f :])

        @pl.when(g == 2)
        def _():
            edge = 3 * width_a
            low, high = edge // 128 * 128, -(-edge // 128) * 128
            left = dot(x_all[0, cut, :], ya_all[yy, :, :high])
            right = dot(x_all[1, cut, :], ya_all[yy, :, low:])
            lane = lax.broadcasted_iota(jnp.int32, (rows, high - low), 1)
            work[:, :low] = left[:, :low]
            work[:, low:high] = jnp.where(lane < edge - low, left[:, low:], right[:, : high - low])
            work[:, high:] = right[:, high - low :]

    def sent(slot):
        return (
            pltpu.make_async_copy(q_send.at[slot], q_send.at[slot], send.at[0, slot]),
            pltpu.make_async_copy(u_send.at[slot], u_send.at[slot], send.at[1, slot]),
        )

    def ship(t, g, dst_slot, target):
        slot = t % RING

        @pl.when(t >= RING)
        def _():
            for move in sent(slot):
                move.wait()

        code, unit = encode(work[...])
        q_send[slot] = code
        u_send[slot] = unit
        for i, (a, b) in enumerate(((q_send, q_recv), (u_send, u_recv))):
            pltpu.make_async_remote_copy(
                src_ref=a.at[slot], dst_ref=b.at[g, dst_slot],
                send_sem=send.at[i, slot], recv_sem=recv.at[i, g, dst_slot],
                device_id=target, device_id_type=MESH,
            ).start()

    def landed(g, slot):
        pltpu.make_async_copy(q_recv.at[g, slot], q_recv.at[g, slot], recv.at[0, g, slot]).wait()
        pltpu.make_async_copy(u_recv.at[g, slot], u_recv.at[g, slot], recv.at[1, g, slot]).wait()
        work[...] += decode(q_recv[g, slot], u_recv[g, slot])

    dp, mp = lax.axis_index("dp"), lax.axis_index("mp")
    bases = iter(range(0, 64 * dp_count, dp_count))
    little = lambda axis, count, source, target: Round(
        axis, count, source, target, little_send, little_recv, next(bases)
    )
    own_slot = lambda buf, me: lambda peer: buf.at[me]
    gmod_a = little("dp", dp_count, own_slot(gmod, dp), gmod)
    scaled_r = little("dp", dp_count, lambda peer: scaled_send.at[peer], scaled_recv)
    vec_m = little("mp", mp_count, own_slot(own_vec, mp), own_vec)
    hid_r = little("mp", mp_count, own_slot(hid_part, mp), hid_part)
    vec_a = little("dp", dp_count, own_slot(vec_buf, dp), vec_buf)
    lines = gmod_ref.shape[0]
    images = lines // 8

    def panels(count, source, use, hold):
        fetch = lambda i: pltpu.make_async_copy(source(i), hold.at[i % 2], panel_sem.at[i % 2])
        fetch(0).start()
        for i in range(count):
            if i + 1 < count:
                fetch(i + 1).start()
            fetch(i).wait()
            use(i, hold.at[i % 2])

    def one_hot(shape, hit):
        row, col = (lax.broadcasted_iota(jnp.int32, shape, i) for i in range(2))
        return hit(row, col).astype(F32).astype(LOW)

    def begin():
        gmod[dp] = gmod_ref[...]
        gmod_a.push()

    def scaled_grad():
        gmod_a.wait()
        every = gmod[...].reshape(dp_count * lines, D)
        scaled_send[...] = jnp.zeros(scaled_send.shape, F32)

        def use(j, piece):
            hit = lambda r, q: (r // 8 == q // lines) & (q % lines == j * images + r % 8) & (r % 8 < images)
            part = dot(one_hot((8 * dp_count, dp_count * lines), hit), every).astype(LOW)
            scaled_send[...] += dot_nt(part, piece[...].astype(LOW)).reshape(scaled_send.shape)

        panels(8, lambda j: mod_ref.at[:, pl.ds(j * D, D)], use, panel_f)
        scaled_recv[dp] = scaled_send[dp]
        scaled_r.push()

    def vector_grad():
        scaled_r.wait()
        for d in range(dp_count):
            joined[:, d * rows : (d + 1) * rows] = scaled_recv[d]
        own_vec[mp] = (joined[...] * silu_slope(cond_ref[mp])).astype(LOW).astype(F32)
        vec_m.push()

    def hidden_grad():
        vec_m.wait()
        vectors = own_vec[...].reshape(8 * mp_count, D).astype(LOW)
        def use(i, piece):
            hid_part[mp, :, i * rows : (i + 1) * rows] = dot_nt(vectors, piece[...])

        panels(D // rows, lambda i: t2_ref.at[pl.ds(i * rows, rows), :], use, panel)
        hid_r.push()

    def first_grad():
        hid_r.wait()
        grad = functools.reduce(lambda a, b: a + b, [hid_part[i] for i in range(mp_count)])
        grad_pre = (grad * silu_slope(pre_ref[...])).astype(LOW)
        vectors = own_vec[...].reshape(8 * mp_count, D).astype(LOW)
        hit = lambda r, q: (r // images == q // 8) & (r % images == q % 8)
        pick = one_hot((images * mp_count, 8 * mp_count), hit)
        count = images * mp_count
        vec_buf[dp, :count, :] = dot(pick, vectors).astype(LOW)
        vec_buf[dp, count:, :] = dot(pick, grad_pre).astype(LOW)
        vec_a.push()

    hooks = tuple(zip(BETWEEN, (begin, scaled_grad, vector_grad, hidden_grad, first_grad), strict=True))

    to_second = (z * 2 + second[0], second[1] * 2 + c)
    to_first = (z * 2 + first[0], first[1] * 2 + c)
    to_up = ((z + 1) * 2 + x, y * 2 + c)
    to_down = ((z - 1) * 2 + x, y * 2 + c)
    kept, passed = 2 * depth, 3 * depth + 1
    after_line = passed + depth + 1

    def step(t, _):
        g, kind, zz, xx, yy = plan(t)
        for at, numbers in waits:
            pl.when(t == at)(functools.partial(ready, numbers))
        for at, hook in hooks:
            pl.when(t == at)(hook)
        product(g, zz, xx, yy)
        line_first = g < 2
        late, mine = kind >= 2, zz == z
        along = late & ((kind == 3) | line_first)
        line = jnp.where(kind == 3, kept, passed)

        @pl.when(kind < 2)
        def _():
            ship(t, g, kind * depth + zz, to_second)

        @pl.when(late)
        def _():
            landed(g, (kind - 2) * depth + zz)

        @pl.when((kind == 3) & (jnp.logical_not(line_first) | mine))
        def _():
            landed(g, jnp.where(line_first, after_line, passed + zz))

        @pl.when(along & (zz >= z) & (z > 0))
        def _():
            landed(g, line + zz)

        @pl.when(along & (zz <= z) & (z < depth - 1))
        def _():
            landed(g, line + jnp.where(mine, depth, zz))

        @pl.when(along & (zz > z))
        def _():
            ship(t, g, line + zz, to_up)

        @pl.when(along & (zz < z))
        def _():
            ship(t, g, line + jnp.where(zz == z - 1, depth, zz), to_down)

        @pl.when((kind == 2) & (jnp.logical_not(line_first) | mine))
        def _():
            ship(t, g, jnp.where(line_first, after_line, passed + zz), to_first)

        @pl.when((kind == 3) & mine)
        def _():
            out_ref[g] = work[...]

        return 0

    lax.fori_loop(0, total, step, 0)

    def drain(slot, _):
        for move in sent(slot):
            move.wait()
        return 0

    lax.fori_loop(0, RING, drain, 0)
    for move in remote:
        move.wait_send()
    vec_a.wait()
    vec_ref[...] = vec_buf[...]
    for one in (gmod_a, scaled_r, vec_m, hid_r, vec_a):
        one.finish()


def weight_grads(turned, ya, yf, grad_mod, mod_rows, second, cond, pre, dp, collective_id=1):
    depth, mp = dp // 2, ya.shape[0]
    tokens = turned[0].shape[1]
    rows = D // dp
    slots = 4 * depth + 3
    images = grad_mod.shape[0] // 8
    hbm, vmem = pl.BlockSpec(memory_space=pl.ANY), pl.BlockSpec(memory_space=pltpu.VMEM)
    vectors = (dp, 2 * images * mp, D)
    return pl.pallas_call(
        functools.partial(weight_grad_kernel, depth, (ya.shape[2] // 4, yf.shape[2] // 3), mp),
        out_shape=[jax.ShapeDtypeStruct((3, rows, STEP), F32), jax.ShapeDtypeStruct(vectors, LOW)],
        in_specs=[hbm] * 6 + [vmem, hbm, hbm, vmem, vmem],
        out_specs=[vmem, vmem],
        scratch_shapes=[
            pltpu.VMEM((4, D, 2 * tokens), LOW),
            pltpu.VMEM((2, 2 * tokens, ya.shape[2]), LOW),
            pltpu.VMEM((2, 2 * tokens, yf.shape[2]), LOW),
            pltpu.VMEM((rows, STEP), F32),
            pltpu.VMEM((RING, rows, STEP), jnp.int16),
            pltpu.VMEM((RING, 1, STEP), F32),
            pltpu.VMEM((3, slots, rows, STEP), jnp.int16),
            pltpu.VMEM((3, slots, 1, STEP), F32),
            pltpu.VMEM((dp, *grad_mod.shape), LOW),
            pltpu.VMEM((2, rows, D), LOW),
            pltpu.VMEM((2, rows, D), F32),
            pltpu.VMEM((dp, 8, rows), F32),
            pltpu.VMEM((dp, 8, rows), F32),
            pltpu.VMEM((8, D), F32),
            pltpu.VMEM((mp, 8, D), F32),
            pltpu.VMEM((mp, 8 * mp, D), F32),
            pltpu.VMEM(vectors, LOW),
            pltpu.SemaphoreType.DMA((9,)),
            pltpu.SemaphoreType.DMA((9,)),
            pltpu.SemaphoreType.DMA((9,)),
            pltpu.SemaphoreType.DMA((2, RING)),
            pltpu.SemaphoreType.DMA((2, 3, slots)),
            pltpu.SemaphoreType.DMA((2,)),
            pltpu.SemaphoreType.DMA((5 * dp,)),
            pltpu.SemaphoreType.DMA((5 * dp,)),
        ],
        compiler_params=pltpu.CompilerParams(
            collective_id=collective_id, has_side_effects=True, vmem_limit_bytes=62 * 1024 * 1024
        ),
        name="weight_grads",
    )(*turned, ya, yf, grad_mod, mod_rows, second, cond, pre)


def sum_kernel(mp_count, dp_count, in_ref, out_ref, over_dp, over_mp, send, recv):
    dp, mp = lax.axis_index("dp"), lax.axis_index("mp")
    peers_greet(dp_count, mp_count)
    first = Round("dp", dp_count, lambda peer: over_dp.at[dp], over_dp, send, recv, 0)
    second = Round("mp", mp_count, lambda peer: over_mp.at[mp], over_mp, send, recv, dp_count)
    over_dp[dp] = in_ref[...]
    first.push()
    first.wait()
    over_mp[mp] = functools.reduce(lambda a, b: a + b, [over_dp[i] for i in range(dp_count)])
    second.push()
    second.wait()
    out_ref[...] = functools.reduce(lambda a, b: a + b, [over_mp[i] for i in range(mp_count)])
    first.finish()
    second.finish()


def sum_pallas(values, dp, mp, collective_id=2):
    return pl.pallas_call(
        functools.partial(sum_kernel, mp, dp),
        out_shape=jax.ShapeDtypeStruct(values.shape, F32),
        in_specs=[pl.BlockSpec(memory_space=pltpu.VMEM)],
        out_specs=pl.BlockSpec(memory_space=pltpu.VMEM),
        scratch_shapes=[
            pltpu.VMEM((dp, *values.shape), F32), pltpu.VMEM((mp, *values.shape), F32),
            pltpu.SemaphoreType.DMA((dp + mp,)), pltpu.SemaphoreType.DMA((dp + mp,)),
        ],
        compiler_params=pltpu.CompilerParams(collective_id=collective_id, has_side_effects=True),
        name="sum_scalars",
    )(values)


SLAB = 64
VMEM_LIMIT = 60 * 1024 * 1024


def whole(shape):
    return pl.BlockSpec(shape, lambda m: (0,) * len(shape), pipeline_mode=pl.Buffered(1))


def by_block(*shape):
    return pl.BlockSpec((1, *shape), lambda m: (m,) + (0,) * len(shape))


def dot(left, right):
    return lax.dot_general(left, right, (((1,), (0,)), ((), ())), preferred_element_type=F32)


def dot_nt(left, right):
    return lax.dot_general(left, right, (((1,), (1,)), ((), ())), preferred_element_type=F32)


def dot_tn(left, right):
    return lax.dot_general(left, right, (((0,), (0,)), ((), ())), preferred_element_type=F32)


def slabs(tokens, body, sums=0):
    totals = []
    for block in range(tokens // PAIR):

        def step(i, carry, block=block):
            rows = pl.ds(pl.multiple_of(block * PAIR + i * SLAB, SLAB), SLAB)
            lead, values = body(block, rows)
            head, rest = carry
            head = tuple(h + jnp.sum(jnp.where(lead, v, 0.0), 0, keepdims=True) for h, v in zip(head, values))
            rest = tuple(r + jnp.sum(jnp.where(lead, 0.0, v), 0, keepdims=True) for r, v in zip(rest, values))
            return head, rest

        zero = tuple(jnp.zeros((1, D), F32) for _ in range(sums))
        totals.extend(lax.fori_loop(0, PAIR // SLAB, step, (zero, zero)))
    return totals


def spread(mod_ref, j, block, lead):
    row = lambda i: mod_ref[2 * block + i : 2 * block + i + 1, j * D : (j + 1) * D]
    return jnp.where(lead, row(0), row(1))


def turn(values, cos_row, sin_row, direction):
    quarter = HD // 4
    width = values.shape[1]
    lane = lax.broadcasted_iota(jnp.int32, values.shape, 1)
    ahead = pltpu.roll(values, width - quarter, 1)
    behind = pltpu.roll(values, quarter, 1)
    partner = jnp.where(lane % (2 * quarter) < quarter, ahead, behind)
    return values * cos_row + partner * (sin_row * direction)


def same_image(even_col, even_row, block):
    rows = slice(block * PAIR, (block + 1) * PAIR)
    return even_col[rows, :1] == even_row[block, :1, :]


def softmax(query, key, same):
    scores = jnp.where(same, dot_nt(key, query) * (HD ** (-0.5) * math.log2(math.e)), -1e30)
    expo = jnp.exp2(scores - jnp.max(scores, 0, keepdims=True))
    return expo * (1.0 / jnp.sum(expo, 0, keepdims=True))


def attn_begin(patch_ref, patch_rows, patch_bias, mod_ref, col_ref, x0_ref, a_ref, at_ref):
    x0_ref[...] = dot_tn(patch_ref[...], patch_rows) + patch_bias

    def body(block, rows):
        lead = col_ref[rows, :1] != 0
        normed, _ = layer_norm(x0_ref[rows, :])
        shift, scale = spread(mod_ref, 0, block, lead), spread(mod_ref, 1, block, lead)
        a_ref[rows, :] = (normed * (1.0 + scale) + shift).astype(LOW)
        return lead, ()

    slabs(a_ref.shape[0], body)
    at_ref[...] = a_ref[...].T


def attn_block(w_ref, cos_ref, sin_ref, col_ref, row_ref, a_ref, qkv_ref, att_ref, keep):
    tokens, width = att_ref.shape
    made = dot(a_ref[...], w_ref[:, : 3 * width])
    qkv_ref[:, : 2 * width] = turn(made[:, : 2 * width], cos_ref[...], sin_ref[...], 1.0).astype(LOW)
    qkv_ref[:, 2 * width :] = made[:, 2 * width :].astype(LOW)
    for block in range(tokens // PAIR):
        same = same_image(col_ref, row_ref, block)
        rows = slice(block * PAIR, (block + 1) * PAIR)
        for head in range(width // HD):
            take = lambda i: qkv_ref[rows, i * width + head * HD : i * width + (head + 1) * HD]
            probs = softmax(take(0), take(1), same)
            keep(block * (width // HD) + head, probs)
            att_ref[rows, head * HD : (head + 1) * HD] = dot_tn(probs.astype(LOW), take(2)).astype(LOW)
    return dot_nt(att_ref[...], w_ref[:, 3 * width :])


def attn_end(mod_ref, col_ref, x0_ref, proj_ref, x1_ref, m_ref, mt_ref):
    def body(block, rows):
        lead = col_ref[rows, :1] != 0
        x_one = x0_ref[rows, :] + spread(mod_ref, 2, block, lead) * proj_ref[rows, :]
        x1_ref[rows, :] = x_one
        normed, _ = layer_norm(x_one)
        shift, scale = spread(mod_ref, 3, block, lead), spread(mod_ref, 4, block, lead)
        m_ref[rows, :] = (normed * (1.0 + scale) + shift).astype(LOW)
        return lead, ()

    slabs(m_ref.shape[0], body)
    mt_ref[...] = m_ref[...].T


def attn_forward_kernel(
    patch_ref, prow_ref, pbias_ref, mod_ref, w_ref, cos_ref, sin_ref, col_ref, row_ref,
    x0_ref, x1_ref, proj_ref, m_ref, at_ref, mt_ref, qkv_ref, att_ref, probs_ref, a_ref,
):
    step, last = pl.program_id(0), pl.num_programs(0) - 1

    @pl.when(step == 0)
    def _():
        attn_begin(patch_ref, prow_ref[...], pbias_ref[...], mod_ref, col_ref, x0_ref, a_ref, at_ref)
        proj_ref[...] = jnp.zeros(proj_ref.shape, F32)

    def keep(i, probs):
        probs_ref[0, i] = probs

    proj_ref[...] += attn_block(
        w_ref.at[0], cos_ref, sin_ref, col_ref, row_ref, a_ref, qkv_ref.at[0], att_ref.at[0], keep
    )

    @pl.when(step == last)
    def _():
        attn_end(mod_ref, col_ref, x0_ref, proj_ref, x1_ref, m_ref, mt_ref)


def attn_forward(patches, patch_rows, patch_bias, modulation, wa_all, tables):
    blocks, _, width = wa_all.shape
    width //= 4
    tokens = patches.shape[1]
    full, turned = (tokens, D), (D, tokens)
    ins = (patches, patch_rows, patch_bias, modulation)
    return pl.pallas_call(
        attn_forward_kernel,
        grid=(blocks,),
        out_shape=[jax.ShapeDtypeStruct(full, F32)] * 3
        + [jax.ShapeDtypeStruct(full, LOW)]
        + [jax.ShapeDtypeStruct(turned, LOW)] * 2
        + [
            jax.ShapeDtypeStruct((blocks, tokens, 3 * width), LOW),
            jax.ShapeDtypeStruct((blocks, tokens, width), LOW),
            jax.ShapeDtypeStruct((blocks, tokens // PAIR * (width // HD), PAIR, PAIR), F32),
        ],
        in_specs=[whole(a.shape) for a in ins] + [by_block(D, 4 * width)] + [whole(a.shape) for a in tables],
        out_specs=[whole(full)] * 4
        + [whole(turned)] * 2
        + [by_block(tokens, 3 * width), by_block(tokens, width)]
        + [by_block(tokens // PAIR * (width // HD), PAIR, PAIR)],
        scratch_shapes=[pltpu.VMEM(full, LOW)],
        compiler_params=pltpu.CompilerParams(vmem_limit_bytes=VMEM_LIMIT),
        name="attn_forward",
    )(*ins, wa_all, *tables)


PARTS = 1


def units(part, width):
    size = width // PARTS
    return slice(part * size, (part + 1) * size), slice(width + part * size, width + (part + 1) * size)


def ffn_kernel(
    m_ref, x1_ref, proj_ref, mod_ref, head_ref, target_ref, weight_ref, col_ref, w_ref,
    yf_ref, gx1_ref, gp_ref, gpt_ref, gmot_ref, ghead_ref, loss_ref, sums_ref,
    gu_ref, out_ref, back_ref, low_ref,
):
    width = gu_ref.shape[2] // 2
    tokens = m_ref.shape[0]
    step, count = pl.program_id(0), pl.num_programs(0) // 2

    @pl.when(step == 0)
    def _():
        out_ref[...] = jnp.zeros(out_ref.shape, F32)

    @pl.when(step == count)
    def _():
        back_ref[...] = jnp.zeros(back_ref.shape, F32)

    @pl.when(step < count)
    def _():
        for part in range(PARTS):
            own, other = units(part, width)
            gate, up_val = dot(m_ref[...], w_ref[0, :, own]), dot(m_ref[...], w_ref[0, :, other])
            gu_ref[step, :, own] = gate
            gu_ref[step, :, other] = up_val
            hidden = (gate * lax.logistic(gate) * up_val).astype(LOW)
            last = slice(other.start + width, other.stop + width)
            out_ref[...] += dot_nt(hidden, w_ref[0, :, last])

    @pl.when(step == count - 1)
    def _():
        def final_norm(block, rows):
            lead = col_ref[rows, :1] != 0
            x_two = x1_ref[rows, :] + spread(mod_ref, 5, block, lead) * out_ref[rows, :]
            return lead, spread(mod_ref, 7, block, lead), *layer_norm(x_two)

        def before(block, rows):
            lead, scale, normed, _ = final_norm(block, rows)
            low_ref[rows, :] = (normed * (1.0 + scale) + spread(mod_ref, 6, block, lead)).astype(LOW)
            return lead, ()

        slabs(tokens, before)
        diff = dot_nt(head_ref[...], low_ref[...]) - target_ref[...]
        loss = jnp.sum(weight_ref[:1, :] * jnp.mean(diff * diff, 0, keepdims=True), 1, keepdims=True)
        loss_ref[...] = jnp.broadcast_to(loss, loss_ref.shape)
        grad_pred = (2.0 / OUT * diff * weight_ref[1:2, :]).astype(LOW)
        ghead_ref[...] = dot(grad_pred, low_ref[...])
        back_ref[...] = dot_tn(grad_pred, head_ref[...])

        def after(block, rows):
            lead, scale, normed, inv_std = final_norm(block, rows)
            grad_f = back_ref[rows, :]
            grad_x2 = norm_back(grad_f, normed, inv_std, scale)
            gx1_ref[rows, :] = grad_x2
            low_ref[rows, :] = (spread(mod_ref, 5, block, lead) * grad_x2).astype(LOW)
            return lead, (grad_f, grad_f * normed, grad_x2 * out_ref[rows, :])

        for image, rows in enumerate(slabs(tokens, after, 3)):
            for k in range(3):
                sums_ref[k, image : image + 1, :] = rows[k]
        gmot_ref[...] = low_ref[...].T

    @pl.when(step >= count)
    def _():
        for part in range(PARTS):
            own, other = units(part, width)
            last = slice(other.start + width, other.stop + width)
            grad_hid = dot(low_ref[...], w_ref[0, :, last])
            back = 2 * count - 1 - step
            gate, up_val = gu_ref[back, :, own], gu_ref[back, :, other]
            sigma = lax.logistic(gate)
            act = gate * sigma
            slope = sigma * (1.0 + gate * (1.0 - sigma))
            yf_ref[0, :, own] = (grad_hid * up_val * slope).astype(LOW)
            yf_ref[0, :, other] = (grad_hid * act).astype(LOW)
            yf_ref[0, :, last] = (act * up_val).astype(LOW)
        back_ref[...] += dot_nt(yf_ref[0, :, : 2 * width], w_ref[0, :, : 2 * width])

    @pl.when(step == 2 * count - 1)
    def _():
        def body(block, rows):
            lead = col_ref[rows, :1] != 0
            grad_m = back_ref[rows, :]
            normed, inv_std = layer_norm(x1_ref[rows, :])
            grad_x1 = gx1_ref[rows, :] + norm_back(grad_m, normed, inv_std, spread(mod_ref, 4, block, lead))
            gx1_ref[rows, :] = grad_x1
            gp_ref[rows, :] = (spread(mod_ref, 2, block, lead) * grad_x1).astype(LOW)
            return lead, (grad_m, grad_m * normed, grad_x1 * proj_ref[rows, :])

        for image, rows in enumerate(slabs(tokens, body, 3)):
            for k in range(3):
                sums_ref[3 + k, image : image + 1, :] = rows[k]
        gpt_ref[...] = gp_ref[...].T


def ffn(m_in, x_one, proj, modulation, head_rows, target, weights, even_col, wf_all):
    blocks, _, width = wf_all.shape
    width //= 3
    tokens = m_in.shape[0]
    full, turned = (tokens, D), (D, tokens)
    ins = (m_in, x_one, proj, modulation, head_rows, target, weights, even_col)
    there_and_back = lambda i: (jnp.where(i < blocks, i, 2 * blocks - 1 - i), 0, 0)
    back = lambda i: (jnp.where(i < blocks, blocks - 1, 2 * blocks - 1 - i), 0, 0)
    outs = [
        (full, F32), (full, LOW), (turned, LOW), (turned, LOW),
        ((OUT, D), F32), ((8, 128), F32), ((6, modulation.shape[0], D), F32),
    ]
    return pl.pallas_call(
        ffn_kernel,
        grid=(2 * blocks,),
        out_shape=[jax.ShapeDtypeStruct((blocks, tokens, 3 * width), LOW)]
        + [jax.ShapeDtypeStruct(*o) for o in outs],
        in_specs=[whole(a.shape) for a in ins] + [pl.BlockSpec((1, D, 3 * width), there_and_back)],
        out_specs=[pl.BlockSpec((1, tokens, 3 * width), back)] + [whole(o[0]) for o in outs],
        scratch_shapes=[
            pltpu.VMEM((blocks, tokens, 2 * width), F32),
            pltpu.VMEM(full, F32), pltpu.VMEM(full, F32), pltpu.VMEM(full, LOW),
        ],
        compiler_params=pltpu.CompilerParams(vmem_limit_bytes=VMEM_LIMIT),
        name="feed_forward",
    )(*ins, wf_all)


def attn_backward_kernel(
    grad_ref, gx1_ref, x0_ref, patch_ref, mod_ref, w_ref, qkv_ref, att_ref, probs_ref, cos_ref, sin_ref, col_ref, row_ref,
    out_ref, rows_ref, sums_ref, tmp_ref, back_att, back_ref, low_ref,
):
    width = att_ref.shape[2]
    tokens = grad_ref.shape[0]
    scale = HD ** (-0.5)
    step, last = pl.program_id(0), pl.num_programs(0) - 1
    back_att[...] = dot(grad_ref[...], w_ref[0, :, 3 * width :]).astype(LOW)
    for block in range(tokens // PAIR):
        rows = slice(block * PAIR, (block + 1) * PAIR)
        for head in range(width // HD):
            lanes = lambda i: slice(i * width + head * HD, i * width + (head + 1) * HD)
            query, key, value = (qkv_ref[0, rows, lanes(i)] for i in range(3))
            grad = back_att[rows, lanes(0)]
            probs = probs_ref[0, block * (width // HD) + head]
            grad_p = dot_nt(value, grad)
            centre = jnp.sum(probs * grad_p, 0, keepdims=True)
            grad_s = (probs * (grad_p - centre)).astype(LOW)
            tmp_ref[rows, lanes(0)] = dot_tn(grad_s, key) * scale
            tmp_ref[rows, lanes(1)] = dot(grad_s, query) * scale
            tmp_ref[rows, lanes(2)] = dot(probs.astype(LOW), grad)
    out_ref[0, :, : 2 * width] = turn(tmp_ref[:, : 2 * width], cos_ref[...], sin_ref[...], -1.0).astype(LOW)
    out_ref[0, :, 2 * width : 3 * width] = tmp_ref[:, 2 * width :].astype(LOW)
    out_ref[0, :, 3 * width :] = att_ref[0]
    part = dot_nt(out_ref[0, :, : 3 * width], w_ref[0, :, : 3 * width])

    @pl.when(step == 0)
    def _():
        back_ref[...] = part

    @pl.when(step > 0)
    def _():
        back_ref[...] += part

    @pl.when(step == last)
    def _():
        def body(block, rows):
            lead = col_ref[rows, :1] != 0
            grad_a = back_ref[rows, :]
            normed, inv_std = layer_norm(x0_ref[rows, :])
            back = norm_back(grad_a, normed, inv_std, spread(mod_ref, 1, block, lead))
            grad_x0 = (gx1_ref[rows, :] + back).astype(LOW)
            low_ref[rows, :] = grad_x0
            return lead, (grad_a, grad_a * normed, grad_x0.astype(F32))

        bias = jnp.zeros((1, D), F32)
        for image, rows in enumerate(slabs(tokens, body, 3)):
            for k in range(2):
                sums_ref[k, image : image + 1, :] = rows[k]
            bias = bias + rows[2]
        rows_ref[:PATCH_IN, :] = dot(patch_ref[...], low_ref[...])
        rows_ref[PATCH_IN : PATCH_IN + 1, :] = bias
        rows_ref[PATCH_IN + 1 :, :] = jnp.zeros((7, D), F32)


def attn_backward(grad_proj, gx1, x_zero, patches, modulation, wa_all, qkv, att, probs, tables):
    blocks, tokens, width = att.shape
    full = (tokens, D)
    ins = (grad_proj, gx1, x_zero, patches, modulation)
    outs = [((PATCH_IN + 8, D), F32), ((2, modulation.shape[0], D), F32)]
    return pl.pallas_call(
        attn_backward_kernel,
        grid=(blocks,),
        out_shape=[jax.ShapeDtypeStruct((blocks, tokens, 4 * width), LOW)]
        + [jax.ShapeDtypeStruct(*o) for o in outs],
        in_specs=[whole(a.shape) for a in ins]
        + [by_block(D, 4 * width), by_block(tokens, 3 * width), by_block(tokens, width), by_block(*probs.shape[1:])]
        + [whole(a.shape) for a in tables],
        out_specs=[by_block(tokens, 4 * width)] + [whole(o[0]) for o in outs],
        scratch_shapes=[
            pltpu.VMEM((tokens, 3 * width), F32), pltpu.VMEM((tokens, width), LOW),
            pltpu.VMEM(full, F32), pltpu.VMEM(full, LOW),
        ],
        compiler_params=pltpu.CompilerParams(vmem_limit_bytes=VMEM_LIMIT),
        name="attn_backward",
    )(*ins, wa_all, qkv, att, probs, *tables)


def gather_library(wa, wf, small):
    dp, mp = lax.axis_size("dp"), lax.axis_size("mp")
    info, embed, first, first_bias, second, part, tail, columns = small
    depth = wa.shape[0]

    def one(w):
        full = lax.all_gather(w, BOTH, axis=0)
        full = full.reshape(dp, mp, *w.shape).transpose(1, 0, 2, 3)
        return full.reshape(mp, dp * w.shape[0], w.shape[1])

    over_dp = lambda v: lax.all_gather(v, "dp", axis=0)
    pre = lax.psum(dot(embed, first) + first_bias, "mp")
    cond = lax.psum(dot(jax.nn.silu(pre).astype(LOW), second) + part, "mp")
    scaled_all = over_dp(jax.nn.silu(cond).astype(LOW))
    scaled = scaled_all.reshape(-1, D)
    mine = lax.dynamic_slice_in_dim(scaled, lax.axis_index("dp") * depth, depth, 1)
    mod = lax.psum_scatter(dot(mine, columns), "dp", scatter_dimension=0, tiled=True)
    over_mp = lambda v: lax.all_gather(v, "mp", axis=0)
    return one(wa), one(wf), over_mp(mod), over_mp(tail), pre, cond, scaled_all, over_dp(info), over_dp(jax.nn.silu(pre).astype(LOW))


def sibling(value):
    mp = lax.axis_size("mp")
    return lax.ppermute(value, "mp", [(i, i + 1 - 2 * (i % 2)) for i in range(mp)])


def vector_grads(grad_mod, mod_rows, second, cond, pre):
    images = grad_mod.shape[0] // 8
    group = lax.all_gather(grad_mod.reshape(8, images, D), "mp", axis=1, tiled=True)
    group = group.transpose(1, 0, 2).reshape(cond.shape[0], 8 * D)
    every = lax.all_gather(group, "dp", axis=0, tiled=True)
    scaled = lax.all_gather(dot_nt(every, mod_rows), "dp", axis=1, tiled=True)
    scaled = lax.dynamic_slice_in_dim(scaled, lax.axis_index("dp") * cond.shape[0], cond.shape[0], 0)
    grad_cond = (scaled * silu_slope(cond)).astype(LOW)
    hidden = lax.psum(dot_nt(grad_cond, second), "mp")
    grad_pre = (hidden * silu_slope(pre)).astype(LOW)
    return lax.all_gather(jnp.concatenate([grad_cond, grad_pre], 0), "dp", axis=0)


def plane_grads(turned, ya, yf):
    dp, mp = lax.axis_size("dp"), lax.axis_size("mp")
    core, place = lax.axis_index("mp") % 2, lax.axis_index("mp") // 2
    x_all = jnp.stack(turned)
    x_two = jnp.concatenate([x_all, sibling(x_all)], 2)
    width_a, width_f = ya.shape[2] // 4, yf.shape[2] // 3

    def halves(values):
        split = values.reshape(mp // 2, 2, *values.shape[1:])
        mine = lax.dynamic_index_in_dim(split, core, 1, False)
        theirs = lax.dynamic_index_in_dim(split, 1 - core, 1, False)
        return jnp.concatenate([mine, sibling(theirs)], 1)

    def product(x, values):
        return jnp.einsum("dt,btn->bdn", x, values, preferred_element_type=F32)

    ya_two, yf_two = halves(ya), halves(yf)
    grad_a = jnp.concatenate(
        [product(x_two[0], ya_two[..., : 3 * width_a]), product(x_two[1], ya_two[..., 3 * width_a :])], 2
    )
    grad_f = jnp.concatenate(
        [product(x_two[2], yf_two[..., : 2 * width_f]), product(x_two[3], yf_two[..., 2 * width_f :])], 2
    )
    grad = jnp.stack([grad_f[..., :STEP], grad_f[..., STEP:], grad_a])
    part = lax.psum_scatter(grad, "dp", scatter_dimension=2, tiled=True)
    total = lax.dynamic_index_in_dim(part, place, 1, False)
    for hop in range(1, mp // 2):
        perm = [(i, (i + 2 * hop) % mp) for i in range(mp)]
        out = lax.dynamic_index_in_dim(part, (place + hop) % (mp // 2), 1, False)
        total = total + lax.ppermute(out, "mp", perm)
    return total


def per_device(
    patches, target, segments, positions, classes, timesteps, t_weight, step_count,
    qkv_w, qkv_m, qkv_v, out_w, out_m, out_v, ffn_in_w, ffn_in_m, ffn_in_v,
    ffn_out_w, ffn_out_m, ffn_out_v, mod_w, mod_m, mod_v, table_w, table_m, table_v,
):
    mp_count, dp_count = lax.axis_size("mp"), lax.axis_size("dp")
    mp_index, dp_index = lax.axis_index("mp"), lax.axis_index("dp")
    tokens = patches.shape[1]
    pairs = tokens // PAIR
    images = 2 * pairs
    own_rows = table_w.shape[0]
    depth = mod_w.shape[0]
    width_a, width_f = qkv_w.shape[2], ffn_in_w.shape[2]

    regular = dp_count == 2 * DEPTH and mp_count == 4
    group_images = classes.shape[0]
    wa = jnp.concatenate([qkv_w[0], qkv_w[1], qkv_w[2], out_w.T], 1).astype(LOW)
    wf = jnp.concatenate([ffn_in_w[0], ffn_in_w[1], ffn_out_w.T], 1).astype(LOW)

    table_b = table_w.astype(LOW)
    gap = D + 16
    padded = lax.dynamic_update_slice(jnp.zeros((2 * gap + own_rows, D), LOW), table_b, (gap, 0))

    def placed(row, count):
        return lax.dynamic_slice_in_dim(padded, row - mp_index * own_rows + gap, count, 0)

    half = FREQ // 2
    freqs = jnp.exp(-math.log(10000.0) * jnp.arange(half, dtype=F32) / half)

    def embedding(times):
        angles = times[:, None] * freqs[None, :]
        return jnp.concatenate([jnp.cos(angles), jnp.sin(angles)], 1).astype(LOW)

    row_ids = mp_index * own_rows + jnp.arange(own_rows, dtype=jnp.int32)
    own_hot = (classes[:, None] == row_ids[None, :]).astype(LOW)
    part = matmul(own_hot, table_b) + placed(ROW_OUT_BIAS, 1).astype(F32)
    info = jnp.zeros((8, 128), F32)
    for i, values in enumerate((classes, timesteps, t_weight)):
        info = info.at[i, :group_images].set(values.astype(F32))
    mod_cols = mod_w.shape[1] // mp_count
    small = (
        info, embedding(timesteps.astype(F32)), placed(ROW_TIME_IN, FREQ),
        placed(ROW_TIME_BIAS, 1).astype(F32), placed(ROW_TIME_OUT, D), part,
        jnp.pad(placed(ROW_PATCH, TAIL), ((0, 64 - TAIL), (0, 0))),
        lax.dynamic_slice_in_dim(mod_w, mp_index * mod_cols, mod_cols, 1).astype(LOW),
    )
    own_seg = lax.dynamic_slice_in_dim(segments, mp_index * tokens, tokens)
    own_pos = lax.dynamic_slice_in_dim(positions, mp_index * tokens, tokens, 1)
    even = (own_seg % 2 == 0).reshape(pairs, PAIR)
    heads = 2 * width_a // HD
    cos_row, sin_row = (jnp.tile(t, (1, heads)) for t in rotary_tables(own_pos))
    even_col = even.astype(jnp.int32).reshape(tokens, 1)
    even_row = jnp.broadcast_to(even.astype(jnp.int32)[:, None], (pairs, 8, PAIR))
    tables = (cos_row, sin_row, even_col, even_row)

    if regular:
        gathered = gather_pallas(wa, wf, small, patches, tables, dp_count, mp_count)
        wa_all, wf_all, modulation, tail, pre, cond, scaled, infos, hidden = gathered[:9]
        x_zero, x_one, proj, m_in, a_turned, m_turned, qkv, att, probs = gathered[9:]
    else:
        wa_all, wf_all, mod_all, tails, pre, cond, scaled, infos, hidden = gather_library(wa, wf, small)
        tail = jnp.sum(tails.astype(F32), 0)
        mod_own = lax.dynamic_slice_in_dim(mod_all, mp_index * images, images, 1)
        mod_bias = tail[ROW_MOD_BIAS - ROW_PATCH : TAIL].reshape(-1)
        modulation = mod_own.transpose(1, 0, 2).reshape(images, -1) + mod_bias
        x_zero, x_one, proj, m_in, a_turned, m_turned, qkv, att, probs = attn_forward(
            patches, tail[:PATCH_IN].astype(LOW), tail[PATCH_IN][None, :], modulation, wa_all, tables
        )
    count_all = dp_count * group_images
    scaled = scaled.reshape(count_all, D)
    classes_all, times_all, weights_all = (infos[:, i, :group_images].reshape(-1) for i in range(3))
    head_rows = tail[PATCH_IN + 1 : PATCH_IN + 1 + OUT].astype(LOW)
    weight_sum = jnp.sum(weights_all)

    ones = jnp.ones((count_all, 1), LOW)
    zeros = lambda n: jnp.zeros((count_all, n), LOW)
    own_cols = lambda a: lax.dynamic_slice_in_dim(a, mp_index * own_rows, own_rows, 1)
    left_pre = own_cols(
        jnp.concatenate([zeros(NCLS), embedding(times_all), ones, zeros(ROWS - ROW_TIME_OUT)], 1)
    )
    class_hot = (classes_all[:, None] == jnp.arange(NCLS, dtype=F32)[None, :]).astype(LOW)
    hidden = hidden.reshape(count_all, D)
    left_cond = own_cols(
        jnp.concatenate(
            [class_hot, zeros(ROW_TIME_OUT - NCLS), hidden, ones, zeros(ROWS - ROW_PATCH)], 1
        )
    )
    own_scaled = lax.dynamic_slice_in_dim(scaled, dp_index * depth, depth, 1)

    first_len = jnp.sum(even.astype(F32), 1)
    own_tw = lax.dynamic_slice_in_dim(t_weight, mp_index * images, images).reshape(pairs, 2)
    per_tok = own_tw / jnp.stack([first_len, PAIR - first_len], 1)
    tok_weight = jnp.where(even, per_tok[:, :1], per_tok[:, 1:]).reshape(1, tokens)
    weights = jnp.concatenate([tok_weight, tok_weight / weight_sum], 0)
    yf, grad_x1, grad_proj, proj_turned, mo_turned, grad_head, loss, sums_f = ffn(
        m_in, x_one, proj, modulation, head_rows, target, weights, even_col, wf_all
    )
    ya, grad_patch, sums_a = attn_backward(
        grad_proj, grad_x1, x_zero, patches, modulation, wa_all, qkv, att, probs, tables
    )
    loss_part = loss[0, 0]
    x_turned = (a_turned, proj_turned, m_turned, mo_turned)
    grad_mod = jnp.concatenate(
        [sums_a[0], sums_a[1], sums_f[5], sums_f[3], sums_f[4], sums_f[2], sums_f[0], sums_f[1]], 0
    ).astype(LOW)
    cond_own = jnp.pad(cond.reshape(mp_count, images, D), ((0, 0), (0, 8 - images), (0, 0)))
    pre_own = jnp.pad(pre.reshape(mp_count, images, D), ((0, 0), (0, 8 - images), (0, 0)))
    if regular:
        summed, vectors = weight_grads(
            x_turned, ya, yf, grad_mod, mod_w, small[4], cond_own, pre_own.reshape(-1, D), dp_count
        )
    else:
        summed = plane_grads(x_turned, ya, yf)
        vectors = vector_grads(grad_mod, mod_w.astype(LOW), small[4], cond, pre)
    own_wf, own_wa = jnp.concatenate([summed[0], summed[1]], 1), summed[2]

    grad_mod_all = lax.all_gather(grad_mod, BOTH, axis=0).reshape(-1, 8, images, D)
    grad_mod_all = grad_mod_all.transpose(0, 2, 1, 3).reshape(count_all, 8 * D)
    grad_mod_w = matmul_tn(own_scaled, grad_mod_all)
    grad_mod_bias = jnp.sum(grad_mod_all.astype(F32), 0).reshape(8, D)
    grad_cvec = vectors[:, :group_images].reshape(count_all, D)
    grad_pre = vectors[:, group_images:].reshape(count_all, D)
    token_rows = jnp.concatenate([grad_patch[: PATCH_IN + 1], grad_head], 0)
    token_rows = jnp.concatenate([lax.psum(token_rows, BOTH), grad_mod_bias], 0)
    blank = -(-own_rows // 8) * 8
    start = jnp.clip(mp_index * own_rows - ROW_PATCH + blank, 0, blank + 64)
    spaced = lax.dynamic_update_slice(jnp.zeros((2 * blank + 64, D), F32), token_rows, (blank, 0))
    tail_own = lax.dynamic_slice_in_dim(spaced, start, own_rows, 0)
    grad_table = matmul_tn(left_cond, grad_cvec) + matmul_tn(left_pre, grad_pre) + tail_own

    grad_qkv = jnp.stack([own_wa[:, j * width_a : (j + 1) * width_a] for j in range(3)])
    grad_out_w = own_wa[:, 3 * width_a :].T
    grad_ffn_in = jnp.stack([own_wf[:, j * width_f : (j + 1) * width_f] for j in range(2)])
    grad_ffn_out = own_wf[:, 2 * width_f :].T
    sharded_sq = jnp.sum(own_wa * own_wa) + jnp.sum(own_wf * own_wf)
    copied_sq = (
        jnp.sum(grad_mod_w * grad_mod_w) / mp_count + jnp.sum(grad_table * grad_table) / dp_count
    )
    scalars = jnp.concatenate(
        [jnp.full((1, 128), sharded_sq + copied_sq), jnp.full((1, 128), loss_part), jnp.zeros((6, 128), F32)], 0
    )
    scalars = sum_pallas(scalars, dp_count, mp_count) if regular else lax.psum(scalars, BOTH)
    square_sum, loss_sum = scalars[0, 0], scalars[1, 0]
    norm = jnp.sqrt(square_sum)
    total_tokens = tokens * mp_count * dp_count
    clip = jnp.minimum(1.0, CLIP_SCALE / math.sqrt(total_tokens) / (norm + 1e-06))
    count = step_count[0].astype(F32)
    results = [(loss_sum / weight_sum).reshape(1), norm.reshape(1)]
    for weight, first, second, grad in (
        (qkv_w, qkv_m, qkv_v, grad_qkv),
        (out_w, out_m, out_v, grad_out_w),
        (ffn_in_w, ffn_in_m, ffn_in_v, grad_ffn_in),
        (ffn_out_w, ffn_out_m, ffn_out_v, grad_ffn_out),
        (mod_w, mod_m, mod_v, grad_mod_w),
        (table_w, table_m, table_v, grad_table),
    ):
        results.extend(adam(weight, first, second, grad * clip, count))
    return tuple(results)


def solution(mesh):
    tok, grp = P(None, BOTH), P("dp")
    cols, rows = P(None, "dp", "mp"), P("mp", "dp")
    weights = (cols,) * 3 + (rows,) * 3 + (cols,) * 3 + (rows,) * 3
    weights += (P("dp", None),) * 3 + (P("mp", None),) * 3
    in_specs = (tok, tok, grp, P(None, "dp"), grp, grp, grp, P()) + weights
    return jax.shard_map(
        per_device, mesh=mesh, in_specs=in_specs, out_specs=(P(), P()) + weights, check_vma=False
    )
```

```python
import functools
import math

import jax
import jax.numpy as jnp
from jax import lax
from jax.experimental import pallas as pl
from jax.experimental.pallas import tpu as pltpu
from jax.sharding import PartitionSpec as P

D = 1152
HD = 72
PATCH_IN = 16
OUT = 32
FREQ = 256
NCLS = 1001
PAIR = 320

ROW_TIME_IN = NCLS
ROW_TIME_BIAS = ROW_TIME_IN + FREQ
ROW_TIME_OUT = ROW_TIME_BIAS + 1
ROW_OUT_BIAS = ROW_TIME_OUT + D
ROW_PATCH = ROW_OUT_BIAS + 1
ROW_PATCH_BIAS = ROW_PATCH + PATCH_IN
ROW_HEAD = ROW_PATCH_BIAS + 1
ROW_MOD_BIAS = ROW_HEAD + OUT
ROWS = ROW_MOD_BIAS + 8
TAIL = ROWS - ROW_PATCH

EPS_NORM = 1e-06
BETA_ONE = 0.9
BETA_TWO = 0.95
ADAM_EPS = 1e-08
LEARN_RATE = 0.03
WEIGHT_DECAY = 0.1
CLIP_SCALE = 0.5
LOW = jnp.bfloat16
F32 = jnp.float32
BOTH = ("dp", "mp")
MESH = pl.DeviceIdType.MESH
STEP = 1152
HOOKS = (0, 1, 2, 3)
LINE_FIRST = (True, True, False)
BEHIND = (0, 4, 5)
SENDS = 20
DEPTH = 4


def matmul(left, right):
    return jnp.dot(left, right, preferred_element_type=F32)


def matmul_tn(left, right):
    return lax.dot_general(left, right, (((0,), (0,)), ((), ())), preferred_element_type=F32)


def matmul_nt(left, right):
    return lax.dot_general(left, right, (((1,), (1,)), ((), ())), preferred_element_type=F32)


def layer_norm(values):
    centred = values - jnp.mean(values, -1, keepdims=True)
    inv_std = lax.rsqrt(jnp.mean(centred * centred, -1, keepdims=True) + EPS_NORM)
    return (centred * inv_std, inv_std)


def norm_back(grad, normed, inv_std, scale_rows):
    inner = grad * (1.0 + scale_rows)
    return inv_std * (
        inner
        - jnp.mean(inner, -1, keepdims=True)
        - normed * jnp.mean(inner * normed, -1, keepdims=True)
    )


def silu_slope(values):
    sigma = jax.nn.sigmoid(values)
    return sigma * (1.0 + values * (1.0 - sigma))


def adam(weight, first, second, grad, count):
    first = BETA_ONE * first + (1.0 - BETA_ONE) * grad
    second = BETA_TWO * second + (1.0 - BETA_TWO) * grad * grad
    m_hat = first / (1.0 - BETA_ONE**count)
    v_hat = second / (1.0 - BETA_TWO**count)
    weight = weight - LEARN_RATE * (m_hat / (jnp.sqrt(v_hat) + ADAM_EPS) + WEIGHT_DECAY * weight)
    return (weight, first, second)


def rotary_tables(positions):
    quarter = HD // 4
    freqs = jnp.exp(-math.log(10000.0) * jnp.arange(quarter, dtype=F32) / quarter)
    angle = positions.astype(F32)[:, :, None] * freqs[None, None, :]
    cosine, sine = jnp.cos(angle), jnp.sin(angle)
    cos_row = jnp.concatenate([cosine[0], cosine[0], cosine[1], cosine[1]], 1)
    sin_row = jnp.concatenate([-sine[0], sine[0], -sine[1], sine[1]], 1)
    return cos_row, sin_row


def coordinates():
    dp, mp = lax.axis_index("dp"), lax.axis_index("mp")
    z, x = dp // 2, dp % 2
    y, c = mp // 2, mp % 2
    first = (x + (1 - c) * (1 - 2 * x), y + c * (1 - 2 * y))
    second = (x + c * (1 - 2 * x), y + (1 - c) * (1 - 2 * y))
    return z, x, y, c, first, second


def greet(z, x, y, c, first, second, depth):
    barrier = pltpu.get_barrier_semaphore()

    def signal(dp, mp):
        pl.semaphore_signal(barrier, inc=1, device_id=(dp, mp), device_id_type=MESH)

    signal(z * 2 + first[0], first[1] * 2 + c)
    signal(z * 2 + second[0], second[1] * 2 + c)
    signal(z * 2 + x, y * 2 + 1 - c)
    pl.when(z > 0)(lambda: signal((z - 1) * 2 + x, y * 2 + c))
    pl.when(z < depth - 1)(lambda: signal((z + 1) * 2 + x, y * 2 + c))
    peers = 3 + jnp.minimum(z, 1) + jnp.minimum(depth - 1 - z, 1)
    pl.semaphore_wait(barrier, peers)


def peers_greet(dp_count, mp_count):
    dp, mp = lax.axis_index("dp"), lax.axis_index("mp")
    barrier = pltpu.get_barrier_semaphore()
    for hop in range(1, dp_count):
        pl.semaphore_signal(
            barrier, inc=1, device_id=(lax.rem(dp + hop, dp_count), mp), device_id_type=MESH
        )
    for hop in range(1, mp_count):
        pl.semaphore_signal(
            barrier, inc=1, device_id=(dp, lax.rem(mp + hop, mp_count)), device_id_type=MESH
        )
    pl.semaphore_wait(barrier, dp_count + mp_count - 2)


class Round:
    def __init__(self, axis, count, source, target, send, recv, base):
        self.me = lax.axis_index(axis)
        self.axis, self.count, self.source, self.target = axis, count, source, target
        self.send, self.recv, self.base = send, recv, base

    def moves(self):
        for hop in range(1, self.count):
            peer = lax.rem(self.me + hop, self.count)
            other = {"dp": (peer, lax.axis_index("mp")), "mp": (lax.axis_index("dp"), peer)}[self.axis]
            yield pltpu.make_async_remote_copy(
                src_ref=self.source(peer), dst_ref=self.target.at[self.me],
                send_sem=self.send.at[self.base + hop], recv_sem=self.recv.at[self.base + hop],
                device_id=other, device_id_type=MESH,
            )

    def push(self):
        for move in self.moves():
            move.start()

    def wait(self):
        for hop in range(1, self.count):
            slot = self.target.at[lax.rem(self.me + self.count - hop, self.count)]
            pltpu.make_async_copy(slot, slot, self.recv.at[self.base + hop]).wait()

    def finish(self):
        for move in self.moves():
            move.wait_send()


def gather_kernel(
    depth, mp_count, wa_ref, wf_ref, info_ref, emb_ref, t1_ref, b1_ref, t2_ref, part_ref, tail_ref, mcol_ref,
    patch_ref, cos_ref, sin_ref, col_ref, row_ref,
    wa_all, wf_all, mod_ref, tails_ref, pre_ref, cond_ref, scaled_ref, infos_ref, hid_ref,
    x0_out, x1_out, proj_out, m_out, at_out, mt_out, qkv_out, att_out, probs_out,
    info_buf, pre_sum, cond_sum, tail_buf, scaled_buf, hid_buf, mod_part, mod_sum, mod_buf, a_ref, wa_buf,
    x0_ref, x1_ref, proj_ref, m_ref, at_ref, mt_ref, qkv_ref, att_ref, probs_buf,
    recv, send, local, little_recv, little_send, wa_sem, out_sem, probs_sem,
):
    dp_count = 2 * depth
    z, x, y, c, first, second = coordinates()
    dp, mp = lax.axis_index("dp"), lax.axis_index("mp")
    rows = wa_ref.shape[0]
    images = emb_ref.shape[0]
    peers_greet(dp_count, mp_count)

    bases = iter(range(0, 64 * dp_count, dp_count))
    little = lambda axis, count, source, target: Round(
        axis, count, source, target, little_send, little_recv, next(bases)
    )
    own = lambda buf, me: lambda peer: buf.at[me]
    info = little("dp", dp_count, own(info_buf, dp), info_buf)
    pre_r = little("mp", mp_count, own(pre_sum, mp), pre_sum)
    tail_r = little("mp", mp_count, own(tail_buf, mp), tail_buf)
    cond_r = little("mp", mp_count, own(cond_sum, mp), cond_sum)
    scaled_a = little("dp", dp_count, own(scaled_buf, dp), scaled_buf)
    hid_a = little("dp", dp_count, own(hid_buf, dp), hid_buf)
    mod_r = little("dp", dp_count, lambda peer: mod_part.at[peer], mod_sum)
    mod_a = little("mp", mp_count, own(mod_buf, mp), mod_buf)
    rounds = (info, pre_r, tail_r, cond_r, scaled_a, hid_a, mod_r, mod_a)
    total = lambda buf, count: functools.reduce(lambda a, b: a + b, [buf[i] for i in range(count)])

    def begin():
        info_buf[dp] = info_ref[...]
        info.push()
        pre_sum[mp] = dot(emb_ref[...], t1_ref[...]) + b1_ref[...]
        pre_r.push()
        tail_buf[mp] = tail_ref[...]
        tail_r.push()

    def hidden():
        pre_r.wait()
        pre = total(pre_sum, mp_count)
        pre_ref[...] = pre
        act = (pre * lax.logistic(pre)).astype(LOW)
        cond_sum[mp] = dot(act, t2_ref[...]) + part_ref[...]
        cond_r.push()
        hid_buf[dp] = act

    def condition():
        cond_r.wait()
        cond = total(cond_sum, mp_count)
        cond_ref[...] = cond
        scaled_buf[dp] = (cond * lax.logistic(cond)).astype(LOW)
        scaled_a.push()

    def modulate():
        scaled_a.wait()
        scaled = scaled_buf[...].reshape(dp_count * images, D)
        row = lax.broadcasted_iota(jnp.int32, (D, rows), 0)
        col = lax.broadcasted_iota(jnp.int32, (D, rows), 1)
        pick = (row == col + dp * rows).astype(F32).astype(LOW)
        mine = dot(scaled, pick).astype(LOW)
        mod_part[...] = dot(mine, mcol_ref[...]).reshape(mod_part.shape)
        mod_sum[dp] = mod_part[dp]
        mod_r.push()

    def collect():
        mod_r.wait()
        mod_buf[mp] = total(mod_sum, dp_count)
        mod_a.push()
        hid_a.push()

    hooks = (hidden, condition, modulate, collect)

    corner = (first[0] + second[0] - x, first[1] + second[1] - y)
    spots = {"here": (x, y), "first": first, "second": second, "corner": corner}
    ids = {"here": 0, "first": 1, "second": 2, "corner": 3}
    swapped = {"here": 0, "first": 2, "second": 1, "corner": 3}
    groups = [(wa_ref, wa_all, 0, LINE_FIRST[0])]
    groups += [(wf_ref, wf_all, i * STEP, LINE_FIRST[1 + i]) for i in range(wf_ref.shape[1] // STEP)]
    count = len(groups)

    def slot(g, zz, spot, core):
        _, ref, column, _ = groups[g]
        return ref.at[spot[1] * 2 + core, pl.ds((zz * 2 + spot[0]) * rows, rows), pl.ds(column, STEP)]

    def mine(g):
        return groups[g][0].at[:, pl.ds(groups[g][2], STEP)]

    def arrive(g, zz, kind, cond=None, plane=0):
        dst = slot(g, zz, spots[kind], c if plane == 0 else 1 - c)
        sem = recv.at[g, plane, ids[kind] if plane == 0 else swapped[kind], zz]
        wait = pltpu.make_async_copy(dst, dst, sem)
        if cond is None:
            wait.wait()
        else:
            pl.when(cond)(wait.wait)

    def sides(k):
        below, above = jnp.maximum(z - k, 0), jnp.minimum(z + k, depth - 1)
        return ((below, z >= k, "up", z < depth - 1), (above, z < depth - k, "down", z > 0))[: 1 if k == 0 else 2]

    def stage(g, k, live=True):
        line_first = groups[g][3]
        numbers = iter(range((g * (depth + 2) + k) * SENDS, (g * (depth + 2) + k + 1) * SENDS))

        def copy(zz, kind, route, cond=None, own=False):
            plane, sem_kind = 0, kind
            if route == "up":
                target = ((z + 1) * 2 + x, mp)
            elif route == "down":
                target = ((z - 1) * 2 + x, mp)
            elif route == "first":
                target, sem_kind = (z * 2 + first[0], first[1] * 2 + c), "first"
            elif route == "second":
                target = (z * 2 + second[0], second[1] * 2 + c)
                sem_kind = "second" if kind == "here" else "corner"
            else:
                target, plane = (dp, y * 2 + 1 - c), 1
            made = pltpu.make_async_remote_copy(
                src_ref=mine(g) if own else slot(g, zz, spots[kind], c), dst_ref=slot(g, zz, spots[kind], c),
                send_sem=send.at[next(numbers)], recv_sem=recv.at[g, plane, ids[sem_kind], zz],
                device_id=target, device_id_type=MESH,
            )
            act = made.start if live else made.wait_send
            if cond is None:
                act()
            else:
                pl.when(cond)(act)

        def take(zz, kind, cond=None):
            if live:
                arrive(g, zz, kind, cond)

        if k == 0:
            if live:
                pltpu.make_async_copy(mine(g), slot(g, z, spots["here"], c), local.at[g]).start()
            copy(z, "here", "first", None, True)
            copy(z, "here", "up", z < depth - 1, True)
            copy(z, "here", "down", z > 0, True)
            copy(z, "here", "second", None, True)
            copy(z, "here", "core", None, True)
        if k == 1 and not line_first:
            take(z, "first")
            copy(z, "first", "up", z < depth - 1)
            copy(z, "first", "down", z > 0)
            copy(z, "first", "second")
            copy(z, "first", "core")
        if 0 < k < depth:
            for zz, cond, route, more in sides(k):
                take(zz, "here", cond)
                copy(zz, "here", route, cond & more)
                if line_first:
                    copy(zz, "here", "first", cond)
                copy(zz, "here", "second", cond)
                copy(zz, "here", "core", cond)
        if 0 <= k - 1 < depth and (line_first or k > 1):
            for zz, cond, route, more in sides(k - 1):
                take(zz, "first", cond)
                if not line_first:
                    copy(zz, "first", route, cond & more)
                copy(zz, "first", "second", cond)
                copy(zz, "first", "core", cond)
        if 0 <= k - 2 < depth:
            for zz, cond, _, _ in sides(k - 2):
                for kind in ("second", "corner"):
                    take(zz, kind, cond)
                    copy(zz, kind, "core", cond)

    def settle(g):
        for zz in range(depth):
            for kind in ("here", "first", "second", "corner"):
                arrive(g, zz, kind, None, 1)
        pltpu.make_async_copy(mine(g), slot(g, z, spots["here"], c), local.at[g]).wait()

    begin()
    steps = [
        [(g, moment - BEHIND[g]) for g in range(count) if 0 <= moment - BEHIND[g] < depth + 2]
        for moment in range(depth + 2 + max(BEHIND))
    ]
    for moment in range(depth + 2):
        for g, k in steps[moment]:
            stage(g, k)
        for number, hook in enumerate(hooks):
            if HOOKS[number] == moment:
                hook()
    settle(0)
    load = lambda m: pltpu.make_async_copy(wa_all.at[m], wa_buf.at[m % 2], wa_sem.at[m % 2])
    load(0).start()
    mod_a.wait()
    tail_r.wait()
    tails_ref[...] = functools.reduce(lambda a, b: a + b, [tail_buf[i].astype(F32) for i in range(mp_count)])
    own_images = images // mp_count
    width = mcol_ref.shape[1]
    for i in range(mp_count):
        rows_of = lambda m: mod_buf[i, m * own_images : (m + 1) * own_images, :]
        picked = functools.reduce(lambda a, m: jnp.where(mp == m, rows_of(m), a), range(1, mp_count), rows_of(0))
        mod_ref[:, i * width : (i + 1) * width] = picked
    for j in range(8):
        bias = tails_ref[ROW_MOD_BIAS - ROW_PATCH + j : ROW_MOD_BIAS - ROW_PATCH + j + 1, :]
        mod_ref[:, j * D : (j + 1) * D] += bias
    attn_begin(
        patch_ref, tails_ref[:PATCH_IN, :].astype(LOW), tails_ref[PATCH_IN : PATCH_IN + 1, :],
        mod_ref, col_ref, x0_ref, a_ref, at_ref,
    )
    proj_ref[...] = jnp.zeros(proj_ref.shape, F32)

    later = [pair for moment in steps[depth + 2 :] for pair in moment]

    def stored(m, i):
        return pltpu.make_async_copy(probs_buf.at[i % 2], probs_out.at[m, i], probs_sem.at[i % 2])

    def heads(m, _):
        pl.when(m + 1 < mp_count)(lambda: load(m + 1).start())
        load(m).wait()

        def keep(i, probs):
            if i > 1:
                stored(m, i - 2).wait()
            else:
                pl.when(m > 0)(lambda: stored(m - 1, probs_out.shape[1] - 2 + i).wait())
            probs_buf[i % 2] = probs
            stored(m, i).start()

        proj_ref[...] += attn_block(
            wa_buf.at[m % 2], cos_ref, sin_ref, col_ref, row_ref, a_ref, qkv_ref.at[m], att_ref.at[m], keep
        )
        for i in range(mp_count):
            part = later[i * len(later) // mp_count : (i + 1) * len(later) // mp_count]

            @pl.when(m == i)
            def _(part=part):
                for g, k in part:
                    stage(g, k)

        return 0

    lax.fori_loop(0, mp_count, heads, 0)
    for i in range(2):
        stored(mp_count - 1, probs_out.shape[1] - 2 + i).wait()
    hid_a.wait()
    info.wait()
    scaled_ref[...] = scaled_buf[...]
    infos_ref[...] = info_buf[...]
    hid_ref[...] = hid_buf[...]
    attn_end(mod_ref, col_ref, x0_ref, proj_ref, x1_ref, m_ref, mt_ref)
    made = (
        (x0_ref, x0_out), (x1_ref, x1_out), (proj_ref, proj_out), (m_ref, m_out),
        (at_ref, at_out), (mt_ref, mt_out), (qkv_ref, qkv_out), (att_ref, att_out),
    )
    leaving = [pltpu.make_async_copy(a, b, out_sem.at[i]) for i, (a, b) in enumerate(made)]
    for move in leaving:
        move.start()
    for g in range(1, count):
        settle(g)
    for move in leaving:
        move.wait()
    for g in range(count):
        for k in range(depth + 2):
            stage(g, k, False)
    for one in rounds:
        one.finish()


def gather_pallas(wa, wf, small, patches, tables, dp, mp, collective_id=0):
    depth = dp // 2
    groups = 1 + wf.shape[1] // STEP
    images, width = small[1].shape[0], small[7].shape[1]
    tail = small[6].shape[0]
    tokens, heads = patches.shape[1], wa.shape[1] // 4
    full, turned = (tokens, D), (D, tokens)
    shapes = [
        ((images // mp, mp * width), F32), ((tail, D), F32), ((images, D), F32), ((images, D), F32),
        ((dp, images, D), LOW), ((dp, 8, 128), F32), ((dp, images, D), LOW),
    ]
    late = [
        (full, F32), (full, F32), (full, F32), (full, LOW), (turned, LOW), (turned, LOW),
        ((mp, tokens, 3 * heads), LOW), ((mp, tokens, heads), LOW),
    ]
    probs = ((mp, tokens // PAIR * (heads // HD), PAIR, PAIR), F32)
    hbm, vmem = pl.BlockSpec(memory_space=pl.ANY), pl.BlockSpec(memory_space=pltpu.VMEM)
    return pl.pallas_call(
        functools.partial(gather_kernel, depth, mp),
        out_shape=[jax.ShapeDtypeStruct((mp, dp * s.shape[0], s.shape[1]), s.dtype) for s in (wa, wf)]
        + [jax.ShapeDtypeStruct(*s) for s in shapes + late + [probs]],
        in_specs=[hbm] * 2 + [vmem] * 13,
        out_specs=[hbm] * 2 + [vmem] * len(shapes) + [hbm] * (len(late) + 1),
        scratch_shapes=[
            pltpu.VMEM((dp, 8, 128), F32), pltpu.VMEM((mp, images, D), F32), pltpu.VMEM((mp, images, D), F32),
            pltpu.VMEM((mp, tail, D), LOW), pltpu.VMEM((dp, images, D), LOW), pltpu.VMEM((dp, images, D), LOW),
            pltpu.VMEM((dp, images, width), F32), pltpu.VMEM((dp, images, width), F32),
            pltpu.VMEM((mp, images, width), F32),
            pltpu.VMEM(full, LOW), pltpu.VMEM((2, D, wa.shape[1]), LOW),
            *(pltpu.VMEM(*s) for s in late),
            pltpu.VMEM((2, PAIR, PAIR), F32),
            pltpu.SemaphoreType.DMA((groups, 2, 4, depth)),
            pltpu.SemaphoreType.DMA((groups * (depth + 2) * SENDS,)),
            pltpu.SemaphoreType.DMA((groups,)),
            pltpu.SemaphoreType.DMA((8 * dp,)),
            pltpu.SemaphoreType.DMA((8 * dp,)),
            pltpu.SemaphoreType.DMA((2,)),
            pltpu.SemaphoreType.DMA((len(late),)),
            pltpu.SemaphoreType.DMA((2,)),
        ],
        compiler_params=pltpu.CompilerParams(
            collective_id=collective_id, has_side_effects=True, vmem_limit_bytes=60 * 1024 * 1024
        ),
        name="gather_weights",
    )(wa, wf, *small, patches, *tables)


TOP = 32766.0
RING = 14
BETWEEN = (0, 12, 20, 28, 36)
ORDER = (
    (0, 0, 0), (0, 0, 2), (0, 0, 1), (0, 2, 0), (0, 0, 3), (1, 0, 0), (0, 2, 2), (2, 0, 3), (1, 0, 1), (0, 2, 1),
    (0, 1, 0), (1, 1, 0), (1, 1, 1), (1, 2, 0), (2, 0, 0), (1, 2, 1), (1, 0, 2), (0, 1, 2), (2, 1, 1), (0, 1, 1),
    (1, 0, 3), (1, 3, 1), (1, 2, 2), (2, 0, 1), (1, 1, 2), (0, 3, 0), (2, 1, 0), (2, 1, 3), (0, 1, 3), (2, 0, 2),
    (0, 3, 1), (0, 3, 2), (2, 2, 0), (1, 2, 3), (2, 2, 1), (1, 3, 0), (2, 1, 2), (2, 2, 2), (1, 3, 2), (0, 2, 3),
    (2, 2, 3), (2, 3, 0), (2, 3, 1), (1, 1, 3), (2, 3, 2), (0, 3, 3), (1, 3, 3), (2, 3, 3),
)


def lookup(values, base, t):
    digits = {4: 15, 64: 5}[base]
    words = [
        sum(v * base**i for i, v in enumerate(values[at : at + digits])) for at in range(0, len(values), digits)
    ]
    word = functools.reduce(lambda a, iw: jnp.where(t // digits == iw[0], iw[1], a), enumerate(words), 0)
    unit = functools.reduce(lambda a, i: jnp.where(t % digits == i, base**i, a), range(digits), 1)
    return word // unit % base


def encode(value):
    peak = jnp.maximum(jnp.max(jnp.abs(value), 0, keepdims=True), 1e-30)
    return jnp.round(value * (TOP / peak)).astype(jnp.int32).astype(jnp.int16), peak * (1.0 / TOP)


def decode(code, unit):
    return code.astype(jnp.int32).astype(F32) * unit


def weight_grad_kernel(
    depth, widths, mp_count, at_ref, pt_ref, mt_ref, ot_ref, ya_ref, yf_ref, gmod_ref, mod_ref, t2_ref, cond_ref, pre_ref,
    out_ref, vec_ref,
    x_all, ya_all, yf_all, work, q_send, u_send, q_recv, u_recv,
    gmod, panel, panel_f, scaled_send, scaled_recv, joined, own_vec, hid_part, vec_buf,
    moves, swaps, landing, send, recv, panel_sem, little_send, little_recv,
):
    z, x, y, c, first, second = coordinates()
    dp_count = 2 * depth
    peers_greet(dp_count, mp_count)
    rows = out_ref.shape[1]
    x_refs = (at_ref, pt_ref, mt_ref, ot_ref)
    tokens = at_ref.shape[1]
    width_a, width_f = widths
    here = (x, y)
    corner = (first[0] + second[0] - x, first[1] + second[1] - y)
    mate = (z * 2 + x, y * 2 + 1 - c)
    total = len(ORDER)

    own, theirs = pl.ds(0, tokens), pl.ds(tokens, tokens)
    local, remote = [], []

    def trade(mine, give, to, land):
        n = len(local)
        remote.append(pltpu.make_async_remote_copy(
            src_ref=give, dst_ref=land, send_sem=swaps.at[n], recv_sem=landing.at[n],
            device_id=mate, device_id_type=MESH,
        ))
        local.append(pltpu.make_async_copy(mine, to, moves.at[n]))
        remote[-1].start()
        local[-1].start()

    def trade_x(i):
        trade(x_refs[i], x_refs[i], x_all.at[i, :, own], x_all.at[i, :, theirs])

    def trade_y(ref, full, j):
        trade(ref.at[2 * j + c], ref.at[2 * j + 1 - c], full.at[j, own, :], full.at[j, theirs, :])

    trade_x(2)
    for columns in (pl.ds(0, STEP), pl.ds(STEP, STEP)):
        j = 1 - y
        trade(
            yf_ref.at[2 * j + c, :, columns], yf_ref.at[2 * j + 1 - c, :, columns],
            yf_all.at[j, own, columns], yf_all.at[j, theirs, columns],
        )
    trade_x(3)
    trade_x(0)
    trade_x(1)
    trade_y(ya_ref, ya_all, 1 - y)
    trade_y(yf_ref, yf_all, y)
    trade_y(ya_ref, ya_all, y)
    waits, known = [], set()
    for t, (g, kind, _) in enumerate(ORDER):
        need = [{0, 1}, {0, 2, 3}, {4, 5, 6}][g] | (set() if kind == 0 else {8} if g == 2 else {7})
        if need - known:
            waits.append((t, sorted(need - known)))
            known |= need

    def ready(numbers):
        for n in numbers:
            local[n].wait()
            remote[n].wait_recv()

    codes = tuple(16 * g + 4 * kind + j for g, kind, j in ORDER)

    def plan(t):
        code = lookup(codes, 64, t)
        g, kind, j = code // 16, code // 4 % 4, code % 4
        falling = jnp.where(depth - 1 - j <= z, depth - 2 - j, depth - 1 - j)
        rising = jnp.where(j >= z, j + 1, j)
        zz = jnp.where(z * 2 < depth, falling, rising)
        zz = jnp.where(j == depth - 1, z, zz)
        pick = lambda i: jnp.where(
            kind == 0, corner[i], jnp.where(kind == 1, second[i], jnp.where(kind == 2, first[i], here[i]))
        )
        return g, kind, zz, pick(0), pick(1)

    def product(g, zz, xx, yy):
        cut = pl.ds((zz * 2 + xx) * rows, rows)

        @pl.when(g == 0)
        def _():
            work[...] = dot(x_all[2, cut, :], yf_all[yy, :, :STEP])

        @pl.when(g == 1)
        def _():
            middle = 2 * width_f - STEP
            work[:, :middle] = dot(x_all[2, cut, :], yf_all[yy, :, STEP : 2 * width_f])
            work[:, middle:] = dot(x_all[3, cut, :], yf_all[yy, :, 2 * width_f :])

        @pl.when(g == 2)
        def _():
            edge = 3 * width_a
            low, high = edge // 128 * 128, -(-edge // 128) * 128
            left = dot(x_all[0, cut, :], ya_all[yy, :, :high])
            right = dot(x_all[1, cut, :], ya_all[yy, :, low:])
            lane = lax.broadcasted_iota(jnp.int32, (rows, high - low), 1)
            work[:, :low] = left[:, :low]
            work[:, low:high] = jnp.where(lane < edge - low, left[:, low:], right[:, : high - low])
            work[:, high:] = right[:, high - low :]

    def sent(slot):
        return (
            pltpu.make_async_copy(q_send.at[slot], q_send.at[slot], send.at[0, slot]),
            pltpu.make_async_copy(u_send.at[slot], u_send.at[slot], send.at[1, slot]),
        )

    def ship(t, g, dst_slot, target):
        slot = t % RING

        @pl.when(t >= RING)
        def _():
            for move in sent(slot):
                move.wait()

        code, unit = encode(work[...])
        q_send[slot] = code
        u_send[slot] = unit
        for i, (a, b) in enumerate(((q_send, q_recv), (u_send, u_recv))):
            pltpu.make_async_remote_copy(
                src_ref=a.at[slot], dst_ref=b.at[g, dst_slot],
                send_sem=send.at[i, slot], recv_sem=recv.at[i, g, dst_slot],
                device_id=target, device_id_type=MESH,
            ).start()

    def landed(g, slot):
        pltpu.make_async_copy(q_recv.at[g, slot], q_recv.at[g, slot], recv.at[0, g, slot]).wait()
        pltpu.make_async_copy(u_recv.at[g, slot], u_recv.at[g, slot], recv.at[1, g, slot]).wait()
        work[...] += decode(q_recv[g, slot], u_recv[g, slot])

    dp, mp = lax.axis_index("dp"), lax.axis_index("mp")
    bases = iter(range(0, 64 * dp_count, dp_count))
    little = lambda axis, count, source, target: Round(
        axis, count, source, target, little_send, little_recv, next(bases)
    )
    own_slot = lambda buf, me: lambda peer: buf.at[me]
    gmod_a = little("dp", dp_count, own_slot(gmod, dp), gmod)
    scaled_r = little("dp", dp_count, lambda peer: scaled_send.at[peer], scaled_recv)
    vec_m = little("mp", mp_count, own_slot(own_vec, mp), own_vec)
    hid_r = little("mp", mp_count, own_slot(hid_part, mp), hid_part)
    vec_a = little("dp", dp_count, own_slot(vec_buf, dp), vec_buf)
    lines = gmod_ref.shape[0]
    images = lines // 8

    def panels(count, source, use, hold):
        fetch = lambda i: pltpu.make_async_copy(source(i), hold.at[i % 2], panel_sem.at[i % 2])
        fetch(0).start()
        for i in range(count):
            if i + 1 < count:
                fetch(i + 1).start()
            fetch(i).wait()
            use(i, hold.at[i % 2])

    def one_hot(shape, hit):
        row, col = (lax.broadcasted_iota(jnp.int32, shape, i) for i in range(2))
        return hit(row, col).astype(F32).astype(LOW)

    def begin():
        gmod[dp] = gmod_ref[...]
        gmod_a.push()

    def scaled_grad():
        gmod_a.wait()
        every = gmod[...].reshape(dp_count * lines, D)
        scaled_send[...] = jnp.zeros(scaled_send.shape, F32)

        def use(j, piece):
            hit = lambda r, q: (r // 8 == q // lines) & (q % lines == j * images + r % 8) & (r % 8 < images)
            part = dot(one_hot((8 * dp_count, dp_count * lines), hit), every).astype(LOW)
            scaled_send[...] += dot_nt(part, piece[...].astype(LOW)).reshape(scaled_send.shape)

        panels(8, lambda j: mod_ref.at[:, pl.ds(j * D, D)], use, panel_f)
        scaled_recv[dp] = scaled_send[dp]
        scaled_r.push()

    def vector_grad():
        scaled_r.wait()
        for d in range(dp_count):
            joined[:, d * rows : (d + 1) * rows] = scaled_recv[d]
        own_vec[mp] = (joined[...] * silu_slope(cond_ref[mp])).astype(LOW).astype(F32)
        vec_m.push()

    def hidden_grad():
        vec_m.wait()
        vectors = own_vec[...].reshape(8 * mp_count, D).astype(LOW)
        def use(i, piece):
            hid_part[mp, :, i * rows : (i + 1) * rows] = dot_nt(vectors, piece[...])

        panels(D // rows, lambda i: t2_ref.at[pl.ds(i * rows, rows), :], use, panel)
        hid_r.push()

    def first_grad():
        hid_r.wait()
        grad = functools.reduce(lambda a, b: a + b, [hid_part[i] for i in range(mp_count)])
        grad_pre = (grad * silu_slope(pre_ref[...])).astype(LOW)
        vectors = own_vec[...].reshape(8 * mp_count, D).astype(LOW)
        hit = lambda r, q: (r // images == q // 8) & (r % images == q % 8)
        pick = one_hot((images * mp_count, 8 * mp_count), hit)
        count = images * mp_count
        vec_buf[dp, :count, :] = dot(pick, vectors).astype(LOW)
        vec_buf[dp, count:, :] = dot(pick, grad_pre).astype(LOW)
        vec_a.push()

    hooks = tuple(zip(BETWEEN, (begin, scaled_grad, vector_grad, hidden_grad, first_grad), strict=True))

    to_second = (z * 2 + second[0], second[1] * 2 + c)
    to_first = (z * 2 + first[0], first[1] * 2 + c)
    to_up = ((z + 1) * 2 + x, y * 2 + c)
    to_down = ((z - 1) * 2 + x, y * 2 + c)
    kept, passed = 2 * depth, 3 * depth + 1
    after_line = passed + depth + 1

    def step(t, _):
        g, kind, zz, xx, yy = plan(t)
        for at, numbers in waits:
            pl.when(t == at)(functools.partial(ready, numbers))
        for at, hook in hooks:
            pl.when(t == at)(hook)
        product(g, zz, xx, yy)
        line_first = g < 2
        late, mine = kind >= 2, zz == z
        along = late & ((kind == 3) | line_first)
        line = jnp.where(kind == 3, kept, passed)

        @pl.when(kind < 2)
        def _():
            ship(t, g, kind * depth + zz, to_second)

        @pl.when(late)
        def _():
            landed(g, (kind - 2) * depth + zz)

        @pl.when((kind == 3) & (jnp.logical_not(line_first) | mine))
        def _():
            landed(g, jnp.where(line_first, after_line, passed + zz))

        @pl.when(along & (zz >= z) & (z > 0))
        def _():
            landed(g, line + zz)

        @pl.when(along & (zz <= z) & (z < depth - 1))
        def _():
            landed(g, line + jnp.where(mine, depth, zz))

        @pl.when(along & (zz > z))
        def _():
            ship(t, g, line + zz, to_up)

        @pl.when(along & (zz < z))
        def _():
            ship(t, g, line + jnp.where(zz == z - 1, depth, zz), to_down)

        @pl.when((kind == 2) & (jnp.logical_not(line_first) | mine))
        def _():
            ship(t, g, jnp.where(line_first, after_line, passed + zz), to_first)

        @pl.when((kind == 3) & mine)
        def _():
            out_ref[g] = work[...]

        return 0

    lax.fori_loop(0, total, step, 0)

    def drain(slot, _):
        for move in sent(slot):
            move.wait()
        return 0

    lax.fori_loop(0, RING, drain, 0)
    for move in remote:
        move.wait_send()
    vec_a.wait()
    vec_ref[...] = vec_buf[...]
    for one in (gmod_a, scaled_r, vec_m, hid_r, vec_a):
        one.finish()


def weight_grads(turned, ya, yf, grad_mod, mod_rows, second, cond, pre, dp, collective_id=1):
    depth, mp = dp // 2, ya.shape[0]
    tokens = turned[0].shape[1]
    rows = D // dp
    slots = 4 * depth + 3
    images = grad_mod.shape[0] // 8
    hbm, vmem = pl.BlockSpec(memory_space=pl.ANY), pl.BlockSpec(memory_space=pltpu.VMEM)
    vectors = (dp, 2 * images * mp, D)
    return pl.pallas_call(
        functools.partial(weight_grad_kernel, depth, (ya.shape[2] // 4, yf.shape[2] // 3), mp),
        out_shape=[jax.ShapeDtypeStruct((3, rows, STEP), F32), jax.ShapeDtypeStruct(vectors, LOW)],
        in_specs=[hbm] * 6 + [vmem, hbm, hbm, vmem, vmem],
        out_specs=[vmem, vmem],
        scratch_shapes=[
            pltpu.VMEM((4, D, 2 * tokens), LOW),
            pltpu.VMEM((2, 2 * tokens, ya.shape[2]), LOW),
            pltpu.VMEM((2, 2 * tokens, yf.shape[2]), LOW),
            pltpu.VMEM((rows, STEP), F32),
            pltpu.VMEM((RING, rows, STEP), jnp.int16),
            pltpu.VMEM((RING, 1, STEP), F32),
            pltpu.VMEM((3, slots, rows, STEP), jnp.int16),
            pltpu.VMEM((3, slots, 1, STEP), F32),
            pltpu.VMEM((dp, *grad_mod.shape), LOW),
            pltpu.VMEM((2, rows, D), LOW),
            pltpu.VMEM((2, rows, D), F32),
            pltpu.VMEM((dp, 8, rows), F32),
            pltpu.VMEM((dp, 8, rows), F32),
            pltpu.VMEM((8, D), F32),
            pltpu.VMEM((mp, 8, D), F32),
            pltpu.VMEM((mp, 8 * mp, D), F32),
            pltpu.VMEM(vectors, LOW),
            pltpu.SemaphoreType.DMA((9,)),
            pltpu.SemaphoreType.DMA((9,)),
            pltpu.SemaphoreType.DMA((9,)),
            pltpu.SemaphoreType.DMA((2, RING)),
            pltpu.SemaphoreType.DMA((2, 3, slots)),
            pltpu.SemaphoreType.DMA((2,)),
            pltpu.SemaphoreType.DMA((5 * dp,)),
            pltpu.SemaphoreType.DMA((5 * dp,)),
        ],
        compiler_params=pltpu.CompilerParams(
            collective_id=collective_id, has_side_effects=True, vmem_limit_bytes=62 * 1024 * 1024
        ),
        name="weight_grads",
    )(*turned, ya, yf, grad_mod, mod_rows, second, cond, pre)


def sum_kernel(mp_count, dp_count, in_ref, out_ref, over_dp, over_mp, send, recv):
    dp, mp = lax.axis_index("dp"), lax.axis_index("mp")
    peers_greet(dp_count, mp_count)
    first = Round("dp", dp_count, lambda peer: over_dp.at[dp], over_dp, send, recv, 0)
    second = Round("mp", mp_count, lambda peer: over_mp.at[mp], over_mp, send, recv, dp_count)
    over_dp[dp] = in_ref[...]
    first.push()
    first.wait()
    over_mp[mp] = functools.reduce(lambda a, b: a + b, [over_dp[i] for i in range(dp_count)])
    second.push()
    second.wait()
    out_ref[...] = functools.reduce(lambda a, b: a + b, [over_mp[i] for i in range(mp_count)])
    first.finish()
    second.finish()


def sum_pallas(values, dp, mp, collective_id=2):
    return pl.pallas_call(
        functools.partial(sum_kernel, mp, dp),
        out_shape=jax.ShapeDtypeStruct(values.shape, F32),
        in_specs=[pl.BlockSpec(memory_space=pltpu.VMEM)],
        out_specs=pl.BlockSpec(memory_space=pltpu.VMEM),
        scratch_shapes=[
            pltpu.VMEM((dp, *values.shape), F32), pltpu.VMEM((mp, *values.shape), F32),
            pltpu.SemaphoreType.DMA((dp + mp,)), pltpu.SemaphoreType.DMA((dp + mp,)),
        ],
        compiler_params=pltpu.CompilerParams(collective_id=collective_id, has_side_effects=True),
        name="sum_scalars",
    )(values)


SLAB = 160
VMEM_LIMIT = 60 * 1024 * 1024


def whole(shape):
    return pl.BlockSpec(shape, lambda m: (0,) * len(shape), pipeline_mode=pl.Buffered(1))


def by_block(*shape):
    return pl.BlockSpec((1, *shape), lambda m: (m,) + (0,) * len(shape))


def dot(left, right):
    return lax.dot_general(left, right, (((1,), (0,)), ((), ())), preferred_element_type=F32)


def dot_nt(left, right):
    return lax.dot_general(left, right, (((1,), (1,)), ((), ())), preferred_element_type=F32)


def dot_tn(left, right):
    return lax.dot_general(left, right, (((0,), (0,)), ((), ())), preferred_element_type=F32)


def slabs(tokens, body, sums=0):
    totals = []
    for block in range(tokens // PAIR):

        def step(i, carry, block=block):
            rows = pl.ds(pl.multiple_of(block * PAIR + i * SLAB, SLAB), SLAB)
            lead, values = body(block, rows)
            head, rest = carry
            head = tuple(h + jnp.sum(jnp.where(lead, v, 0.0), 0, keepdims=True) for h, v in zip(head, values))
            rest = tuple(r + jnp.sum(jnp.where(lead, 0.0, v), 0, keepdims=True) for r, v in zip(rest, values))
            return head, rest

        zero = tuple(jnp.zeros((1, D), F32) for _ in range(sums))
        totals.extend(lax.fori_loop(0, PAIR // SLAB, step, (zero, zero)))
    return totals


def spread(mod_ref, j, block, lead):
    row = lambda i: mod_ref[2 * block + i : 2 * block + i + 1, j * D : (j + 1) * D]
    return jnp.where(lead, row(0), row(1))


def turn(values, cos_row, sin_row, direction):
    quarter = HD // 4
    width = values.shape[1]
    lane = lax.broadcasted_iota(jnp.int32, values.shape, 1)
    ahead = pltpu.roll(values, width - quarter, 1)
    behind = pltpu.roll(values, quarter, 1)
    partner = jnp.where(lane % (2 * quarter) < quarter, ahead, behind)
    return values * cos_row + partner * (sin_row * direction)


def same_image(even_col, even_row, block):
    rows = slice(block * PAIR, (block + 1) * PAIR)
    return even_col[rows, :1] == even_row[block, :1, :]


def softmax(query, key, same):
    scores = jnp.where(same, dot_nt(key, query) * (HD ** (-0.5) * math.log2(math.e)), -1e30)
    expo = jnp.exp2(scores - jnp.max(scores, 0, keepdims=True))
    return expo * (1.0 / jnp.sum(expo, 0, keepdims=True))


def attn_begin(patch_ref, patch_rows, patch_bias, mod_ref, col_ref, x0_ref, a_ref, at_ref):
    x0_ref[...] = dot_tn(patch_ref[...], patch_rows) + patch_bias

    def body(block, rows):
        lead = col_ref[rows, :1] != 0
        normed, _ = layer_norm(x0_ref[rows, :])
        shift, scale = spread(mod_ref, 0, block, lead), spread(mod_ref, 1, block, lead)
        a_ref[rows, :] = (normed * (1.0 + scale) + shift).astype(LOW)
        return lead, ()

    slabs(a_ref.shape[0], body)
    at_ref[...] = a_ref[...].T


def attn_block(w_ref, cos_ref, sin_ref, col_ref, row_ref, a_ref, qkv_ref, att_ref, keep):
    tokens, width = att_ref.shape
    made = dot(a_ref[...], w_ref[:, : 3 * width])
    qkv_ref[:, : 2 * width] = turn(made[:, : 2 * width], cos_ref[...], sin_ref[...], 1.0).astype(LOW)
    qkv_ref[:, 2 * width :] = made[:, 2 * width :].astype(LOW)
    for block in range(tokens // PAIR):
        same = same_image(col_ref, row_ref, block)
        rows = slice(block * PAIR, (block + 1) * PAIR)
        for head in range(width // HD):
            take = lambda i: qkv_ref[rows, i * width + head * HD : i * width + (head + 1) * HD]
            probs = softmax(take(0), take(1), same)
            keep(block * (width // HD) + head, probs)
            att_ref[rows, head * HD : (head + 1) * HD] = dot_tn(probs.astype(LOW), take(2)).astype(LOW)
    return dot_nt(att_ref[...], w_ref[:, 3 * width :])


def attn_end(mod_ref, col_ref, x0_ref, proj_ref, x1_ref, m_ref, mt_ref):
    def body(block, rows):
        lead = col_ref[rows, :1] != 0
        x_one = x0_ref[rows, :] + spread(mod_ref, 2, block, lead) * proj_ref[rows, :]
        x1_ref[rows, :] = x_one
        normed, _ = layer_norm(x_one)
        shift, scale = spread(mod_ref, 3, block, lead), spread(mod_ref, 4, block, lead)
        m_ref[rows, :] = (normed * (1.0 + scale) + shift).astype(LOW)
        return lead, ()

    slabs(m_ref.shape[0], body)
    mt_ref[...] = m_ref[...].T


def attn_forward_kernel(
    patch_ref, prow_ref, pbias_ref, mod_ref, w_ref, cos_ref, sin_ref, col_ref, row_ref,
    x0_ref, x1_ref, proj_ref, m_ref, at_ref, mt_ref, qkv_ref, att_ref, probs_ref, a_ref,
):
    step, last = pl.program_id(0), pl.num_programs(0) - 1

    @pl.when(step == 0)
    def _():
        attn_begin(patch_ref, prow_ref[...], pbias_ref[...], mod_ref, col_ref, x0_ref, a_ref, at_ref)
        proj_ref[...] = jnp.zeros(proj_ref.shape, F32)

    def keep(i, probs):
        probs_ref[0, i] = probs

    proj_ref[...] += attn_block(
        w_ref.at[0], cos_ref, sin_ref, col_ref, row_ref, a_ref, qkv_ref.at[0], att_ref.at[0], keep
    )

    @pl.when(step == last)
    def _():
        attn_end(mod_ref, col_ref, x0_ref, proj_ref, x1_ref, m_ref, mt_ref)


def attn_forward(patches, patch_rows, patch_bias, modulation, wa_all, tables):
    blocks, _, width = wa_all.shape
    width //= 4
    tokens = patches.shape[1]
    full, turned = (tokens, D), (D, tokens)
    ins = (patches, patch_rows, patch_bias, modulation)
    return pl.pallas_call(
        attn_forward_kernel,
        grid=(blocks,),
        out_shape=[jax.ShapeDtypeStruct(full, F32)] * 3
        + [jax.ShapeDtypeStruct(full, LOW)]
        + [jax.ShapeDtypeStruct(turned, LOW)] * 2
        + [
            jax.ShapeDtypeStruct((blocks, tokens, 3 * width), LOW),
            jax.ShapeDtypeStruct((blocks, tokens, width), LOW),
            jax.ShapeDtypeStruct((blocks, tokens // PAIR * (width // HD), PAIR, PAIR), F32),
        ],
        in_specs=[whole(a.shape) for a in ins] + [by_block(D, 4 * width)] + [whole(a.shape) for a in tables],
        out_specs=[whole(full)] * 4
        + [whole(turned)] * 2
        + [by_block(tokens, 3 * width), by_block(tokens, width)]
        + [by_block(tokens // PAIR * (width // HD), PAIR, PAIR)],
        scratch_shapes=[pltpu.VMEM(full, LOW)],
        compiler_params=pltpu.CompilerParams(vmem_limit_bytes=VMEM_LIMIT),
        name="attn_forward",
    )(*ins, wa_all, *tables)


PARTS = 1


def units(part, width):
    size = width // PARTS
    return slice(part * size, (part + 1) * size), slice(width + part * size, width + (part + 1) * size)


def ffn_kernel(
    m_ref, x1_ref, proj_ref, mod_ref, head_ref, target_ref, weight_ref, col_ref, w_ref,
    yf_ref, gx1_ref, gp_ref, gpt_ref, gmot_ref, ghead_ref, loss_ref, sums_ref,
    gu_ref, out_ref, back_ref, low_ref,
):
    width = gu_ref.shape[2] // 2
    tokens = m_ref.shape[0]
    step, count = pl.program_id(0), pl.num_programs(0) // 2

    @pl.when(step == 0)
    def _():
        out_ref[...] = jnp.zeros(out_ref.shape, F32)

    @pl.when(step == count)
    def _():
        back_ref[...] = jnp.zeros(back_ref.shape, F32)

    @pl.when(step < count)
    def _():
        for part in range(PARTS):
            own, other = units(part, width)
            gate, up_val = dot(m_ref[...], w_ref[0, :, own]), dot(m_ref[...], w_ref[0, :, other])
            gu_ref[step, :, own] = gate
            gu_ref[step, :, other] = up_val
            hidden = (gate * lax.logistic(gate) * up_val).astype(LOW)
            last = slice(other.start + width, other.stop + width)
            out_ref[...] += dot_nt(hidden, w_ref[0, :, last])

    @pl.when(step == count - 1)
    def _():
        def final_norm(block, rows):
            lead = col_ref[rows, :1] != 0
            x_two = x1_ref[rows, :] + spread(mod_ref, 5, block, lead) * out_ref[rows, :]
            return lead, spread(mod_ref, 7, block, lead), *layer_norm(x_two)

        def before(block, rows):
            lead, scale, normed, _ = final_norm(block, rows)
            low_ref[rows, :] = (normed * (1.0 + scale) + spread(mod_ref, 6, block, lead)).astype(LOW)
            return lead, ()

        slabs(tokens, before)
        diff = dot_nt(head_ref[...], low_ref[...]) - target_ref[...]
        loss = jnp.sum(weight_ref[:1, :] * jnp.mean(diff * diff, 0, keepdims=True), 1, keepdims=True)
        loss_ref[...] = jnp.broadcast_to(loss, loss_ref.shape)
        grad_pred = (2.0 / OUT * diff * weight_ref[1:2, :]).astype(LOW)
        ghead_ref[...] = dot(grad_pred, low_ref[...])
        back_ref[...] = dot_tn(grad_pred, head_ref[...])

        def after(block, rows):
            lead, scale, normed, inv_std = final_norm(block, rows)
            grad_f = back_ref[rows, :]
            grad_x2 = norm_back(grad_f, normed, inv_std, scale)
            gx1_ref[rows, :] = grad_x2
            low_ref[rows, :] = (spread(mod_ref, 5, block, lead) * grad_x2).astype(LOW)
            return lead, (grad_f, grad_f * normed, grad_x2 * out_ref[rows, :])

        for image, rows in enumerate(slabs(tokens, after, 3)):
            for k in range(3):
                sums_ref[k, image : image + 1, :] = rows[k]
        gmot_ref[...] = low_ref[...].T

    @pl.when(step >= count)
    def _():
        for part in range(PARTS):
            own, other = units(part, width)
            last = slice(other.start + width, other.stop + width)
            grad_hid = dot(low_ref[...], w_ref[0, :, last])
            back = 2 * count - 1 - step
            gate, up_val = gu_ref[back, :, own], gu_ref[back, :, other]
            sigma = lax.logistic(gate)
            act = gate * sigma
            slope = sigma * (1.0 + gate * (1.0 - sigma))
            yf_ref[0, :, own] = (grad_hid * up_val * slope).astype(LOW)
            yf_ref[0, :, other] = (grad_hid * act).astype(LOW)
            yf_ref[0, :, last] = (act * up_val).astype(LOW)
        back_ref[...] += dot_nt(yf_ref[0, :, : 2 * width], w_ref[0, :, : 2 * width])

    @pl.when(step == 2 * count - 1)
    def _():
        def body(block, rows):
            lead = col_ref[rows, :1] != 0
            grad_m = back_ref[rows, :]
            normed, inv_std = layer_norm(x1_ref[rows, :])
            grad_x1 = gx1_ref[rows, :] + norm_back(grad_m, normed, inv_std, spread(mod_ref, 4, block, lead))
            gx1_ref[rows, :] = grad_x1
            gp_ref[rows, :] = (spread(mod_ref, 2, block, lead) * grad_x1).astype(LOW)
            return lead, (grad_m, grad_m * normed, grad_x1 * proj_ref[rows, :])

        for image, rows in enumerate(slabs(tokens, body, 3)):
            for k in range(3):
                sums_ref[3 + k, image : image + 1, :] = rows[k]
        gpt_ref[...] = gp_ref[...].T


def ffn(m_in, x_one, proj, modulation, head_rows, target, weights, even_col, wf_all):
    blocks, _, width = wf_all.shape
    width //= 3
    tokens = m_in.shape[0]
    full, turned = (tokens, D), (D, tokens)
    ins = (m_in, x_one, proj, modulation, head_rows, target, weights, even_col)
    there_and_back = lambda i: (jnp.where(i < blocks, i, 2 * blocks - 1 - i), 0, 0)
    back = lambda i: (jnp.where(i < blocks, blocks - 1, 2 * blocks - 1 - i), 0, 0)
    outs = [
        (full, F32), (full, LOW), (turned, LOW), (turned, LOW),
        ((OUT, D), F32), ((8, 128), F32), ((6, modulation.shape[0], D), F32),
    ]
    return pl.pallas_call(
        ffn_kernel,
        grid=(2 * blocks,),
        out_shape=[jax.ShapeDtypeStruct((blocks, tokens, 3 * width), LOW)]
        + [jax.ShapeDtypeStruct(*o) for o in outs],
        in_specs=[whole(a.shape) for a in ins] + [pl.BlockSpec((1, D, 3 * width), there_and_back)],
        out_specs=[pl.BlockSpec((1, tokens, 3 * width), back)] + [whole(o[0]) for o in outs],
        scratch_shapes=[
            pltpu.VMEM((blocks, tokens, 2 * width), F32),
            pltpu.VMEM(full, F32), pltpu.VMEM(full, F32), pltpu.VMEM(full, LOW),
        ],
        compiler_params=pltpu.CompilerParams(vmem_limit_bytes=VMEM_LIMIT),
        name="feed_forward",
    )(*ins, wf_all)


def attn_backward_kernel(
    grad_ref, gx1_ref, x0_ref, patch_ref, mod_ref, w_ref, qkv_ref, att_ref, probs_ref, cos_ref, sin_ref, col_ref, row_ref,
    out_ref, rows_ref, sums_ref, tmp_ref, back_att, back_ref, low_ref,
):
    width = att_ref.shape[2]
    tokens = grad_ref.shape[0]
    scale = HD ** (-0.5)
    step, last = pl.program_id(0), pl.num_programs(0) - 1
    back_att[...] = dot(grad_ref[...], w_ref[0, :, 3 * width :]).astype(LOW)
    for block in range(tokens // PAIR):
        rows = slice(block * PAIR, (block + 1) * PAIR)
        for head in range(width // HD):
            lanes = lambda i: slice(i * width + head * HD, i * width + (head + 1) * HD)
            query, key, value = (qkv_ref[0, rows, lanes(i)] for i in range(3))
            grad = back_att[rows, lanes(0)]
            probs = probs_ref[0, block * (width // HD) + head]
            grad_p = dot_nt(value, grad)
            centre = jnp.sum(probs * grad_p, 0, keepdims=True)
            grad_s = (probs * (grad_p - centre)).astype(LOW)
            tmp_ref[rows, lanes(0)] = dot_tn(grad_s, key) * scale
            tmp_ref[rows, lanes(1)] = dot(grad_s, query) * scale
            tmp_ref[rows, lanes(2)] = dot(probs.astype(LOW), grad)
    out_ref[0, :, : 2 * width] = turn(tmp_ref[:, : 2 * width], cos_ref[...], sin_ref[...], -1.0).astype(LOW)
    out_ref[0, :, 2 * width : 3 * width] = tmp_ref[:, 2 * width :].astype(LOW)
    out_ref[0, :, 3 * width :] = att_ref[0]
    part = dot_nt(out_ref[0, :, : 3 * width], w_ref[0, :, : 3 * width])

    @pl.when(step == 0)
    def _():
        back_ref[...] = part

    @pl.when(step > 0)
    def _():
        back_ref[...] += part

    @pl.when(step == last)
    def _():
        def body(block, rows):
            lead = col_ref[rows, :1] != 0
            grad_a = back_ref[rows, :]
            normed, inv_std = layer_norm(x0_ref[rows, :])
            back = norm_back(grad_a, normed, inv_std, spread(mod_ref, 1, block, lead))
            grad_x0 = (gx1_ref[rows, :] + back).astype(LOW)
            low_ref[rows, :] = grad_x0
            return lead, (grad_a, grad_a * normed, grad_x0.astype(F32))

        bias = jnp.zeros((1, D), F32)
        for image, rows in enumerate(slabs(tokens, body, 3)):
            for k in range(2):
                sums_ref[k, image : image + 1, :] = rows[k]
            bias = bias + rows[2]
        rows_ref[:PATCH_IN, :] = dot(patch_ref[...], low_ref[...])
        rows_ref[PATCH_IN : PATCH_IN + 1, :] = bias
        rows_ref[PATCH_IN + 1 :, :] = jnp.zeros((7, D), F32)


def attn_backward(grad_proj, gx1, x_zero, patches, modulation, wa_all, qkv, att, probs, tables):
    blocks, tokens, width = att.shape
    full = (tokens, D)
    ins = (grad_proj, gx1, x_zero, patches, modulation)
    outs = [((PATCH_IN + 8, D), F32), ((2, modulation.shape[0], D), F32)]
    return pl.pallas_call(
        attn_backward_kernel,
        grid=(blocks,),
        out_shape=[jax.ShapeDtypeStruct((blocks, tokens, 4 * width), LOW)]
        + [jax.ShapeDtypeStruct(*o) for o in outs],
        in_specs=[whole(a.shape) for a in ins]
        + [by_block(D, 4 * width), by_block(tokens, 3 * width), by_block(tokens, width), by_block(*probs.shape[1:])]
        + [whole(a.shape) for a in tables],
        out_specs=[by_block(tokens, 4 * width)] + [whole(o[0]) for o in outs],
        scratch_shapes=[
            pltpu.VMEM((tokens, 3 * width), F32), pltpu.VMEM((tokens, width), LOW),
            pltpu.VMEM(full, F32), pltpu.VMEM(full, LOW),
        ],
        compiler_params=pltpu.CompilerParams(vmem_limit_bytes=VMEM_LIMIT),
        name="attn_backward",
    )(*ins, wa_all, qkv, att, probs, *tables)


def gather_library(wa, wf, small):
    dp, mp = lax.axis_size("dp"), lax.axis_size("mp")
    info, embed, first, first_bias, second, part, tail, columns = small
    depth = wa.shape[0]

    def one(w):
        full = lax.all_gather(w, BOTH, axis=0)
        full = full.reshape(dp, mp, *w.shape).transpose(1, 0, 2, 3)
        return full.reshape(mp, dp * w.shape[0], w.shape[1])

    over_dp = lambda v: lax.all_gather(v, "dp", axis=0)
    pre = lax.psum(dot(embed, first) + first_bias, "mp")
    cond = lax.psum(dot(jax.nn.silu(pre).astype(LOW), second) + part, "mp")
    scaled_all = over_dp(jax.nn.silu(cond).astype(LOW))
    scaled = scaled_all.reshape(-1, D)
    mine = lax.dynamic_slice_in_dim(scaled, lax.axis_index("dp") * depth, depth, 1)
    mod = lax.psum_scatter(dot(mine, columns), "dp", scatter_dimension=0, tiled=True)
    over_mp = lambda v: lax.all_gather(v, "mp", axis=0)
    return one(wa), one(wf), over_mp(mod), over_mp(tail), pre, cond, scaled_all, over_dp(info), over_dp(jax.nn.silu(pre).astype(LOW))


def sibling(value):
    mp = lax.axis_size("mp")
    return lax.ppermute(value, "mp", [(i, i + 1 - 2 * (i % 2)) for i in range(mp)])


def vector_grads(grad_mod, mod_rows, second, cond, pre):
    images = grad_mod.shape[0] // 8
    group = lax.all_gather(grad_mod.reshape(8, images, D), "mp", axis=1, tiled=True)
    group = group.transpose(1, 0, 2).reshape(cond.shape[0], 8 * D)
    every = lax.all_gather(group, "dp", axis=0, tiled=True)
    scaled = lax.all_gather(dot_nt(every, mod_rows), "dp", axis=1, tiled=True)
    scaled = lax.dynamic_slice_in_dim(scaled, lax.axis_index("dp") * cond.shape[0], cond.shape[0], 0)
    grad_cond = (scaled * silu_slope(cond)).astype(LOW)
    hidden = lax.psum(dot_nt(grad_cond, second), "mp")
    grad_pre = (hidden * silu_slope(pre)).astype(LOW)
    return lax.all_gather(jnp.concatenate([grad_cond, grad_pre], 0), "dp", axis=0)


def plane_grads(turned, ya, yf):
    dp, mp = lax.axis_size("dp"), lax.axis_size("mp")
    core, place = lax.axis_index("mp") % 2, lax.axis_index("mp") // 2
    x_all = jnp.stack(turned)
    x_two = jnp.concatenate([x_all, sibling(x_all)], 2)
    width_a, width_f = ya.shape[2] // 4, yf.shape[2] // 3

    def halves(values):
        split = values.reshape(mp // 2, 2, *values.shape[1:])
        mine = lax.dynamic_index_in_dim(split, core, 1, False)
        theirs = lax.dynamic_index_in_dim(split, 1 - core, 1, False)
        return jnp.concatenate([mine, sibling(theirs)], 1)

    def product(x, values):
        return jnp.einsum("dt,btn->bdn", x, values, preferred_element_type=F32)

    ya_two, yf_two = halves(ya), halves(yf)
    grad_a = jnp.concatenate(
        [product(x_two[0], ya_two[..., : 3 * width_a]), product(x_two[1], ya_two[..., 3 * width_a :])], 2
    )
    grad_f = jnp.concatenate(
        [product(x_two[2], yf_two[..., : 2 * width_f]), product(x_two[3], yf_two[..., 2 * width_f :])], 2
    )
    grad = jnp.stack([grad_f[..., :STEP], grad_f[..., STEP:], grad_a])
    part = lax.psum_scatter(grad, "dp", scatter_dimension=2, tiled=True)
    total = lax.dynamic_index_in_dim(part, place, 1, False)
    for hop in range(1, mp // 2):
        perm = [(i, (i + 2 * hop) % mp) for i in range(mp)]
        out = lax.dynamic_index_in_dim(part, (place + hop) % (mp // 2), 1, False)
        total = total + lax.ppermute(out, "mp", perm)
    return total


def per_device(
    patches, target, segments, positions, classes, timesteps, t_weight, step_count,
    qkv_w, qkv_m, qkv_v, out_w, out_m, out_v, ffn_in_w, ffn_in_m, ffn_in_v,
    ffn_out_w, ffn_out_m, ffn_out_v, mod_w, mod_m, mod_v, table_w, table_m, table_v,
):
    mp_count, dp_count = lax.axis_size("mp"), lax.axis_size("dp")
    mp_index, dp_index = lax.axis_index("mp"), lax.axis_index("dp")
    tokens = patches.shape[1]
    pairs = tokens // PAIR
    images = 2 * pairs
    own_rows = table_w.shape[0]
    depth = mod_w.shape[0]
    width_a, width_f = qkv_w.shape[2], ffn_in_w.shape[2]

    regular = dp_count == 2 * DEPTH and mp_count == 4
    group_images = classes.shape[0]
    wa = jnp.concatenate([qkv_w[0], qkv_w[1], qkv_w[2], out_w.T], 1).astype(LOW)
    wf = jnp.concatenate([ffn_in_w[0], ffn_in_w[1], ffn_out_w.T], 1).astype(LOW)

    table_b = table_w.astype(LOW)
    gap = D + 16
    padded = lax.dynamic_update_slice(jnp.zeros((2 * gap + own_rows, D), LOW), table_b, (gap, 0))

    def placed(row, count):
        return lax.dynamic_slice_in_dim(padded, row - mp_index * own_rows + gap, count, 0)

    half = FREQ // 2
    freqs = jnp.exp(-math.log(10000.0) * jnp.arange(half, dtype=F32) / half)

    def embedding(times):
        angles = times[:, None] * freqs[None, :]
        return jnp.concatenate([jnp.cos(angles), jnp.sin(angles)], 1).astype(LOW)

    row_ids = mp_index * own_rows + jnp.arange(own_rows, dtype=jnp.int32)
    own_hot = (classes[:, None] == row_ids[None, :]).astype(LOW)
    part = matmul(own_hot, table_b) + placed(ROW_OUT_BIAS, 1).astype(F32)
    info = jnp.zeros((8, 128), F32)
    for i, values in enumerate((classes, timesteps, t_weight)):
        info = info.at[i, :group_images].set(values.astype(F32))
    mod_cols = mod_w.shape[1] // mp_count
    small = (
        info, embedding(timesteps.astype(F32)), placed(ROW_TIME_IN, FREQ),
        placed(ROW_TIME_BIAS, 1).astype(F32), placed(ROW_TIME_OUT, D), part,
        jnp.pad(placed(ROW_PATCH, TAIL), ((0, 64 - TAIL), (0, 0))),
        lax.dynamic_slice_in_dim(mod_w, mp_index * mod_cols, mod_cols, 1).astype(LOW),
    )
    own_seg = lax.dynamic_slice_in_dim(segments, mp_index * tokens, tokens)
    own_pos = lax.dynamic_slice_in_dim(positions, mp_index * tokens, tokens, 1)
    even = (own_seg % 2 == 0).reshape(pairs, PAIR)
    heads = 2 * width_a // HD
    cos_row, sin_row = (jnp.tile(t, (1, heads)) for t in rotary_tables(own_pos))
    even_col = even.astype(jnp.int32).reshape(tokens, 1)
    even_row = jnp.broadcast_to(even.astype(jnp.int32)[:, None], (pairs, 8, PAIR))
    tables = (cos_row, sin_row, even_col, even_row)

    if regular:
        gathered = gather_pallas(wa, wf, small, patches, tables, dp_count, mp_count)
        wa_all, wf_all, modulation, tail, pre, cond, scaled, infos, hidden = gathered[:9]
        x_zero, x_one, proj, m_in, a_turned, m_turned, qkv, att, probs = gathered[9:]
    else:
        wa_all, wf_all, mod_all, tails, pre, cond, scaled, infos, hidden = gather_library(wa, wf, small)
        tail = jnp.sum(tails.astype(F32), 0)
        mod_own = lax.dynamic_slice_in_dim(mod_all, mp_index * images, images, 1)
        mod_bias = tail[ROW_MOD_BIAS - ROW_PATCH : TAIL].reshape(-1)
        modulation = mod_own.transpose(1, 0, 2).reshape(images, -1) + mod_bias
        x_zero, x_one, proj, m_in, a_turned, m_turned, qkv, att, probs = attn_forward(
            patches, tail[:PATCH_IN].astype(LOW), tail[PATCH_IN][None, :], modulation, wa_all, tables
        )
    count_all = dp_count * group_images
    scaled = scaled.reshape(count_all, D)
    classes_all, times_all, weights_all = (infos[:, i, :group_images].reshape(-1) for i in range(3))
    head_rows = tail[PATCH_IN + 1 : PATCH_IN + 1 + OUT].astype(LOW)
    weight_sum = jnp.sum(weights_all)

    ones = jnp.ones((count_all, 1), LOW)
    zeros = lambda n: jnp.zeros((count_all, n), LOW)
    own_cols = lambda a: lax.dynamic_slice_in_dim(a, mp_index * own_rows, own_rows, 1)
    left_pre = own_cols(
        jnp.concatenate([zeros(NCLS), embedding(times_all), ones, zeros(ROWS - ROW_TIME_OUT)], 1)
    )
    class_hot = (classes_all[:, None] == jnp.arange(NCLS, dtype=F32)[None, :]).astype(LOW)
    hidden = hidden.reshape(count_all, D)
    left_cond = own_cols(
        jnp.concatenate(
            [class_hot, zeros(ROW_TIME_OUT - NCLS), hidden, ones, zeros(ROWS - ROW_PATCH)], 1
        )
    )
    own_scaled = lax.dynamic_slice_in_dim(scaled, dp_index * depth, depth, 1)

    first_len = jnp.sum(even.astype(F32), 1)
    own_tw = lax.dynamic_slice_in_dim(t_weight, mp_index * images, images).reshape(pairs, 2)
    per_tok = own_tw / jnp.stack([first_len, PAIR - first_len], 1)
    tok_weight = jnp.where(even, per_tok[:, :1], per_tok[:, 1:]).reshape(1, tokens)
    weights = jnp.concatenate([tok_weight, tok_weight / weight_sum], 0)
    yf, grad_x1, grad_proj, proj_turned, mo_turned, grad_head, loss, sums_f = ffn(
        m_in, x_one, proj, modulation, head_rows, target, weights, even_col, wf_all
    )
    ya, grad_patch, sums_a = attn_backward(
        grad_proj, grad_x1, x_zero, patches, modulation, wa_all, qkv, att, probs, tables
    )
    loss_part = loss[0, 0]
    x_turned = (a_turned, proj_turned, m_turned, mo_turned)
    grad_mod = jnp.concatenate(
        [sums_a[0], sums_a[1], sums_f[5], sums_f[3], sums_f[4], sums_f[2], sums_f[0], sums_f[1]], 0
    ).astype(LOW)
    cond_own = jnp.pad(cond.reshape(mp_count, images, D), ((0, 0), (0, 8 - images), (0, 0)))
    pre_own = jnp.pad(pre.reshape(mp_count, images, D), ((0, 0), (0, 8 - images), (0, 0)))
    if regular:
        summed, vectors = weight_grads(
            x_turned, ya, yf, grad_mod, mod_w, small[4], cond_own, pre_own.reshape(-1, D), dp_count
        )
    else:
        summed = plane_grads(x_turned, ya, yf)
        vectors = vector_grads(grad_mod, mod_w.astype(LOW), small[4], cond, pre)
    own_wf, own_wa = jnp.concatenate([summed[0], summed[1]], 1), summed[2]

    grad_mod_all = lax.all_gather(grad_mod, BOTH, axis=0).reshape(-1, 8, images, D)
    grad_mod_all = grad_mod_all.transpose(0, 2, 1, 3).reshape(count_all, 8 * D)
    grad_mod_w = matmul_tn(own_scaled, grad_mod_all)
    grad_mod_bias = jnp.sum(grad_mod_all.astype(F32), 0).reshape(8, D)
    grad_cvec = vectors[:, :group_images].reshape(count_all, D)
    grad_pre = vectors[:, group_images:].reshape(count_all, D)
    token_rows = jnp.concatenate([grad_patch[: PATCH_IN + 1], grad_head], 0)
    token_rows = jnp.concatenate([lax.psum(token_rows, BOTH), grad_mod_bias], 0)
    blank = -(-own_rows // 8) * 8
    start = jnp.clip(mp_index * own_rows - ROW_PATCH + blank, 0, blank + 64)
    spaced = lax.dynamic_update_slice(jnp.zeros((2 * blank + 64, D), F32), token_rows, (blank, 0))
    tail_own = lax.dynamic_slice_in_dim(spaced, start, own_rows, 0)
    grad_table = matmul_tn(left_cond, grad_cvec) + matmul_tn(left_pre, grad_pre) + tail_own

    grad_qkv = jnp.stack([own_wa[:, j * width_a : (j + 1) * width_a] for j in range(3)])
    grad_out_w = own_wa[:, 3 * width_a :].T
    grad_ffn_in = jnp.stack([own_wf[:, j * width_f : (j + 1) * width_f] for j in range(2)])
    grad_ffn_out = own_wf[:, 2 * width_f :].T
    sharded_sq = jnp.sum(own_wa * own_wa) + jnp.sum(own_wf * own_wf)
    copied_sq = (
        jnp.sum(grad_mod_w * grad_mod_w) / mp_count + jnp.sum(grad_table * grad_table) / dp_count
    )
    scalars = jnp.concatenate(
        [jnp.full((1, 128), sharded_sq + copied_sq), jnp.full((1, 128), loss_part), jnp.zeros((6, 128), F32)], 0
    )
    scalars = sum_pallas(scalars, dp_count, mp_count) if regular else lax.psum(scalars, BOTH)
    square_sum, loss_sum = scalars[0, 0], scalars[1, 0]
    norm = jnp.sqrt(square_sum)
    total_tokens = tokens * mp_count * dp_count
    clip = jnp.minimum(1.0, CLIP_SCALE / math.sqrt(total_tokens) / (norm + 1e-06))
    count = step_count[0].astype(F32)
    results = [(loss_sum / weight_sum).reshape(1), norm.reshape(1)]
    for weight, first, second, grad in (
        (qkv_w, qkv_m, qkv_v, grad_qkv),
        (out_w, out_m, out_v, grad_out_w),
        (ffn_in_w, ffn_in_m, ffn_in_v, grad_ffn_in),
        (ffn_out_w, ffn_out_m, ffn_out_v, grad_ffn_out),
        (mod_w, mod_m, mod_v, grad_mod_w),
        (table_w, table_m, table_v, grad_table),
    ):
        results.extend(adam(weight, first, second, grad * clip, count))
    return tuple(results)


def solution(mesh):
    tok, grp = P(None, BOTH), P("dp")
    cols, rows = P(None, "dp", "mp"), P("mp", "dp")
    weights = (cols,) * 3 + (rows,) * 3 + (cols,) * 3 + (rows,) * 3
    weights += (P("dp", None),) * 3 + (P("mp", None),) * 3
    in_specs = (tok, tok, grp, P(None, "dp"), grp, grp, grp, P()) + weights
    return jax.shard_map(
        per_device, mesh=mesh, in_specs=in_specs, out_specs=(P(), P()) + weights, check_vma=False
    )
```
